32 devices in a mesh: cplx: 4 (over y, x), smp: 4 (over z), qry: 2 (over core).
Axes of the slice: x: 2, y: 2, z: 4, core: 2. Of those that a mesh axis runs over, the one named last changes fastest.
Arguments:
- single: bfloat16 [4, 16, 640, 768], P('cplx', 'smp', 'qry'), may hold values from -6 to 6
- condition: bfloat16 [4, 640, 384], P('cplx', 'qry'), may hold values from -6 to 6
- pair_features: bfloat16 [4, 640, 640, 128], P('cplx', ('qry', 'smp')), may hold values from -6 to 6
- lengths: int32 [4], P('cplx'), may hold values from 448 to 640, as said below
- cotangent: bfloat16 [4, 16, 640, 768], P('cplx', 'smp', 'qry'), may hold values from -6 to 6
- first_gain: bfloat16 [384], replicated, may hold values from 0.099609375 to 1.8984375
- first_scale: bfloat16 [384, 768], replicated, may hold values from -0.3125 to 0.3125
- first_offset: bfloat16 [768], replicated, may hold values from -4 to 4
- first_shift: bfloat16 [384, 768], replicated, may hold values from -0.3125 to 0.3125
- query_projection_weight: bfloat16 [768, 768], replicated, may hold values from -0.21875 to 0.21875
- query_bias_vector: bfloat16 [768], replicated, may hold values from -3 to 3
- key_projection_weight: bfloat16 [768, 768], replicated, may hold values from -0.21875 to 0.21875
- value_projection_weight: bfloat16 [768, 768], replicated, may hold values from -0.21875 to 0.21875
- attention_gate_weight: bfloat16 [768, 768], replicated, may hold values from -0.21875 to 0.21875
- attention_output_weight: bfloat16 [768, 768], replicated, may hold values from -1.25 to 1.25
- pair_gain: bfloat16 [128], replicated, may hold values from 0.099609375 to 1.8984375
- pair_project: bfloat16 [128, 16], replicated, may hold values from -0.5 to 0.5
- finish_weight: bfloat16 [384, 768], replicated, may hold values from -0.3125 to 0.3125
- finish_offset: bfloat16 [768], replicated, may hold values from -4 to 4
- second_gain: bfloat16 [384], replicated, may hold values from 0.099609375 to 1.8984375
- second_scale: bfloat16 [384, 768], replicated, may hold values from -0.3125 to 0.3125
- second_offset: bfloat16 [768], replicated, may hold values from -4 to 4
- second_shift: bfloat16 [384, 768], replicated, may hold values from -0.3125 to 0.3125
- transition_swish_weight: bfloat16 [768, 1536], replicated, may hold values from -0.21875 to 0.21875
- transition_linear_weight: bfloat16 [768, 1536], replicated, may hold values from -0.21875 to 0.21875
- transition_down_weight: bfloat16 [1536, 768], replicated, may hold values from -0.4375 to 0.4375
- closing_weight: bfloat16 [384, 768], replicated, may hold values from -0.3125 to 0.3125
- closing_offset: bfloat16 [768], replicated, may hold values from -4 to 4
Outputs:
- block_out: bfloat16 [4, 16, 640, 768], P('cplx', 'smp', 'qry')
- single_grad: float32 [4, 16, 640, 768], P('cplx', 'smp', 'qry')
- condition_grad: float32 [4, 640, 384], P('cplx', 'qry')
- pair_grad: float32 [4, 640, 640, 128], P('cplx', ('qry', 'smp'))
- first_gain_grad: float32 [384], P('qry')
- first_scale_grad: float32 [384, 768], P(None, 'qry')
- first_offset_grad: float32 [768], P('qry')
- first_shift_grad: float32 [384, 768], P(None, 'qry')
- query_weight_grad: float32 [768, 768], P(None, 'qry')
- query_bias_grad: float32 [768], P('qry')
- key_weight_grad: float32 [768, 768], P(None, 'qry')
- value_weight_grad: float32 [768, 768], P(None, 'qry')
- gating_weight_grad: float32 [768, 768], P(None, 'qry')
- output_weight_grad: float32 [768, 768], P(None, 'qry')
- pair_gain_grad: float32 [128], P('qry')
- pair_project_grad: float32 [128, 16], P(None, 'qry')
- finish_weight_grad: float32 [384, 768], P(None, 'qry')
- finish_offset_grad: float32 [768], P('qry')
- second_gain_grad: float32 [384], P('qry')
- second_scale_grad: float32 [384, 768], P(None, 'qry')
- second_offset_grad: float32 [768], P('qry')
- second_shift_grad: float32 [384, 768], P(None, 'qry')
- swish_weight_grad: float32 [768, 1536], P(None, 'qry')
- linear_weight_grad: float32 [768, 1536], P(None, 'qry')
- down_weight_grad: float32 [1536, 768], P(None, 'qry')
- closing_weight_grad: float32 [384, 768], P(None, 'qry')
- closing_offset_grad: float32 [768], P('qry')
The draws below stay inside these ranges and needn't reach their ends.
Inputs may be any that keep to these rules, and one draw needn't show every extreme that they name: `lengths`: the complexes have different token counts; one of them fills all 640 slots.
All inputs are finite; a program needn't handle non-finite values.
Results may differ from the reference program's by a relative error of at most 0.013.
The reference program's roundings to bfloat16 on the way count: a program that leaves them out, or rounds other values in their place, can miss the bound.
Values may be sent and summed in bfloat16 or wider, within the bound.
No kernel may reach another device: no remote copies, remote signals or barrier semaphores. Data moves between devices by JAX's collectives and lax.ppermute only.
A program may use at most 448 MiB of HBM per device.

```python
import jax
import jax.numpy as jnp
from jax import lax

D = 768
CW = 384
PW = 128
HEADS = 16
FF = 1536
LEN = 640
SAMPLES = 16
COMPLEXES = 4


def draw_lengths(key, part):
    order = jax.random.permutation(key, COMPLEXES)
    return (LEN - LEN // 10 * (order % 4)).astype(jnp.int32)


def raised(array, stream_key, source, target, parts, factor):
    owner, partner = [(jnp.arange(array.shape[axis_at]) // (array.shape[axis_at] // parts)).reshape([-1 if axis == axis_at else 1 for axis in range(array.ndim)]) for axis_at in (source, target)]
    chosen = jax.random.permutation(stream_key, parts)[partner]
    strong = (owner == chosen) | (owner == (partner + parts // 2) % parts)
    return jnp.where(strong, factor * array, array)


def block_levels(own_key, shape, shards, least, largest):
    level = 1.0
    for axis_at, parts in shards:
        steps = jax.random.uniform(jax.random.fold_in(jax.random.fold_in(own_key, 6), axis_at), (parts,), jnp.float32, least / len(shards), largest / len(shards))
        level = level * jnp.repeat(jnp.exp(steps), shape[axis_at] // parts).reshape((-1,) + (1,) * (len(shape) - 1 - axis_at))
    return level


def normal_values(rng, extent, spread, bound, split=(), held_as=jnp.bfloat16):
    drawn = spread * jax.random.normal(rng, extent, jnp.float32)
    if split:
        drawn = drawn * block_levels(rng, extent, split, -0.22, 0.18)
    return jnp.clip(drawn, -bound, bound).astype(held_as)


def heavy_noise(stream_key, shape, scale, most, split, heavy, kind=jnp.bfloat16):
    drawn = scale * jax.random.normal(stream_key, shape, jnp.float32)
    if split:
        drawn = drawn * block_levels(stream_key, shape, split, -0.22, 0.18)
    return jnp.clip(raised(drawn, jax.random.fold_in(stream_key, 3), *heavy), -most, most).astype(kind)


def setup_inputs(seed: int = 0) -> dict:
    key_list = jax.random.split(jax.random.key(seed), 29)
    return {
        "single": normal_values(key_list[0], (COMPLEXES, SAMPLES, LEN, D), 1.0, 6.0, ((0, 4), (1, 4), (2, 2))),
        "condition": normal_values(key_list[1], (COMPLEXES, LEN, CW), 1.0, 6.0, ((0, 4), (1, 2))),
        "pair_features": normal_values(key_list[2], (COMPLEXES, LEN, LEN, PW), 1.0, 6.0, ((0, 4), (1, 8))),
        "lengths": draw_lengths(jax.random.fold_in(key_list[28], 71), 0),
        "cotangent": heavy_noise(key_list[4], (COMPLEXES, SAMPLES, LEN, D), 1.0, 6.0, ((0, 4), (1, 4), (2, 2)), (1, 2, 4, 2.0)),
        "first_gain": jnp.clip(1.0 + 0.18 * jax.random.normal(key_list[5], (CW,), jnp.float32), 0.099609375, 1.8984375).astype(jnp.bfloat16),
        "first_scale": normal_values(key_list[6], (CW, D), CW ** -0.5, 0.3125),
        "first_offset": normal_values(key_list[7], (D,), 1.0, 4.0),
        "first_shift": normal_values(key_list[8], (CW, D), CW ** -0.5, 0.3125),
        "query_projection_weight": normal_values(key_list[9], (D, D), D ** -0.5, 0.21875),
        "query_bias_vector": normal_values(key_list[10], (D,), 0.5, 3.0),
        "key_projection_weight": normal_values(key_list[11], (D, D), D ** -0.5, 0.21875),
        "value_projection_weight": normal_values(key_list[12], (D, D), D ** -0.5, 0.21875),
        "attention_gate_weight": normal_values(key_list[13], (D, D), D ** -0.5, 0.21875),
        "attention_output_weight": normal_values(key_list[14], (D, D), (D // 32) ** -0.5, 1.25),
        "pair_gain": jnp.clip(1.0 + 0.18 * jax.random.normal(key_list[15], (PW,), jnp.float32), 0.099609375, 1.8984375).astype(jnp.bfloat16),
        "pair_project": normal_values(key_list[16], (PW, HEADS), PW ** -0.5, 0.5),
        "finish_weight": normal_values(key_list[17], (CW, D), CW ** -0.5, 0.3125),
        "finish_offset": normal_values(key_list[18], (D,), 1.0, 4.0),
        "second_gain": jnp.clip(1.0 + 0.18 * jax.random.normal(key_list[19], (CW,), jnp.float32), 0.099609375, 1.8984375).astype(jnp.bfloat16),
        "second_scale": normal_values(key_list[20], (CW, D), CW ** -0.5, 0.3125),
        "second_offset": normal_values(key_list[21], (D,), 1.0, 4.0),
        "second_shift": normal_values(key_list[22], (CW, D), CW ** -0.5, 0.3125),
        "transition_swish_weight": normal_values(key_list[23], (D, FF), D ** -0.5, 0.21875),
        "transition_linear_weight": normal_values(key_list[24], (D, FF), D ** -0.5, 0.21875),
        "transition_down_weight": normal_values(key_list[25], (FF, D), (FF // 8) ** -0.5, 0.4375),
        "closing_weight": normal_values(key_list[26], (CW, D), CW ** -0.5, 0.3125),
        "closing_offset": normal_values(key_list[27], (D,), 1.0, 4.0),
    }


@jax.custom_vjp
def low(v):
    return lax.optimization_barrier(v.astype(jnp.bfloat16)).astype(jnp.float32)

@jax.custom_vjp
def low_back(v):
    return v

def low_keep(v):
    return (low(v), None)

def low_pass(kept, grad):
    return (grad,)

def back_keep(v):
    return (v, None)

def back_low(kept, grad):
    return (low(grad),)
low.defvjp(low_keep, low_pass)
low_back.defvjp(back_keep, back_low)
EPSILON = 1e-05
HIGHEST = lax.Precision.HIGHEST

def normalize(values):
    centre = values - lax.optimization_barrier(jnp.mean(values, axis=-1, keepdims=True))
    return centre * lax.rsqrt(lax.optimization_barrier(jnp.mean(centre * centre, axis=-1, keepdims=True)) + EPSILON)

def elementwise_product(form, left, right):
    return jnp.einsum(form, left, right, precision=HIGHEST)

def block_forward(token_count, single, condition, pair_features, weights):
    first_gain, first_scale, first_offset, first_shift, query_projection_weight, query_bias_vector, key_projection_weight, value_projection_weight, attention_gate_weight, attention_output_weight, pair_gain, pair_project, finish_weight, finish_offset, second_gain, second_scale, second_offset, second_shift, transition_swish_weight, transition_linear_weight, transition_down_weight, closing_weight, closing_offset = weights
    length = single.shape[1]
    model_width = single.shape[2]
    head_count = pair_project.shape[1]
    head_width = model_width // head_count
    positions = jnp.arange(length, dtype=jnp.int32)
    key_valid = positions < token_count
    row_mask = key_valid.astype(jnp.float32)[:, None]
    normed = normalize(single)
    condition_norm = normalize(condition)

    def modulate(gain, scale_weight, offset, shift_weight):
        condition_low = low(condition_norm * gain)
        lifting = jax.nn.sigmoid(elementwise_product('lc,cd->ld', condition_low, scale_weight) + offset)
        shifting = elementwise_product('lc,cd->ld', condition_low, shift_weight)
        return low(lifting[None] * normed + shifting[None])
    mixed_first_result = modulate(first_gain, first_scale, first_offset, first_shift)
    mixed_second_result = modulate(second_gain, second_scale, second_offset, second_shift)
    query_rows = low_back(low(elementwise_product('ywg,gr->ywr', mixed_first_result, query_projection_weight) + query_bias_vector))
    every_key_row = low_back(low(elementwise_product('ywg,gr->ywr', mixed_first_result, key_projection_weight)))
    every_value_row = low_back(low(elementwise_product('ywg,gr->ywr', mixed_first_result, value_projection_weight)))
    gate_activation = jax.nn.sigmoid(low_back(elementwise_product('ywg,gr->ywr', mixed_first_result, attention_gate_weight)))
    pair_low = low(normalize(pair_features) * pair_gain)
    bias_all = low_back(low(elementwise_product('ijp,ph->hij', pair_low, pair_project)))
    score_scale = head_width ** (-0.5)

    def attend(items):
        query_one, key_one, value_one = items
        query_heads = query_one.reshape(length, head_count, head_width)
        key_heads = key_one.reshape(length, head_count, head_width)
        value_heads = value_one.reshape(length, head_count, head_width)
        scores = low_back(elementwise_product('qhe,khe->hqk', query_heads, key_heads) * score_scale + bias_all)
        scores = jnp.where(key_valid[None, None, :], scores, -1e+30)
        highest = lax.optimization_barrier(jnp.max(scores, axis=-1, keepdims=True))
        exponent = jnp.exp(scores - highest)
        probability = low(exponent / lax.optimization_barrier(jnp.sum(exponent, axis=-1, keepdims=True)))
        return low_back(elementwise_product('hqk,khe->qhe', probability, value_heads)).reshape(length, model_width)
    attended = lax.map(jax.checkpoint(attend), (query_rows, every_key_row, every_value_row))
    gate_applied = low(gate_activation * attended)
    raised_state = low_back(elementwise_product('ywg,gr->ywr', gate_applied, attention_output_weight))
    finish = jax.nn.sigmoid(elementwise_product('lc,cd->ld', condition, finish_weight) + finish_offset)
    raised_swish_part = low_back(elementwise_product('amy,yt->amt', mixed_second_result, transition_swish_weight))
    raised_linear_part = low_back(elementwise_product('amy,yt->amt', mixed_second_result, transition_linear_weight))
    hidden_state = low(jax.nn.silu(raised_swish_part) * raised_linear_part)
    shifted_state = low_back(elementwise_product('xrn,no->xro', hidden_state, transition_down_weight))
    closing = jax.nn.sigmoid(elementwise_product('lc,cd->ld', condition, closing_weight) + closing_offset)
    return single + row_mask[None] * (finish[None] * raised_state + closing[None] * shifted_state)

def reference(single, condition, pair_features, lengths, cotangent, first_gain, first_scale, first_offset, first_shift, query_projection_weight, query_bias_vector, key_projection_weight, value_projection_weight, attention_gate_weight, attention_output_weight, pair_gain, pair_project, finish_weight, finish_offset, second_gain, second_scale, second_offset, second_shift, transition_swish_weight, transition_linear_weight, transition_down_weight, closing_weight, closing_offset):
    weights = tuple((argument.astype(jnp.float32) for argument in (first_gain, first_scale, first_offset, first_shift, query_projection_weight, query_bias_vector, key_projection_weight, value_projection_weight, attention_gate_weight, attention_output_weight, pair_gain, pair_project, finish_weight, finish_offset, second_gain, second_scale, second_offset, second_shift, transition_swish_weight, transition_linear_weight, transition_down_weight, closing_weight, closing_offset)))

    def one_complex(running, items):
        token_count, single_one, condition_one, pair_one, cotangent_one = items

        def forward(single_value, condition_value, pair_value, weight_values):
            return block_forward(token_count, single_value, condition_value, pair_value, weight_values)
        result, pullback = jax.vjp(forward, single_one.astype(jnp.float32), condition_one.astype(jnp.float32), pair_one.astype(jnp.float32), weights)
        single_grad, condition_grad, pair_grad, weight_grads = pullback(cotangent_one.astype(jnp.float32))
        running = tuple((earlier + addend for earlier, addend in zip(running, weight_grads)))
        return (running, (result.astype(jnp.bfloat16), single_grad, condition_grad, pair_grad))
    initial = tuple((jnp.zeros(argument.shape, jnp.float32) for argument in weights))
    totals, stacked = lax.scan(one_complex, initial, (lengths, single, condition, pair_features, cotangent))
    return (stacked[0], stacked[1], stacked[2], stacked[3], totals[0], totals[1], totals[2], totals[3], totals[4], totals[5], totals[6], totals[7], totals[8], totals[9], totals[10], totals[11], totals[12], totals[13], totals[14], totals[15], totals[16], totals[17], totals[18], totals[19], totals[20], totals[21], totals[22])
```

```python
import functools

import jax
import jax.numpy as jnp
from jax import lax
from jax.experimental import pallas as pl
from jax.experimental.pallas import tpu as pltpu
from jax.sharding import PartitionSpec as P

EPSILON = 1e-05
HIGHEST = lax.Precision.HIGHEST
LANES = 128
VMEM_LIMIT = 56 * 2**20
PARTS = 2
f32 = jnp.float32
bf16 = jnp.bfloat16


def dot(left, right, left_dim, right_dim):
    return lax.dot_general(
        left, right, (((left_dim,), (right_dim,)), ((), ())), preferred_element_type=f32
    )


def attention_kernel(
    meta, query, key_mine, key_other, value_mine, value_other, gate, delta_gated, bias,
    gated, delta_gate, delta_query, dk_mine, dk_other, dv_mine, dv_other, delta_bias,
    score, prob, slope, *, step
):
    samples, head_width, rows = query.shape
    total = 2 * rows
    pieces, piece_rows = bias.shape[0], bias.shape[2]
    scale = head_width ** (-0.5)
    second = meta[1] == 1
    column = lax.broadcasted_iota(jnp.int32, (16, total), 1)
    line = lax.broadcasted_iota(jnp.int32, (16, total), 0)
    masking = jnp.where((line == 0) & (column >= meta[0]), -1e30, 0.0).astype(bf16)
    pair_ones = jnp.where(line < 2, 1.0, 0.0).astype(bf16)
    query_line = lax.broadcasted_iota(jnp.int32, (16, rows), 0)
    one_line = jnp.where(query_line == 0, 1.0, 0.0).astype(bf16)
    spots = [
        (piece, start, piece * piece_rows + start)
        for piece in range(pieces)
        for start in range(0, piece_rows, step)
    ]

    def joined(mine, other):
        first = jnp.where(second, other, mine)
        last = jnp.where(second, mine, other)
        return jnp.concatenate([first, last], axis=1)

    def parted(whole, mine, other, sample):
        first, last = whole[:, :rows], whole[:, rows:]
        mine[sample] = jnp.where(second, last, first)
        other[sample] = jnp.where(second, first, last).astype(other.dtype)

    keys, values = [], []
    for s in range(samples):
        keys.append(joined(key_mine[s], key_other[s]))
        values.append(joined(value_mine[s], value_other[s]))
        score[s] = dot(
            jnp.concatenate([query[s], one_line], axis=0),
            jnp.concatenate([keys[s], masking], axis=0),
            0,
            0,
        )
    for piece, start, place in spots:
        bias_here = bias[piece, 0, start : start + step, :].astype(f32)
        here = slice(place, place + step)
        for s in range(samples):
            line_scores = score[s, here, :] * scale + bias_here
            highest = jnp.max(line_scores, axis=1, keepdims=True)
            exponent = jnp.exp(line_scores - highest)
            soft = exponent * (1.0 / jnp.sum(exponent, axis=1, keepdims=True))
            score[s, here, :] = soft
            prob[s, here, :] = soft.astype(bf16)
    for s in range(samples):
        attended = dot(values[s], prob[s], 1, 1)
        gate_here, delta_here = gate[s], delta_gated[s]
        gated[s] = (gate_here * attended).astype(bf16)
        delta_attended = (delta_here * gate_here).astype(bf16)
        delta_gate[s] = (delta_here * attended * gate_here * (1.0 - gate_here)).astype(bf16)
        centre = jnp.sum(delta_attended.astype(f32) * attended, axis=0, keepdims=True)
        coarse = centre.astype(bf16).astype(f32)
        rest = jnp.where(
            query_line == 0, -coarse, jnp.where(query_line == 1, coarse - centre, 0.0)
        ).astype(bf16)
        slope[s] = dot(
            jnp.concatenate([delta_attended, rest], axis=0),
            jnp.concatenate([values[s], pair_ones], axis=0),
            0,
            0,
        )
        parted(dot(delta_attended, prob[s], 1, 0), dv_mine, dv_other, s)
    for piece, start, place in spots:
        here = slice(place, place + step)
        total_here = None
        for s in range(samples):
            delta_scores = score[s, here, :] * slope[s, here, :]
            prob[s, here, :] = delta_scores.astype(bf16)
            total_here = delta_scores if total_here is None else total_here + delta_scores
        delta_bias[piece, 0, start : start + step, :] = total_here.astype(bf16)
    for s in range(samples):
        delta_query[s] = (dot(keys[s], prob[s], 1, 1) * scale).astype(bf16)
        parted(dot(query[s], prob[s], 1, 0) * scale, dk_mine, dk_other, s)


def attention(meta, query, key_pair, value_pair, gate, delta_gated, bias, part, parts):
    samples, width, rows = query.shape
    pieces, heads, piece_rows, total = bias.shape
    head_width = width // (heads * parts)
    step = 16 if piece_rows % 16 == 0 else piece_rows
    first = part * heads
    inner = pl.BlockSpec((samples, head_width, rows), lambda h, meta: (0, first + h, 0))
    outer = pl.BlockSpec((samples, head_width, rows), lambda h, meta: (0, h, 0))
    tile = pl.BlockSpec((pieces, 1, piece_rows, total), lambda h, meta: (0, h, 0, 0))

    def made(dtype):
        return jax.ShapeDtypeStruct((samples, heads * head_width, rows), dtype)

    return pl.pallas_call(
        functools.partial(attention_kernel, step=step),
        grid_spec=pltpu.PrefetchScalarGridSpec(
            num_scalar_prefetch=1,
            grid=(heads,),
            in_specs=[inner] * 7 + [tile],
            out_specs=[outer] * 7 + [tile],
            scratch_shapes=[
                pltpu.VMEM((samples, rows, total), f32),
                pltpu.VMEM((samples, rows, total), bf16),
                pltpu.VMEM((samples, rows, total), f32),
            ],
        ),
        out_shape=[
            made(bf16), made(bf16), made(bf16), made(f32), made(f32), made(f32), made(f32),
            jax.ShapeDtypeStruct(bias.shape, bf16),
        ],
        compiler_params=pltpu.CompilerParams(vmem_limit_bytes=VMEM_LIMIT),
        cost_estimate=pl.CostEstimate(
            flops=samples * heads * rows * total * 6 * 256 * 2,
            bytes_accessed=samples * heads * head_width * rows * 34 + 4 * rows * total * heads,
            transcendentals=samples * heads * rows * total,
        ),
    )(meta, query, *key_pair, *value_pair, gate, delta_gated, bias)


def pair_forward_kernel(pair, gain, project, *refs, block, heads, parts):
    outs, wide = refs[:-1], refs[-1]
    gain_here = gain[...].astype(f32)

    def one(i, carry):
        normed, _ = normalize(pair[i].astype(f32))
        low = (normed * gain_here).astype(bf16)
        line = dot(project[...], low, 0, 1)
        for t in range(wide.shape[0]):
            wide[t, pl.ds(pl.multiple_of(i * heads, heads), heads), :] = line[
                :, t * LANES : (t + 1) * LANES
            ]
        return carry

    lax.fori_loop(0, block, one, 0, unroll=2)
    share = heads // parts
    for h in range(heads):
        for t in range(wide.shape[0]):
            outs[h // share][h % share, :, t * LANES : (t + 1) * LANES] = wide[
                t, pl.ds(h, block, stride=heads), :
            ].astype(bf16)


def pair_forward(pair, gain, project, parts):
    rows, length, width = pair.shape
    heads = project.shape[1]
    block = 16 if rows % 16 == 0 else rows
    share = heads // parts
    return pl.pallas_call(
        functools.partial(pair_forward_kernel, block=block, heads=heads, parts=parts),
        grid=(rows // block,),
        in_specs=[
            pl.BlockSpec((block, length, width), lambda i: (i, 0, 0)),
            pl.BlockSpec((1, width), lambda i: (0, 0)),
            pl.BlockSpec((width, heads), lambda i: (0, 0)),
        ],
        out_specs=[pl.BlockSpec((share, block, length), lambda i: (0, i, 0))] * parts,
        out_shape=[jax.ShapeDtypeStruct((share, rows, length), bf16)] * parts,
        scratch_shapes=[pltpu.VMEM((length // LANES, block * heads, LANES), f32)],
        compiler_params=pltpu.CompilerParams(vmem_limit_bytes=VMEM_LIMIT),
        cost_estimate=pl.CostEstimate(
            flops=2 * rows * length * width * 256,
            bytes_accessed=2 * rows * length * (width + heads),
            transcendentals=0,
        ),
    )(pair, gain.reshape(1, width), project)


def pair_backward_kernel(pair, gain, project, *refs, block, heads, parts):
    deltas = refs[:parts]
    out, gain_out, project_out, wide, gain_sum, project_sum = refs[parts:]
    step = pl.program_id(0)
    gain_here = gain[...].astype(f32)
    share = heads // parts

    @pl.when(step == 0)
    def _():
        gain_sum[...] = jnp.zeros_like(gain_sum)
        project_sum[...] = jnp.zeros_like(project_sum)

    for h in range(heads):
        for t in range(wide.shape[0]):
            wide[t, h * block : (h + 1) * block, :] = deltas[h // share][
                h % share, :, t * LANES : (t + 1) * LANES
            ].astype(f32)

    def one(i, carry):
        normed, factor = normalize(pair[i].astype(f32))
        low = (normed * gain_here).astype(bf16)
        delta = jnp.concatenate(
            [wide[t, pl.ds(i, heads, stride=block), :] for t in range(wide.shape[0])], axis=1
        ).astype(bf16)
        delta_low = dot(delta, project[...], 0, 1)
        project_sum[...] += dot(delta, low, 1, 0)
        product = delta_low * normed
        gain_sum[...] += jnp.sum(product.reshape(-1, 8, product.shape[-1]), axis=0)
        incoming = delta_low * gain_here
        out[i] = factor * (
            incoming
            - jnp.mean(incoming, axis=-1, keepdims=True)
            - normed * jnp.mean(product * gain_here, axis=-1, keepdims=True)
        )
        return carry

    lax.fori_loop(0, block, one, 0, unroll=2)

    @pl.when(step == pl.num_programs(0) - 1)
    def _():
        gain_out[...] = jnp.sum(gain_sum[...], axis=0, keepdims=True)
        project_out[...] = project_sum[...]


def pair_backward(pair, gain, project, deltas):
    rows, length, width = pair.shape
    heads = project.shape[1]
    parts = len(deltas)
    block = 16 if rows % 16 == 0 else rows
    share = heads // parts
    return pl.pallas_call(
        functools.partial(pair_backward_kernel, block=block, heads=heads, parts=parts),
        grid=(rows // block,),
        in_specs=[
            pl.BlockSpec((block, length, width), lambda i: (i, 0, 0)),
            pl.BlockSpec((1, width), lambda i: (0, 0)),
            pl.BlockSpec((width, heads), lambda i: (0, 0)),
        ]
        + [pl.BlockSpec((share, block, length), lambda i: (0, i, 0))] * parts,
        out_specs=[
            pl.BlockSpec((block, length, width), lambda i: (i, 0, 0)),
            pl.BlockSpec((1, width), lambda i: (0, 0)),
            pl.BlockSpec((heads, width), lambda i: (0, 0)),
        ],
        out_shape=[
            jax.ShapeDtypeStruct((rows, length, width), f32),
            jax.ShapeDtypeStruct((1, width), f32),
            jax.ShapeDtypeStruct((heads, width), f32),
        ],
        scratch_shapes=[
            pltpu.VMEM((length // LANES, block * heads, LANES), f32),
            pltpu.VMEM((8, width), f32),
            pltpu.VMEM((heads, width), f32),
        ],
        compiler_params=pltpu.CompilerParams(vmem_limit_bytes=VMEM_LIMIT),
        cost_estimate=pl.CostEstimate(
            flops=2 * rows * length * width * 512,
            bytes_accessed=2 * rows * length * (3 * width + heads),
            transcendentals=0,
        ),
    )(pair, gain.reshape(1, width), project, *deltas)


def swap_cores(array):
    return lax.ppermute(array, "qry", [(0, 1), (1, 0)])


def halves(array):
    portion = array.shape[-1] // 2
    core = lax.axis_index("qry")
    mine = lax.dynamic_slice_in_dim(array, core * portion, portion, array.ndim - 1)
    other = lax.dynamic_slice_in_dim(array, (1 - core) * portion, portion, array.ndim - 1)
    return mine, other


def chip_sums(arrays, after=None):
    kept = []
    for array in arrays:
        mine, other = halves(array)
        arrived = swap_cores(other.astype(bf16))
        kept.append((mine + arrived.astype(f32)).astype(bf16))
    if after is not None:
        kept, _ = lax.optimization_barrier((kept, after))
    return lax.psum(tuple(kept), ("cplx", "smp"))


def widened(arrays):
    return tuple(array.astype(f32) for array in arrays)


def gather_rows(piece):
    if piece.shape[1] % 16 == 0:
        return lax.all_gather(piece, "smp", axis=0)
    return lax.all_gather(piece, "smp", axis=1, tiled=True)[None]


def scatter_rows(whole):
    if whole.shape[0] == lax.axis_size("smp"):
        return lax.psum_scatter(whole, "smp", scatter_dimension=0)
    return lax.psum_scatter(whole[0], "smp", scatter_dimension=1, tiled=True)


def normalize(values):
    centre = values - jnp.mean(values, axis=-1, keepdims=True)
    factor = lax.rsqrt(jnp.mean(centre * centre, axis=-1, keepdims=True) + EPSILON)
    return (centre * factor, factor)


def normalize_back(incoming, normed, factor):
    return factor * (
        incoming
        - jnp.mean(incoming, axis=-1, keepdims=True)
        - normed * jnp.mean(incoming * normed, axis=-1, keepdims=True)
    )


def matmul(left, right):
    return jnp.dot(left, right, preferred_element_type=jnp.float32)


def contract(form, left, right):
    return jnp.einsum(form, left, right, preferred_element_type=jnp.float32)


def exact_contract(form, left, right):
    return jnp.einsum(form, left.astype(jnp.float32), right.astype(jnp.float32), precision=HIGHEST)


def modulate(condition_norm, normed, gain, scale_weight, offset, shift_weight):
    condition_low = (condition_norm * gain.astype(jnp.float32)).astype(jnp.bfloat16)
    lifting = jax.nn.sigmoid(matmul(condition_low, scale_weight) + offset.astype(jnp.float32))
    shifting = matmul(condition_low, shift_weight)
    blended = (lifting[None] * normed + shifting[None]).astype(jnp.bfloat16)
    return (condition_low, lifting, blended)


def modulate_back(delta_blended, normed, condition_low, lifting, scale_weight, shift_weight):
    delta_lift = jnp.sum(delta_blended * normed, axis=0) * lifting * (1.0 - lifting)
    delta_shift = jnp.sum(delta_blended, axis=0)
    scale_total = exact_contract("qc,qd->cd", condition_low, delta_lift)
    offset_total = jnp.sum(delta_lift, axis=0)
    shift_total = exact_contract("qc,qd->cd", condition_low, delta_shift)
    delta_condition = exact_contract("qd,cd->qc", delta_lift, scale_weight) + exact_contract(
        "qd,cd->qc", delta_shift, shift_weight
    )
    return (delta_blended * lifting[None], delta_condition, scale_total, offset_total, shift_total)


def per_device(
    single,
    condition,
    pair_features,
    lengths,
    cotangent,
    first_gain,
    first_scale,
    first_offset,
    first_shift,
    query_projection_weight,
    query_bias_vector,
    key_projection_weight,
    value_projection_weight,
    attention_gate_weight,
    attention_output_weight,
    pair_gain,
    pair_project,
    finish_weight,
    finish_offset,
    second_gain,
    second_scale,
    second_offset,
    second_shift,
    transition_swish_weight,
    transition_linear_weight,
    transition_down_weight,
    closing_weight,
    closing_offset,
):
    row_count = single.shape[2]
    model_width = single.shape[3]
    head_count = pair_project.shape[1]
    token_count = lengths[0]
    row_ids = lax.axis_index("qry") * row_count + jnp.arange(row_count, dtype=jnp.int32)
    row_mask = (row_ids < token_count).astype(jnp.float32)[:, None]
    residual = single[0].astype(jnp.float32)
    condition_raw = condition[0]
    normed, factor = normalize(residual)
    condition_norm, condition_factor = normalize(condition_raw.astype(jnp.float32))
    condition_first, lifting_first, mixed_first_result = modulate(
        condition_norm, normed, first_gain, first_scale, first_offset, first_shift
    )
    condition_second, lifting_second, mixed_second_result = modulate(
        condition_norm, normed, second_gain, second_scale, second_offset, second_shift
    )
    finish = jax.nn.sigmoid(
        matmul(condition_raw, finish_weight) + finish_offset.astype(jnp.float32)
    )
    bias_pieces = pair_forward(pair_features[0], pair_gain, pair_project, PARTS)
    bias_rows = [gather_rows(piece) for piece in bias_pieces]
    query_turned = (
        contract("srd,de->ser", mixed_first_result, query_projection_weight)
        + query_bias_vector.astype(jnp.float32)[:, None]
    ).astype(jnp.bfloat16)
    key_turned = contract("srd,de->ser", mixed_first_result, key_projection_weight).astype(
        jnp.bfloat16
    )
    value_turned = contract("srd,de->ser", mixed_first_result, value_projection_weight).astype(
        jnp.bfloat16
    )
    key_pair = (key_turned, swap_cores(key_turned))
    value_pair = (value_turned, swap_cores(value_turned))
    gate_turned = jax.nn.sigmoid(contract("srd,de->ser", mixed_first_result, attention_gate_weight))
    outgoing = cotangent[0].astype(jnp.float32)
    branch_grad = row_mask * outgoing
    delta_lifted = (finish[None] * branch_grad).astype(jnp.bfloat16)
    delta_gated_turned = contract("sre,de->sdr", delta_lifted, attention_output_weight)
    raised_swish_part = matmul(mixed_second_result, transition_swish_weight)
    raised_linear_part = matmul(mixed_second_result, transition_linear_weight)
    swish_sigmoid = jax.nn.sigmoid(raised_swish_part)
    hidden_state = (raised_swish_part * swish_sigmoid * raised_linear_part).astype(jnp.bfloat16)
    shifted_state = matmul(hidden_state, transition_down_weight)
    closing = jax.nn.sigmoid(
        matmul(condition_raw, closing_weight) + closing_offset.astype(jnp.float32)
    )
    delta_moved = (closing[None] * branch_grad).astype(jnp.bfloat16)
    delta_closing = jnp.sum(branch_grad * shifted_state, axis=0) * closing * (1.0 - closing)
    closing_total = exact_contract("qc,qd->cd", condition_raw, delta_closing)
    closingoffset_total = jnp.sum(delta_closing, axis=0)
    delta_condition = exact_contract("qd,cd->qc", delta_closing, closing_weight)
    down_total = contract("sqf,sqd->fd", hidden_state, delta_moved)
    delta_hidden = contract("sqd,fd->sqf", delta_moved, transition_down_weight)
    delta_swish = (
        delta_hidden
        * raised_linear_part
        * swish_sigmoid
        * (1.0 + raised_swish_part * (1.0 - swish_sigmoid))
    ).astype(jnp.bfloat16)
    delta_linear = (delta_hidden * raised_swish_part * swish_sigmoid).astype(jnp.bfloat16)
    swish_total = contract("sqd,sqf->df", mixed_second_result, delta_swish)
    linear_total = contract("sqd,sqf->df", mixed_second_result, delta_linear)
    delta_second = contract("sqf,df->sqd", delta_swish, transition_swish_weight) + contract(
        "sqf,df->sqd", delta_linear, transition_linear_weight
    )
    early = chip_sums((swish_total, linear_total, down_total, closing_total))
    meta = jnp.stack([token_count, lax.axis_index("qry")]).astype(jnp.int32)
    attended_parts = [
        attention(
            meta,
            query_turned,
            key_pair,
            value_pair,
            gate_turned,
            delta_gated_turned,
            bias_rows[part],
            part,
            PARTS,
        )
        for part in range(PARTS)
    ]
    delta_bias = [scatter_rows(part[7]) for part in attended_parts]
    gate_applied, delta_gating, delta_queries, dk_mine, dk_other, dv_mine, dv_other = [
        jnp.concatenate([part[i] for part in attended_parts], axis=1) for i in range(7)
    ]
    delta_keys = (dk_mine + swap_cores(dk_other)).astype(jnp.bfloat16)
    delta_values = (dv_mine + swap_cores(dv_other)).astype(jnp.bfloat16)
    raised_state = contract("ser,ed->srd", gate_applied, attention_output_weight)
    block_out = (
        residual + row_mask * (finish[None] * raised_state + closing[None] * shifted_state)
    ).astype(jnp.bfloat16)
    delta_finish = jnp.sum(branch_grad * raised_state, axis=0) * finish * (1.0 - finish)
    finish_total = exact_contract("qc,qd->cd", condition_raw, delta_finish)
    finishoffset_total = jnp.sum(delta_finish, axis=0)
    delta_condition = delta_condition + exact_contract("qd,cd->qc", delta_finish, finish_weight)
    output_total = contract("ser,srd->ed", gate_applied, delta_lifted)
    gating_total = contract("srd,ser->de", mixed_first_result, delta_gating)
    query_total = contract("srd,ser->de", mixed_first_result, delta_queries)
    querybias_total = jnp.sum(delta_queries.astype(jnp.float32), axis=(0, 2))
    key_total = contract("srd,ser->de", mixed_first_result, delta_keys)
    value_total = contract("srd,ser->de", mixed_first_result, delta_values)
    middle = chip_sums(
        (output_total, gating_total, finish_total, query_total, key_total, value_total),
        early,
    )
    delta_first = (
        contract("ser,de->srd", delta_queries, query_projection_weight)
        + contract("ser,de->srd", delta_keys, key_projection_weight)
        + contract("ser,de->srd", delta_values, value_projection_weight)
        + contract("ser,de->srd", delta_gating, attention_gate_weight)
    )
    normed_first, cond_delta_first, scale_first, offset_first, shift_first = modulate_back(
        delta_first, normed, condition_first, lifting_first, first_scale, first_shift
    )
    normed_second, cond_delta_second, scale_second, offset_second, shift_second = modulate_back(
        delta_second, normed, condition_second, lifting_second, second_scale, second_shift
    )
    gain_first = jnp.sum(cond_delta_first * condition_norm, axis=0)
    gain_second = jnp.sum(cond_delta_second * condition_norm, axis=0)
    single_grad = outgoing + normalize_back(normed_first + normed_second, normed, factor)
    condition_local = (
        normalize_back(
            cond_delta_first * first_gain.astype(jnp.float32)
            + cond_delta_second * second_gain.astype(jnp.float32),
            condition_norm,
            condition_factor,
        )
        + delta_condition
    )
    condition_grad = lax.psum(condition_local, "smp")
    pair_grad, pairgain_total, project_total = pair_backward(
        pair_features[0], pair_gain, pair_project, delta_bias
    )
    small = jnp.concatenate(
        [
            jnp.stack(halves(whole))
            for whole in (
                gain_first,
                offset_first,
                querybias_total,
                pairgain_total[0],
                finishoffset_total,
                gain_second,
                offset_second,
                closingoffset_total,
            )
        ]
        + [jnp.stack([half.reshape(-1) for half in halves(project_total.T)])],
        axis=1,
    )
    late = chip_sums((scale_first, shift_first, scale_second, shift_second), middle)
    vectors = lax.psum(
        (small[0] + swap_cores(small[1])), ("cplx", "smp")
    )
    ends, place = [], 0
    wide, narrow, pair_width = model_width // 2, condition_raw.shape[1] // 2, pair_gain.shape[0]
    sizes = (narrow, wide, wide, pair_width // 2, wide, narrow, wide, wide)
    for size in sizes + (pair_width * head_count // 2,):
        ends.append(vectors[place : place + size])
        place += size
    swish_total, linear_total, down_total, closing_total = widened(early)
    output_total, gating_total, finish_total, query_total, key_total, value_total = widened(middle)
    scale_first, shift_first, scale_second, shift_second = widened(late)
    return (
        block_out[None],
        single_grad[None],
        condition_grad[None],
        pair_grad[None],
        ends[0],
        scale_first,
        ends[1],
        shift_first,
        query_total,
        ends[2],
        key_total,
        value_total,
        gating_total,
        output_total,
        ends[3],
        ends[8].reshape(-1, head_count // 2),
        finish_total,
        ends[4],
        ends[5],
        scale_second,
        ends[6],
        shift_second,
        swish_total,
        linear_total,
        down_total,
        closing_total,
        ends[7],
    )


def solution(mesh):
    placed = (
        P("cplx", "smp", "qry", None),
        P("cplx", "qry", None),
        P("cplx", ("qry", "smp"), None, None),
        P("cplx"),
        P("cplx", "smp", "qry", None),
        P(),
        P(),
        P(),
        P(),
        P(),
        P(),
        P(),
        P(),
        P(),
        P(),
        P(),
        P(),
        P(),
        P(),
        P(),
        P(),
        P(),
        P(),
        P(),
        P(),
        P(),
        P(),
        P(),
    )
    return jax.shard_map(
        per_device,
        mesh=mesh,
        in_specs=placed,
        out_specs=(
            P("cplx", "smp", "qry", None),
            P("cplx", "smp", "qry", None),
            P("cplx", "qry", None),
            P("cplx", ("qry", "smp"), None, None),
            P("qry"),
            P(None, "qry"),
            P("qry"),
            P(None, "qry"),
            P(None, "qry"),
            P("qry"),
            P(None, "qry"),
            P(None, "qry"),
            P(None, "qry"),
            P(None, "qry"),
            P("qry"),
            P(None, "qry"),
            P(None, "qry"),
            P("qry"),
            P("qry"),
            P(None, "qry"),
            P("qry"),
            P(None, "qry"),
            P(None, "qry"),
            P(None, "qry"),
            P(None, "qry"),
            P(None, "qry"),
            P("qry"),
        ),
        check_vma=False,
    )
```

```python
import functools

import jax
import jax.numpy as jnp
from jax import lax
from jax.experimental import pallas as pl
from jax.experimental.pallas import tpu as pltpu
from jax.sharding import PartitionSpec as P

EPSILON = 1e-05
LANES = 128
VMEM_LIMIT = 56 * 2**20
PARTS = 2
f32 = jnp.float32
bf16 = jnp.bfloat16


def normalize(values):
    centre = values - jnp.mean(values, axis=-1, keepdims=True)
    factor = lax.rsqrt(jnp.mean(centre * centre, axis=-1, keepdims=True) + EPSILON)
    return (centre * factor, factor)


def normalize_back(incoming, normed, factor):
    return factor * (
        incoming
        - jnp.mean(incoming, axis=-1, keepdims=True)
        - normed * jnp.mean(incoming * normed, axis=-1, keepdims=True)
    )


def matmul(left, right):
    return jnp.dot(left, right, preferred_element_type=jnp.float32)


def contract(form, left, right):
    return jnp.einsum(
        form, left.astype(bf16), right.astype(bf16), preferred_element_type=jnp.float32
    )


def dot(left, right, left_dim, right_dim):
    return lax.dot_general(
        left, right, (((left_dim,), (right_dim,)), ((), ())), preferred_element_type=f32
    )


def attention_kernel(
    meta, query, key_mine, key_other, value_mine, value_other, gate, delta_gated, bias,
    gated, delta_gate, delta_query, dk_mine, dk_other, dv_mine, dv_other, delta_bias,
    score, prob, slope, *, step
):
    samples, head_width, rows = query.shape
    total = 2 * rows
    pieces, piece_rows = bias.shape[0], bias.shape[2]
    scale = head_width ** (-0.5)
    second = meta[1] == 1
    column = lax.broadcasted_iota(jnp.int32, (16, total), 1)
    line = lax.broadcasted_iota(jnp.int32, (16, total), 0)
    masking = jnp.where((line == 0) & (column >= meta[0]), -1e30, 0.0).astype(bf16)
    pair_ones = jnp.where(line < 2, 1.0, 0.0).astype(bf16)
    query_line = lax.broadcasted_iota(jnp.int32, (16, rows), 0)
    one_line = jnp.where(query_line == 0, 1.0, 0.0).astype(bf16)
    spots = [
        (piece, start, piece * piece_rows + start)
        for piece in range(pieces)
        for start in range(0, piece_rows, step)
    ]

    def joined(mine, other):
        mine, other = mine[:, :rows], other[:, :rows]
        first = jnp.where(second, other, mine)
        last = jnp.where(second, mine, other)
        return jnp.concatenate([first, last], axis=1)

    def parted(whole, mine, other, sample):
        first, last = whole[:, :rows], whole[:, rows:]
        mine[sample] = jnp.where(second, last, first)
        other[sample, :, :rows] = jnp.where(second, first, last).astype(other.dtype)

    keys, values = [], []
    for s in range(samples):
        keys.append(joined(key_mine[s], key_other[s]))
        values.append(joined(value_mine[s], value_other[s]))
        score[s] = dot(
            jnp.concatenate([query[s], one_line], axis=0),
            jnp.concatenate([keys[s], masking], axis=0),
            0,
            0,
        )
    for piece, start, place in spots:
        bias_here = bias[piece, 0, start : start + step, :].astype(f32)
        here = slice(place, place + step)
        for s in range(samples):
            line_scores = score[s, here, :] * scale + bias_here
            highest = jnp.max(line_scores, axis=1, keepdims=True)
            exponent = jnp.exp(line_scores - highest)
            soft = exponent * (1.0 / jnp.sum(exponent, axis=1, keepdims=True))
            score[s, here, :] = soft
            prob[s, here, :] = soft.astype(bf16)
    for s in range(samples):
        attended = dot(values[s], prob[s], 1, 1)
        gate_here, delta_here = gate[s], delta_gated[s]
        gated[s] = (gate_here * attended).astype(bf16)
        delta_attended = (delta_here * gate_here).astype(bf16)
        delta_gate[s] = (delta_here * attended * gate_here * (1.0 - gate_here)).astype(bf16)
        centre = jnp.sum(delta_attended.astype(f32) * attended, axis=0, keepdims=True)
        coarse = centre.astype(bf16).astype(f32)
        rest = jnp.where(
            query_line == 0, -coarse, jnp.where(query_line == 1, coarse - centre, 0.0)
        ).astype(bf16)
        slope[s] = dot(
            jnp.concatenate([delta_attended, rest], axis=0),
            jnp.concatenate([values[s], pair_ones], axis=0),
            0,
            0,
        )
        parted(dot(delta_attended, prob[s], 1, 0), dv_mine, dv_other, s)
    for piece, start, place in spots:
        here = slice(place, place + step)
        total_here = None
        for s in range(samples):
            delta_scores = score[s, here, :] * slope[s, here, :]
            prob[s, here, :] = delta_scores.astype(bf16)
            total_here = delta_scores if total_here is None else total_here + delta_scores
        delta_bias[piece, 0, start : start + step, :] = total_here.astype(bf16)
    for s in range(samples):
        delta_query[s] = (dot(keys[s], prob[s], 1, 1) * scale).astype(bf16)
        parted(dot(query[s], prob[s], 1, 0) * scale, dk_mine, dk_other, s)


def attention(meta, query, key_pair, value_pair, gate, delta_gated, bias, part, parts):
    samples, width, rows = query.shape
    pieces, heads, piece_rows, total = bias.shape
    head_width = width // (heads * parts)
    step = 16 if piece_rows % 16 == 0 else piece_rows
    first = part * heads
    inner = pl.BlockSpec((samples, head_width, rows), lambda h, meta: (0, first + h, 0))
    outer = pl.BlockSpec((samples, head_width, rows), lambda h, meta: (0, h, 0))
    tile = pl.BlockSpec((pieces, 1, piece_rows, total), lambda h, meta: (0, h, 0, 0))

    padded = key_pair[0].shape[2]
    inner_wide = pl.BlockSpec((samples, head_width, padded), lambda h, meta: (0, first + h, 0))
    outer_wide = pl.BlockSpec((samples, head_width, padded), lambda h, meta: (0, h, 0))

    def made(dtype, columns=rows):
        return jax.ShapeDtypeStruct((samples, heads * head_width, columns), dtype)

    return pl.pallas_call(
        functools.partial(attention_kernel, step=step),
        grid_spec=pltpu.PrefetchScalarGridSpec(
            num_scalar_prefetch=1,
            grid=(heads,),
            in_specs=[inner] + [inner_wide] * 4 + [inner] * 2 + [tile],
            out_specs=[outer] * 4 + [outer_wide, outer, outer_wide, tile],
            scratch_shapes=[
                pltpu.VMEM((samples, rows, total), f32),
                pltpu.VMEM((samples, rows, total), bf16),
                pltpu.VMEM((samples, rows, total), f32),
            ],
        ),
        out_shape=[
            made(bf16), made(bf16), made(bf16), made(f32), made(bf16, padded), made(f32),
            made(bf16, padded),
            jax.ShapeDtypeStruct(bias.shape, bf16),
        ],
        compiler_params=pltpu.CompilerParams(vmem_limit_bytes=VMEM_LIMIT),
        cost_estimate=pl.CostEstimate(
            flops=samples * heads * rows * total * 6 * 256 * 2,
            bytes_accessed=samples * heads * head_width * rows * 34 + 4 * rows * total * heads,
            transcendentals=samples * heads * rows * total,
        ),
    )(meta, query, *key_pair, *value_pair, gate, delta_gated, bias)


def pair_forward_kernel(pair, gain, project, *refs, block, heads, parts):
    outs, wide = refs[:-1], refs[-1]
    gain_here = gain[...].astype(f32)

    def one(i, carry):
        normed, _ = normalize(pair[i].astype(f32))
        low = (normed * gain_here).astype(bf16)
        line = dot(project[...], low, 0, 1)
        for t in range(wide.shape[0]):
            wide[t, pl.ds(pl.multiple_of(i * heads, heads), heads), :] = line[
                :, t * LANES : (t + 1) * LANES
            ]
        return carry

    lax.fori_loop(0, block, one, 0, unroll=2)
    share = heads // parts
    for h in range(heads):
        for t in range(wide.shape[0]):
            outs[h // share][h % share, :, t * LANES : (t + 1) * LANES] = wide[
                t, pl.ds(h, block, stride=heads), :
            ].astype(bf16)


def pair_forward(pair, gain, project, parts):
    rows, length, width = pair.shape
    heads = project.shape[1]
    block = 16 if rows % 16 == 0 else rows
    share = heads // parts
    return pl.pallas_call(
        functools.partial(pair_forward_kernel, block=block, heads=heads, parts=parts),
        grid=(rows // block,),
        in_specs=[
            pl.BlockSpec((block, length, width), lambda i: (i, 0, 0)),
            pl.BlockSpec((1, width), lambda i: (0, 0)),
            pl.BlockSpec((width, heads), lambda i: (0, 0)),
        ],
        out_specs=[pl.BlockSpec((share, block, length), lambda i: (0, i, 0))] * parts,
        out_shape=[jax.ShapeDtypeStruct((share, rows, length), bf16)] * parts,
        scratch_shapes=[pltpu.VMEM((length // LANES, block * heads, LANES), f32)],
        compiler_params=pltpu.CompilerParams(vmem_limit_bytes=VMEM_LIMIT),
        cost_estimate=pl.CostEstimate(
            flops=2 * rows * length * width * 256,
            bytes_accessed=2 * rows * length * (width + heads),
            transcendentals=0,
        ),
    )(pair, gain.reshape(1, width), project)


def pair_backward_kernel(pair, gain, project, *refs, block, heads, parts):
    deltas = refs[:parts]
    out, gain_out, project_out, wide, gain_sum, project_sum = refs[parts:]
    step = pl.program_id(0)
    gain_here = gain[...].astype(f32)
    share = heads // parts

    @pl.when(step == 0)
    def _():
        gain_sum[...] = jnp.zeros_like(gain_sum)
        project_sum[...] = jnp.zeros_like(project_sum)

    for h in range(heads):
        for t in range(wide.shape[0]):
            wide[t, h * block : (h + 1) * block, :] = deltas[h // share][
                h % share, :, t * LANES : (t + 1) * LANES
            ].astype(f32)

    def one(i, carry):
        normed, factor = normalize(pair[i].astype(f32))
        low = (normed * gain_here).astype(bf16)
        delta = jnp.concatenate(
            [wide[t, pl.ds(i, heads, stride=block), :] for t in range(wide.shape[0])], axis=1
        ).astype(bf16)
        delta_low = dot(delta, project[...], 0, 1)
        project_sum[...] += dot(delta, low, 1, 0)
        product = delta_low * normed
        gain_sum[...] += jnp.sum(product.reshape(-1, 8, product.shape[-1]), axis=0)
        incoming = delta_low * gain_here
        out[i] = factor * (
            incoming
            - jnp.mean(incoming, axis=-1, keepdims=True)
            - normed * jnp.mean(product * gain_here, axis=-1, keepdims=True)
        )
        return carry

    lax.fori_loop(0, block, one, 0, unroll=2)

    @pl.when(step == pl.num_programs(0) - 1)
    def _():
        gain_out[...] = jnp.sum(gain_sum[...], axis=0, keepdims=True)
        project_out[...] = project_sum[...]


def pair_backward(pair, gain, project, deltas):
    rows, length, width = pair.shape
    heads = project.shape[1]
    parts = len(deltas)
    block = 16 if rows % 16 == 0 else rows
    share = heads // parts
    return pl.pallas_call(
        functools.partial(pair_backward_kernel, block=block, heads=heads, parts=parts),
        grid=(rows // block,),
        in_specs=[
            pl.BlockSpec((block, length, width), lambda i: (i, 0, 0)),
            pl.BlockSpec((1, width), lambda i: (0, 0)),
            pl.BlockSpec((width, heads), lambda i: (0, 0)),
        ]
        + [pl.BlockSpec((share, block, length), lambda i: (0, i, 0))] * parts,
        out_specs=[
            pl.BlockSpec((block, length, width), lambda i: (i, 0, 0)),
            pl.BlockSpec((1, width), lambda i: (0, 0)),
            pl.BlockSpec((heads, width), lambda i: (0, 0)),
        ],
        out_shape=[
            jax.ShapeDtypeStruct((rows, length, width), f32),
            jax.ShapeDtypeStruct((1, width), f32),
            jax.ShapeDtypeStruct((heads, width), f32),
        ],
        scratch_shapes=[
            pltpu.VMEM((length // LANES, block * heads, LANES), f32),
            pltpu.VMEM((8, width), f32),
            pltpu.VMEM((heads, width), f32),
        ],
        compiler_params=pltpu.CompilerParams(vmem_limit_bytes=VMEM_LIMIT),
        cost_estimate=pl.CostEstimate(
            flops=2 * rows * length * width * 512,
            bytes_accessed=2 * rows * length * (3 * width + heads),
            transcendentals=0,
        ),
    )(pair, gain.reshape(1, width), project, *deltas)


def fixed(shape):
    return pl.BlockSpec(shape, lambda s, *_: (0,) * len(shape), pipeline_mode=pl.Buffered(1))


def by_sample(shape, buffers=2):
    return pl.BlockSpec(
        (1,) + shape,
        lambda s, *_: (s,) + (0,) * len(shape),
        pipeline_mode=pl.Buffered(buffers),
    )


def row_valid(meta, rows):
    place = lax.broadcasted_iota(jnp.int32, (rows, 1), 0) + meta[1] * rows
    return jnp.where(place < meta[0], 1.0, 0.0)


def pack_columns(meta, packs, arrays, start=0):
    tile = packs[0].shape[1]
    for array in arrays:
        depth, share = array.shape[0], array.shape[1] // 2
        for side in range(2):
            core = meta[1] if side == 0 else 1 - meta[1]
            for block in range(share // tile):
                column = pl.multiple_of(core * share + block * tile, LANES)
                packs[side][start + block * depth : start + (block + 1) * depth, :] = array[
                    :, pl.ds(column, tile)
                ].astype(bf16)
        start += depth * (share // tile)


def project_kernel(
    meta, single, cotangent, lifting, shifting, finish, query_bias,
    query_weight, key_weight, value_weight, gate_weight, output_weight,
    query, key, value, gate, delta_gated, mixed_out,
):
    rows = single.shape[1]
    normed, _ = normalize(single[0].astype(f32))
    mixed = (lifting[...] * normed + shifting[...]).astype(bf16)
    mixed_out[0] = mixed
    query[0] = (dot(mixed, query_weight[...], 1, 0) + query_bias[...]).astype(bf16).T
    key[0, :, :rows] = dot(mixed, key_weight[...], 1, 0).astype(bf16).T
    value[0, :, :rows] = dot(mixed, value_weight[...], 1, 0).astype(bf16).T
    gate[0] = jax.nn.sigmoid(dot(mixed, gate_weight[...], 1, 0)).T
    branch = row_valid(meta, rows) * cotangent[0].astype(f32)
    lifted = (finish[...] * branch).astype(bf16)
    delta_gated[0] = dot(lifted, output_weight[...], 1, 1).T


def project(meta, single, cotangent, lifting, shifting, finish, query_bias, weights):
    samples, rows, width = single.shape
    natural, turned = by_sample((rows, width)), by_sample((width, rows))
    flat, square = fixed((rows, width)), fixed((width, width))
    padded = rows + -rows % LANES
    wide = by_sample((width, padded))
    return pl.pallas_call(
        project_kernel,
        grid_spec=pltpu.PrefetchScalarGridSpec(
            num_scalar_prefetch=1,
            grid=(samples,),
            in_specs=[natural, natural, flat, flat, flat, fixed((1, width))] + [square] * 5,
            out_specs=[turned, wide, wide, turned, turned, natural],
        ),
        out_shape=[
            jax.ShapeDtypeStruct((samples, width, columns), dtype)
            for columns, dtype in (
                (rows, bf16), (padded, bf16), (padded, bf16), (rows, f32), (rows, f32)
            )
        ]
        + [jax.ShapeDtypeStruct((samples, rows, width), bf16)],
        compiler_params=pltpu.CompilerParams(vmem_limit_bytes=VMEM_LIMIT),
        cost_estimate=pl.CostEstimate(
            flops=16 * samples * rows * width * width,
            bytes_accessed=samples * rows * width * 20 + 10 * width * width,
            transcendentals=samples * rows * width,
        ),
    )(meta, single, cotangent, lifting, shifting, finish, query_bias, *weights)


def transition_kernel(
    meta, single, cotangent, lifting, shifting, closing,
    swish_weight, linear_weight, down_weight,
    closed, delta_second, closing_sum, lift_sum, shift_sum, pack_mine, pack_other,
    swish_sum, linear_sum, down_sum,
):
    rows = single.shape[1]
    sample = pl.program_id(0)
    normed, _ = normalize(single[0].astype(f32))
    mixed = (lifting[...] * normed + shifting[...]).astype(bf16)
    up_swish = dot(mixed, swish_weight[...], 1, 0)
    up_linear = dot(mixed, linear_weight[...], 1, 0)
    squash = jax.nn.sigmoid(up_swish)
    silu = up_swish * squash
    hidden = (silu * up_linear).astype(bf16)
    moved = dot(hidden, down_weight[...], 1, 0)
    closing_here = closing[...]
    branch = row_valid(meta, rows) * cotangent[0].astype(f32)
    closed[0] = closing_here * moved
    delta_moved = (closing_here * branch).astype(bf16)
    delta_hidden = dot(delta_moved, down_weight[...], 1, 1)
    delta_swish = (delta_hidden * up_linear * squash * (1.0 + up_swish * (1.0 - squash))).astype(bf16)
    delta_linear = (delta_hidden * silu).astype(bf16)
    second = dot(delta_swish, swish_weight[...], 1, 1) + dot(
        delta_linear, linear_weight[...], 1, 1
    )
    delta_second[0] = second

    def collect(first):
        def put(ref, value):
            if first:
                ref[...] = value
            else:
                ref[...] += value

        put(closing_sum, branch * moved)
        put(lift_sum, second * normed)
        put(shift_sum, second)
        put(swish_sum, dot(mixed, delta_swish, 0, 0))
        put(linear_sum, dot(mixed, delta_linear, 0, 0))
        put(down_sum, dot(hidden, delta_moved, 0, 0))

    @pl.when(sample == 0)
    def _():
        collect(True)

    @pl.when(sample > 0)
    def _():
        collect(False)

    @pl.when(sample == pl.num_programs(0) - 1)
    def _():
        pack_columns(meta, (pack_mine, pack_other), (swish_sum, linear_sum, down_sum))


def transition(meta, single, cotangent, lifting, shifting, closing, weights, pack_rows):
    samples, rows, width = single.shape
    inner = weights[0].shape[1]
    natural, flat = by_sample((rows, width)), fixed((rows, width))
    up, down = (width, inner), (inner, width)
    pack = (pack_rows, width // 2)
    return pl.pallas_call(
        transition_kernel,
        grid_spec=pltpu.PrefetchScalarGridSpec(
            num_scalar_prefetch=1,
            grid=(samples,),
            in_specs=[natural, natural, flat, flat, flat, fixed(up), fixed(up), fixed(down)],
            out_specs=[natural, natural, flat, flat, flat, fixed(pack), fixed(pack)],
            scratch_shapes=[pltpu.VMEM(up, f32), pltpu.VMEM(up, f32), pltpu.VMEM(down, f32)],
        ),
        out_shape=[
            jax.ShapeDtypeStruct(shape, f32)
            for shape in ((samples, rows, width),) * 2 + ((rows, width),) * 3
        ]
        + [jax.ShapeDtypeStruct(pack, bf16)] * 2,
        compiler_params=pltpu.CompilerParams(vmem_limit_bytes=VMEM_LIMIT),
        cost_estimate=pl.CostEstimate(
            flops=18 * samples * rows * width * inner,
            bytes_accessed=samples * rows * width * 12 + 18 * width * inner,
            transcendentals=samples * rows * inner,
        ),
    )(meta, single, cotangent, lifting, shifting, closing, *weights)


def finish_kernel(
    meta, single, cotangent, closed, delta_second, mixed,
    gated_a, gated_b, gate_a, gate_b, query_a, query_b, dk_mine_a, dk_mine_b, dk_other_a,
    dk_other_b, dv_mine_a, dv_mine_b, dv_other_a, dv_other_b,
    lifting_first, lifting_second, finish,
    query_weight, key_weight, value_weight, gate_weight, output_weight,
    block_out, single_grad, finish_sum, lift_first, shift_first, pack_mine, pack_other, bias_sum,
    query_sum, key_sum, value_sum, gate_sum, output_sum,
):
    rows = single.shape[1]

    def whole(*parts):
        return jnp.concatenate([part[0] for part in parts], axis=0)

    gated, delta_gate, delta_query = (
        whole(gated_a, gated_b), whole(gate_a, gate_b), whole(query_a, query_b)
    )
    delta_key = (whole(dk_mine_a, dk_mine_b) + whole(dk_other_a, dk_other_b)[:, :rows].astype(f32)).astype(bf16)
    delta_value = (
        whole(dv_mine_a, dv_mine_b) + whole(dv_other_a, dv_other_b)[:, :rows].astype(f32)
    ).astype(bf16)
    rows = single.shape[1]
    sample = pl.program_id(0)
    residual = single[0].astype(f32)
    normed, factor = normalize(residual)
    valid = row_valid(meta, rows)
    outgoing = cotangent[0].astype(f32)
    branch = valid * outgoing
    finish_here = finish[...]
    raised = dot(gated, output_weight[...], 0, 0)
    block_out[0] = (residual + valid * (finish_here * raised + closed[0])).astype(bf16)
    lifted = (finish_here * branch).astype(bf16)
    delta_first = (
        dot(delta_query, query_weight[...], 0, 1)
        + dot(delta_key, key_weight[...], 0, 1)
        + dot(delta_value, value_weight[...], 0, 1)
        + dot(delta_gate, gate_weight[...], 0, 1)
    )
    second = delta_second[0]
    incoming = delta_first * lifting_first[...] + second * lifting_second[...]
    single_grad[0] = outgoing + normalize_back(incoming, normed, factor)

    def collect(first):
        def put(ref, value):
            if first:
                ref[...] = value
            else:
                ref[...] += value

        put(finish_sum, branch * raised)
        put(lift_first, delta_first * normed)
        put(shift_first, delta_first)
        put(query_sum, dot(delta_query, mixed[0], 1, 0))
        put(key_sum, dot(delta_key, mixed[0], 1, 0))
        put(value_sum, dot(delta_value, mixed[0], 1, 0))
        put(gate_sum, dot(delta_gate, mixed[0], 1, 0))
        put(output_sum, dot(gated, lifted, 1, 0))
        put(bias_sum, jnp.sum(delta_query.astype(f32), axis=1, keepdims=True))

    @pl.when(sample == 0)
    def _():
        collect(True)

    @pl.when(sample > 0)
    def _():
        collect(False)

    @pl.when(sample == pl.num_programs(0) - 1)
    def _():
        width = query_sum.shape[0]
        half = width // 2
        packs = (pack_mine, pack_other)
        for i, array in enumerate((query_sum, key_sum, value_sum, gate_sum)):
            for side in range(2):
                core = meta[1] if side == 0 else 1 - meta[1]
                row = pl.multiple_of(core * half, LANES)
                packs[side][i * width : (i + 1) * width, :] = array[
                    pl.ds(row, half), :
                ].T.astype(bf16)
        pack_columns(meta, packs, (output_sum,), 4 * width)


def finish_block(meta, naturals, turned, flats, weights, pack_rows):
    samples, rows, width = naturals[0].shape
    natural, flat, square = by_sample((rows, width)), fixed((rows, width)), fixed((width, width))
    pack = (pack_rows, width // 2)
    return pl.pallas_call(
        finish_kernel,
        grid_spec=pltpu.PrefetchScalarGridSpec(
            num_scalar_prefetch=1,
            grid=(samples,),
            in_specs=[natural] * 2
            + [by_sample((rows, width), 1)] * 2
            + [natural]
            + [
                by_sample((width // 2, array.shape[2]), 1 if array.dtype == f32 else 2)
                for array in turned
            ]
            + [flat] * 3
            + [square] * 5,
            out_specs=[natural] * 2 + [flat] * 3 + [fixed(pack)] * 2 + [fixed((width, 1))],
            scratch_shapes=[pltpu.VMEM((width, width), f32)] * 5,
        ),
        out_shape=[
            jax.ShapeDtypeStruct((samples, rows, width), bf16),
            jax.ShapeDtypeStruct((samples, rows, width), f32),
        ]
        + [jax.ShapeDtypeStruct((rows, width), f32)] * 3
        + [jax.ShapeDtypeStruct(pack, bf16)] * 2
        + [jax.ShapeDtypeStruct((width, 1), f32)],
        compiler_params=pltpu.CompilerParams(vmem_limit_bytes=VMEM_LIMIT),
        cost_estimate=pl.CostEstimate(
            flops=20 * samples * rows * width * width,
            bytes_accessed=samples * rows * width * 42 + 30 * width * width,
            transcendentals=0,
        ),
    )(meta, *naturals, *turned, *flats, *weights)


def swap_cores(array):
    return lax.ppermute(array, "qry", [(0, 1), (1, 0)])


def exchange(array, axis, bit):
    return lax.ppermute(array, axis, [(i, i ^ bit) for i in range(lax.axis_size(axis))])


def pick(array, index):
    return lax.dynamic_index_in_dim(array, index, 0, keepdims=False)


def placed_by(pieces, place):
    ordered = []
    for j in range(len(pieces)):
        chosen = pieces[j]
        for shift in range(1, len(pieces)):
            chosen = jnp.where(place == shift, pieces[j ^ shift], chosen)
        ordered.append(chosen)
    return ordered


def filled(packs, start, arrays):
    packs = list(packs)
    for array in arrays:
        for side, half in enumerate(halves(array)):
            packs[side] = lax.dynamic_update_slice(packs[side], half.astype(bf16), (start, 0))
        start += array.shape[0]
    return packs


def padded_rows(count):
    return count + -count % 512


def gated_by(values, meta):
    return lax.optimization_barrier((values, meta))


class SliceTotal:
    def __init__(self, mine, other):
        self.columns = mine.shape[1]
        self.shape = (2, 2, 2, mine.shape[0] // 8, self.columns)
        self.mine = mine.reshape(self.shape)
        self.arrived = swap_cores(other).reshape(self.shape)
        self.place, self.level = lax.axis_index("cplx"), lax.axis_index("smp")
        self.levels = lax.axis_size("smp")
        self.bits = (self.place % 2, self.place // 2)

    def local(self, side, near_bit, far_bit):
        at = (far_bit, near_bit) if side == 0 else (near_bit, far_bit)
        pieces = [
            pick(pick(array[side], at[0]), at[1]).astype(f32)
            for array in (self.mine, self.arrived)
        ]
        return pieces[0] + pieces[1]

    def first_sends(self):
        return [
            [
                self.local(side, 1 - self.bits[side], far).astype(bf16)
                for far in (self.bits[1 - side], 1 - self.bits[1 - side])
            ]
            for side in range(2)
        ]

    def first(self, sends):
        self.kept = [
            [exchange(piece, "cplx", 1 << side) for piece in sends[side]] for side in range(2)
        ]

    def second_sends(self):
        return [
            (
                self.local(side, self.bits[side], 1 - self.bits[1 - side])
                + self.kept[side][1].astype(f32)
            ).astype(bf16)
            for side in range(2)
        ]

    def second(self, sends):
        passed = [exchange(sends[side], "cplx", 2 >> side) for side in range(2)]
        sums = [
            self.local(side, self.bits[side], self.bits[1 - side])
            + self.kept[side][0].astype(f32)
            + passed[side].astype(f32)
            for side in range(2)
        ]
        self.quarter = jnp.concatenate(sums, axis=0).reshape(self.levels, -1, self.columns)

    def third_sends(self):
        return [
            pick(self.quarter, self.level ^ shift).astype(bf16) for shift in range(1, self.levels)
        ]

    def third(self, sends):
        own = pick(self.quarter, self.level)
        for shift, piece in enumerate(sends):
            own = own + exchange(piece, "smp", shift + 1).astype(f32)
        self.own = own.astype(bf16)

    def fourth(self):
        pieces = [self.own] + [
            exchange(self.own, "smp", shift) for shift in range(1, self.levels)
        ]
        quarter = jnp.concatenate(placed_by(pieces, self.level), axis=0)
        self.quarter = quarter.reshape(2, -1, self.columns)

    def fifth(self):
        wholes = []
        for side in range(2):
            near, far = 1 << side, 2 >> side
            piece = self.quarter[side]
            at = [None] * 4
            at[0], at[near], at[far] = piece, exchange(piece, "cplx", near), exchange(piece, "cplx", far)
            at[3] = exchange(at[far], "cplx", near)
            wholes += placed_by(at, self.place)
        return jnp.concatenate(wholes, axis=0).astype(f32)


def total_small(vector):
    vector = vector[0] + swap_cores(vector[1])
    for axis in ("cplx", "smp"):
        arrived = [exchange(vector, axis, shift) for shift in range(1, lax.axis_size(axis))]
        vector = sum(arrived, vector)
    return vector


def sum_samples(array):
    narrow = array.astype(bf16)
    arrived = [exchange(narrow, "smp", shift) for shift in range(1, lax.axis_size("smp"))]
    return sum((piece.astype(f32) for piece in arrived), array)


def halves(array):
    portion = array.shape[-1] // 2
    core = lax.axis_index("qry")
    mine = lax.dynamic_slice_in_dim(array, core * portion, portion, array.ndim - 1)
    other = lax.dynamic_slice_in_dim(array, (1 - core) * portion, portion, array.ndim - 1)
    return mine, other


def gather_rows(piece):
    if piece.shape[1] % 16 == 0:
        return lax.all_gather(piece, "smp", axis=0)
    return lax.all_gather(piece, "smp", axis=1, tiled=True)[None]


def scatter_rows(whole):
    if whole.shape[0] == lax.axis_size("smp"):
        return lax.psum_scatter(whole, "smp", scatter_dimension=0)
    return lax.psum_scatter(whole[0], "smp", scatter_dimension=1, tiled=True)


def per_device(
    single,
    condition,
    pair_features,
    lengths,
    cotangent,
    first_gain,
    first_scale,
    first_offset,
    first_shift,
    query_projection_weight,
    query_bias_vector,
    key_projection_weight,
    value_projection_weight,
    attention_gate_weight,
    attention_output_weight,
    pair_gain,
    pair_project,
    finish_weight,
    finish_offset,
    second_gain,
    second_scale,
    second_offset,
    second_shift,
    transition_swish_weight,
    transition_linear_weight,
    transition_down_weight,
    closing_weight,
    closing_offset,
):
    width = single.shape[3]
    narrow = condition.shape[2]
    half = width // 2
    inner = transition_swish_weight.shape[1]
    heads = pair_project.shape[1]
    meta = jnp.stack([lengths[0], lax.axis_index("qry")]).astype(jnp.int32)
    condition_raw = condition[0]
    condition_norm, condition_factor = normalize(condition_raw.astype(f32))
    bias_pieces = pair_forward(pair_features[0], pair_gain, pair_project, PARTS)
    bias_rows = [gather_rows(piece) for piece in bias_pieces]

    def modulation(gain, scale_weight, offset, shift_weight):
        low = (condition_norm * gain.astype(f32)).astype(bf16)
        lifting = jax.nn.sigmoid(matmul(low, scale_weight) + offset.astype(f32))
        return low, lifting, matmul(low, shift_weight)

    condition_first, lifting_first, shifting_first = modulation(
        first_gain, first_scale, first_offset, first_shift
    )
    condition_second, lifting_second, shifting_second = modulation(
        second_gain, second_scale, second_offset, second_shift
    )
    finish = jax.nn.sigmoid(matmul(condition_raw, finish_weight) + finish_offset.astype(f32))
    closing = jax.nn.sigmoid(matmul(condition_raw, closing_weight) + closing_offset.astype(f32))
    square_weights = (
        query_projection_weight,
        key_projection_weight,
        value_projection_weight,
        attention_gate_weight,
        attention_output_weight,
    )
    query, key, value, gate, delta_gated, mixed_first = project(
        meta,
        single[0],
        cotangent[0],
        lifting_first,
        shifting_first,
        finish,
        query_bias_vector.astype(f32)[None],
        square_weights,
    )
    key_pair = (key, swap_cores(key))
    value_pair = (value, swap_cores(value))
    closed, delta_second, closing_sum, lift_second, shift_second, *second_packs = transition(
        meta,
        single[0],
        cotangent[0],
        lifting_second,
        shifting_second,
        closing,
        (transition_swish_weight, transition_linear_weight, transition_down_weight),
        padded_rows(3 * inner + 3 * narrow),
    )

    def modulation_back(lift_sum, shift_sum, low, lifting, scale_weight, shift_weight):
        delta_lift = lift_sum * lifting * (1.0 - lifting)
        scale_total = contract("qc,qd->cd", low, delta_lift)
        shift_total = contract("qc,qd->cd", low, shift_sum)
        delta_condition = contract("qd,cd->qc", delta_lift, scale_weight) + contract(
            "qd,cd->qc", shift_sum, shift_weight
        )
        return scale_total, jnp.sum(delta_lift, axis=0), shift_total, delta_condition

    def gate_back(branch_sum, opened, weight):
        delta = branch_sum * opened * (1.0 - opened)
        return (
            contract("qc,qd->cd", condition_raw, delta),
            jnp.sum(delta, axis=0),
            contract("qd,cd->qc", delta, weight),
        )

    scale_second, offset_second, shift_total_second, cond_delta_second = modulation_back(
        lift_second, shift_second, condition_second, lifting_second, second_scale, second_shift
    )
    closing_total, closing_offset_total, condition_closing = gate_back(
        closing_sum, closing, closing_weight
    )
    early = SliceTotal(
        *filled(second_packs, 3 * inner, (scale_second, shift_total_second, closing_total))
    )

    def attend(meta, part):
        return attention(
            meta, query, key_pair, value_pair, gate, delta_gated, bias_rows[part], part, PARTS
        )

    attended = [attend(meta, 0)]
    sends, meta_next = gated_by(early.first_sends(), meta)
    early.first(sends)
    attended.append(attend(meta_next, 1))
    sends, meta_next = gated_by(early.second_sends(), meta)
    early.second(sends)
    delta_bias = [scatter_rows(part[7]) for part in attended]
    arrived_keys = [swap_cores(part[4]) for part in attended]
    arrived_values = [swap_cores(part[6]) for part in attended]
    turned = (
        [part[0] for part in attended]
        + [part[1] for part in attended]
        + [part[2] for part in attended]
        + [part[3] for part in attended]
        + arrived_keys
        + [part[5] for part in attended]
        + arrived_values
    )
    block_out, single_grad, finish_sum, lift_first, shift_first, *first_packs, query_bias_total = (
        finish_block(
            meta_next,
            (single[0], cotangent[0], closed, delta_second, mixed_first),
            turned,
            (lifting_first, lifting_second, finish),
            square_weights,
            padded_rows(5 * width + 3 * narrow),
        )
    )
    scale_first, offset_first, shift_total_first, cond_delta_first = modulation_back(
        lift_first, shift_first, condition_first, lifting_first, first_scale, first_shift
    )
    finish_total, finish_offset_total, condition_finish = gate_back(
        finish_sum, finish, finish_weight
    )
    late = SliceTotal(
        *filled(first_packs, 5 * width, (scale_first, shift_total_first, finish_total))
    )
    early.third(early.third_sends())
    late.first(late.first_sends())
    early.fourth()
    late.second(late.second_sends())
    early = early.fifth()
    late.third(late.third_sends())
    late.fourth()
    late = late.fifth()
    gain_first = jnp.sum(cond_delta_first * condition_norm, axis=0)
    gain_second = jnp.sum(cond_delta_second * condition_norm, axis=0)
    condition_grad = sum_samples(
        normalize_back(
            cond_delta_first * first_gain.astype(f32) + cond_delta_second * second_gain.astype(f32),
            condition_norm,
            condition_factor,
        )
        + condition_closing
        + condition_finish
    )
    pair_grad, pair_gain_total, pair_project_total = pair_backward(
        pair_features[0], pair_gain, pair_project, delta_bias
    )
    vectors = (
        gain_first,
        offset_first,
        query_bias_total[:, 0],
        finish_offset_total,
        gain_second,
        offset_second,
        closing_offset_total,
        pair_gain_total[0],
    )
    small = total_small(
        jnp.concatenate(
            [jnp.stack(halves(vector)) for vector in vectors]
            + [jnp.stack([half.reshape(-1) for half in halves(pair_project_total.T)])],
            axis=1,
        )
    )
    ends, place = [], 0
    for vector in vectors:
        ends.append(small[place : place + vector.shape[0] // 2])
        place += vector.shape[0] // 2
    def unpack(total, sizes):
        arrays, start = [], 0
        for depth, columns in sizes:
            blocks = columns // half
            arrays.append(
                jnp.concatenate(
                    [
                        total[start + b * depth : start + (b + 1) * depth]
                        for b in range(blocks)
                    ],
                    axis=1,
                )
            )
            start += depth * blocks
        return arrays

    swish_total, linear_total, down_total, scale_second, shift_second, closing_total = unpack(
        early,
        ((width, inner // 2), (width, inner // 2), (inner, half)) + ((narrow, half),) * 3,
    )
    query_total, key_total, value_total, gate_total, output_total, *others = unpack(
        late, ((width, half),) * 5 + ((narrow, half),) * 3
    )
    scale_first, shift_first, finish_total = others
    return (
        block_out[None],
        single_grad[None],
        condition_grad[None],
        pair_grad[None],
        ends[0],
        scale_first,
        ends[1],
        shift_first,
        query_total,
        ends[2],
        key_total,
        value_total,
        gate_total,
        output_total,
        ends[7],
        small[place:].reshape(-1, heads // 2),
        finish_total,
        ends[3],
        ends[4],
        scale_second,
        ends[5],
        shift_second,
        swish_total,
        linear_total,
        down_total,
        closing_total,
        ends[6],
    )


def solution(mesh):
    placed = (
        P("cplx", "smp", "qry", None),
        P("cplx", "qry", None),
        P("cplx", ("qry", "smp"), None, None),
        P("cplx"),
        P("cplx", "smp", "qry", None),
        P(),
        P(),
        P(),
        P(),
        P(),
        P(),
        P(),
        P(),
        P(),
        P(),
        P(),
        P(),
        P(),
        P(),
        P(),
        P(),
        P(),
        P(),
        P(),
        P(),
        P(),
        P(),
        P(),
    )
    return jax.shard_map(
        per_device,
        mesh=mesh,
        in_specs=placed,
        out_specs=(
            P("cplx", "smp", "qry", None),
            P("cplx", "smp", "qry", None),
            P("cplx", "qry", None),
            P("cplx", ("qry", "smp"), None, None),
            P("qry"),
            P(None, "qry"),
            P("qry"),
            P(None, "qry"),
            P(None, "qry"),
            P("qry"),
            P(None, "qry"),
            P(None, "qry"),
            P(None, "qry"),
            P(None, "qry"),
            P("qry"),
            P(None, "qry"),
            P(None, "qry"),
            P("qry"),
            P("qry"),
            P(None, "qry"),
            P("qry"),
            P(None, "qry"),
            P(None, "qry"),
            P(None, "qry"),
            P(None, "qry"),
            P(None, "qry"),
            P("qry"),
        ),
        check_vma=False,
    )
```

```python
import functools

import jax
import jax.numpy as jnp
from jax import lax
from jax.experimental import pallas as pl
from jax.experimental.pallas import tpu as pltpu
from jax.sharding import PartitionSpec as P

EPSILON = 1e-05
LANES = 128
VMEM_LIMIT = 56 * 2**20
SHARES = (10, 6)
CALLS = 2
EARLY_APART = ("smp",)
LATE_APART = ("smp",)
f32 = jnp.float32
bf16 = jnp.bfloat16


def normalize(values):
    centre = values - jnp.mean(values, axis=-1, keepdims=True)
    factor = lax.rsqrt(jnp.mean(centre * centre, axis=-1, keepdims=True) + EPSILON)
    return (centre * factor, factor)


def normalize_back(incoming, normed, factor):
    return factor * (
        incoming
        - jnp.mean(incoming, axis=-1, keepdims=True)
        - normed * jnp.mean(incoming * normed, axis=-1, keepdims=True)
    )


def matmul(left, right):
    return jnp.dot(left, right, preferred_element_type=jnp.float32)


def contract(form, left, right):
    return jnp.einsum(
        form, left.astype(bf16), right.astype(bf16), preferred_element_type=jnp.float32
    )


def dot(left, right, left_dim, right_dim):
    return lax.dot_general(
        left, right, (((left_dim,), (right_dim,)), ((), ())), preferred_element_type=f32
    )


def attention_kernel(
    meta, query, mine, other, gate, delta_gated, bias, *refs, step
):
    (
        gated, delta_gate, delta_query, kept, sent, delta_bias, score, prob, slope,
    ) = refs[-9:]
    samples, head_width, rows = query.shape
    total = 2 * rows
    pieces, piece_rows = bias.shape[0], bias.shape[2]
    scale = head_width ** (-0.5)
    second = meta[1] == 1
    column = lax.broadcasted_iota(jnp.int32, (16, total), 1)
    line = lax.broadcasted_iota(jnp.int32, (16, total), 0)
    masking = jnp.where((line == 0) & (column >= meta[0]), -1e30, 0.0).astype(bf16)
    pair_ones = jnp.where(line < 2, 1.0, 0.0).astype(bf16)
    query_line = lax.broadcasted_iota(jnp.int32, (16, rows), 0)
    one_line = jnp.where(query_line == 0, 1.0, 0.0).astype(bf16)
    spots = [
        (piece, start, piece * piece_rows + start)
        for piece in range(pieces)
        for start in range(0, piece_rows, step)
    ]

    def joined(mine, other):
        mine, other = mine[:, :rows], other[:, :rows]
        first = jnp.where(second, other, mine)
        last = jnp.where(second, mine, other)
        return jnp.concatenate([first, last], axis=1)

    def parted(whole, sample, which):
        first, last = whole[:, :rows], whole[:, rows:]
        kept[sample, which] = jnp.where(second, last, first)
        sent[sample, which, :, :rows] = jnp.where(second, first, last).astype(sent.dtype)

    keys, values = [], []
    for s in range(samples):
        keys.append(joined(mine[s, 0], other[s, 0]))
        values.append(joined(mine[s, 1], other[s, 1]))
        score[s] = dot(
            jnp.concatenate([query[s], one_line], axis=0),
            jnp.concatenate([keys[s], masking], axis=0),
            0,
            0,
        )
    for piece, start, place in spots:
        bias_here = bias[piece, 0, start : start + step, :].astype(f32)
        here = slice(place, place + step)
        for s in range(samples):
            line_scores = score[s, here, :] * scale + bias_here
            highest = jnp.max(line_scores, axis=1, keepdims=True)
            exponent = jnp.exp(line_scores - highest)
            soft = exponent * (1.0 / jnp.sum(exponent, axis=1, keepdims=True))
            score[s, here, :] = soft
            prob[s, here, :] = soft.astype(bf16)
    for s in range(samples):
        attended = dot(values[s], prob[s], 1, 1)
        gate_here, delta_here = gate[s], delta_gated[s]
        gated[s] = (gate_here * attended).astype(bf16)
        delta_attended = (delta_here * gate_here).astype(bf16)
        delta_gate[s] = (delta_here * attended * gate_here * (1.0 - gate_here)).astype(bf16)
        centre = jnp.sum(delta_attended.astype(f32) * attended, axis=0, keepdims=True)
        coarse = centre.astype(bf16).astype(f32)
        rest = jnp.where(
            query_line == 0, -coarse, jnp.where(query_line == 1, coarse - centre, 0.0)
        ).astype(bf16)
        slope[s] = dot(
            jnp.concatenate([delta_attended, rest], axis=0),
            jnp.concatenate([values[s], pair_ones], axis=0),
            0,
            0,
        )
        parted(dot(delta_attended, prob[s], 1, 0), s, 1)
    for piece, start, place in spots:
        here = slice(place, place + step)
        total_here = None
        for s in range(samples):
            delta_scores = score[s, here, :] * slope[s, here, :]
            prob[s, here, :] = delta_scores.astype(bf16)
            total_here = delta_scores if total_here is None else total_here + delta_scores
        delta_bias[piece, 0, start : start + step, :] = total_here.astype(bf16)
    for s in range(samples):
        delta_query[s] = (dot(keys[s], prob[s], 1, 1) * scale).astype(bf16)
        parted(dot(query[s], prob[s], 1, 0) * scale, s, 0)


def attention(
    meta, query, pair_of_cores, gate, delta_gated, bias, part, call, calls, earlier
):
    samples, width, rows = query.shape
    pieces, heads, piece_rows, total = bias.shape
    head_width = width // sum(SHARES)
    step = 16 if piece_rows % 16 == 0 else piece_rows
    count = heads // calls
    inside = call * count
    first = sum(SHARES[:part]) + inside
    padded = pair_of_cores[0].shape[3]

    def spec(columns, offset):
        return pl.BlockSpec((samples, head_width, columns), lambda h, meta: (0, offset + h, 0))

    inner, outer = spec(rows, first), spec(rows, inside)

    def double(columns, offset):
        return pl.BlockSpec(
            (samples, 2, head_width, columns), lambda h, meta: (0, 0, offset + h, 0)
        )

    tile = pl.BlockSpec((pieces, 1, piece_rows, total), lambda h, meta: (0, inside + h, 0, 0))

    def made(dtype, columns=rows, lead=(samples,)):
        return jax.ShapeDtypeStruct(lead + (heads * head_width, columns), dtype)

    return pl.pallas_call(
        functools.partial(attention_kernel, step=step),
        grid_spec=pltpu.PrefetchScalarGridSpec(
            num_scalar_prefetch=1,
            grid=(count,),
            in_specs=[inner]
            + [double(padded, first)] * 2
            + [inner] * 2
            + [tile]
            + [pl.BlockSpec(memory_space=pl.ANY)] * len(earlier),
            out_specs=[outer] * 3 + [double(rows, inside), double(padded, inside), tile],
            scratch_shapes=[
                pltpu.VMEM((samples, rows, total), f32),
                pltpu.VMEM((samples, rows, total), bf16),
                pltpu.VMEM((samples, rows, total), f32),
            ],
        ),
        out_shape=[
            made(bf16), made(bf16), made(bf16), made(f32, rows, (samples, 2)),
            made(bf16, padded, (samples, 2)),
            jax.ShapeDtypeStruct(bias.shape, bf16),
        ],
        input_output_aliases={7 + i: i for i in range(len(earlier))},
        compiler_params=pltpu.CompilerParams(vmem_limit_bytes=VMEM_LIMIT),
        cost_estimate=pl.CostEstimate(flops=1, bytes_accessed=1, transcendentals=0),
    )(meta, query, *pair_of_cores, gate, delta_gated, bias, *earlier)


def centred_project(gain, project):
    weight = (project.astype(f32) * gain.astype(f32)[:, None]).T
    weight = weight - jnp.mean(weight, axis=1, keepdims=True)
    high = lax.reduce_precision(weight, 8, 7)
    return jnp.concatenate([high.astype(bf16), (weight - high).astype(bf16)], axis=0)


def turned_norm(rows):
    turned = rows.T.astype(f32)
    centre = turned - jnp.mean(turned, axis=0, keepdims=True)
    return centre, lax.rsqrt(jnp.mean(centre * centre, axis=0, keepdims=True) + EPSILON)


def head_spots():
    return [(part, i) for part, share in enumerate(SHARES) for i in range(share)]


def pair_forward_kernel(pair, weight, *refs, block, heads):
    outs, wide = refs[:-1], refs[-1]

    def one(i, carry):
        _, factor = turned_norm(pair[i])
        both = dot(weight[...], pair[i], 1, 1)
        line = (both[:heads] + both[heads:]) * factor
        for t in range(wide.shape[0]):
            wide[t, pl.ds(pl.multiple_of(i * heads, heads), heads), :] = line[
                :, t * LANES : (t + 1) * LANES
            ]
        return carry

    lax.fori_loop(0, block, one, 0, unroll=8 if block % 8 == 0 else 1)
    for h, (part, i) in enumerate(head_spots()):
        for t in range(wide.shape[0]):
            outs[part][i, :, t * LANES : (t + 1) * LANES] = wide[
                t, pl.ds(h, block, stride=heads), :
            ].astype(bf16)


def pair_forward(pair, weight):
    rows, length, width = pair.shape
    heads = weight.shape[0] // 2
    block = 16 if rows % 16 == 0 else rows
    return pl.pallas_call(
        functools.partial(pair_forward_kernel, block=block, heads=heads),
        grid=(rows // block,),
        in_specs=[
            pl.BlockSpec((block, length, width), lambda i: (i, 0, 0)),
            pl.BlockSpec((2 * heads, width), lambda i: (0, 0)),
        ],
        out_specs=[pl.BlockSpec((share, block, length), lambda i: (0, i, 0)) for share in SHARES],
        out_shape=[jax.ShapeDtypeStruct((share, rows, length), bf16) for share in SHARES],
        scratch_shapes=[pltpu.VMEM((length // LANES, block * heads, LANES), f32)],
        compiler_params=pltpu.CompilerParams(vmem_limit_bytes=VMEM_LIMIT),
        cost_estimate=pl.CostEstimate(flops=1, bytes_accessed=1, transcendentals=0),
    )(pair, weight)


def pair_backward_kernel(pair, weight, *refs, block, heads):
    deltas = refs[: len(SHARES)]
    out, inner_out, wide, inner_sum = refs[-4:]
    step = pl.program_id(0)

    @pl.when(step == 0)
    def _():
        inner_sum[...] = jnp.zeros_like(inner_sum)

    for h, (part, place) in enumerate(head_spots()):
        for t in range(wide.shape[0]):
            wide[t, h * block : (h + 1) * block, :] = deltas[part][
                place, :, t * LANES : (t + 1) * LANES
            ].astype(f32)

    def one(i, carry):
        centre, factor = turned_norm(pair[i])
        normed = centre * factor
        delta = jnp.concatenate(
            [wide[t, pl.ds(i, heads, stride=block), :] for t in range(wide.shape[0])], axis=1
        ).astype(bf16)
        incoming = dot(weight[...], jnp.concatenate([delta, delta], axis=0), 0, 0)
        inner_sum[...] += dot(delta, normed.astype(bf16), 1, 1)
        along = jnp.mean(incoming * normed, axis=0, keepdims=True)
        out[i] = ((incoming - normed * along) * factor).T
        return carry

    lax.fori_loop(0, block, one, 0, unroll=4 if block % 4 == 0 else 1)

    @pl.when(step == pl.num_programs(0) - 1)
    def _():
        inner_out[...] = inner_sum[...]


def pair_backward(pair, weight, deltas, start, count, earlier):
    rows, length, width = pair.shape
    heads = weight.shape[0] // 2
    parts = len(deltas)
    block = 16 if rows % 16 == 0 else rows
    return pl.pallas_call(
        functools.partial(pair_backward_kernel, block=block, heads=heads),
        grid=(count,),
        in_specs=[
            pl.BlockSpec((block, length, width), lambda i: (start + i, 0, 0)),
            pl.BlockSpec((2 * heads, width), lambda i: (0, 0)),
        ]
        + [
            pl.BlockSpec((share, block, length), lambda i: (0, start + i, 0)) for share in SHARES
        ]
        + [pl.BlockSpec(memory_space=pl.ANY)] * len(earlier),
        out_specs=[
            pl.BlockSpec((block, length, width), lambda i: (start + i, 0, 0)),
            pl.BlockSpec((heads, width), lambda i: (0, 0)),
        ],
        out_shape=[
            jax.ShapeDtypeStruct((rows, length, width), f32),
            jax.ShapeDtypeStruct((heads, width), f32),
        ],
        scratch_shapes=[
            pltpu.VMEM((length // LANES, block * heads, LANES), f32),
            pltpu.VMEM((heads, width), f32),
        ],
        input_output_aliases={2 + parts: 0} if earlier else {},
        compiler_params=pltpu.CompilerParams(vmem_limit_bytes=VMEM_LIMIT),
        cost_estimate=pl.CostEstimate(flops=1, bytes_accessed=1, transcendentals=0),
    )(pair, weight, *deltas, *earlier)


def fixed(shape):
    return pl.BlockSpec(shape, lambda s, *_: (0,) * len(shape), pipeline_mode=pl.Buffered(1))


def by_sample(shape, buffers=2):
    return pl.BlockSpec(
        (1,) + shape,
        lambda s, *_: (s,) + (0,) * len(shape),
        pipeline_mode=pl.Buffered(buffers),
    )


def row_valid(meta, rows):
    place = lax.broadcasted_iota(jnp.int32, (rows, 1), 0) + meta[1] * rows
    return jnp.where(place < meta[0], 1.0, 0.0)


def pack_columns(meta, packs, arrays, start=0):
    tile = packs[0].shape[1]
    for array in arrays:
        depth, share = array.shape[0], array.shape[1] // 2
        for side in range(2):
            core = meta[1] if side == 0 else 1 - meta[1]
            for block in range(share // tile):
                column = pl.multiple_of(core * share + block * tile, LANES)
                packs[side][start + block * depth : start + (block + 1) * depth, :] = array[
                    :, pl.ds(column, tile)
                ].astype(bf16)
        start += depth * (share // tile)


def project_kernel(
    meta, single, cotangent, lifting, shifting, finish, query_bias,
    query_weight, key_weight, value_weight, gate_weight, output_weight,
    query, key_value, gate, delta_gated, mixed_out,
):
    rows = single.shape[1]
    normed, _ = normalize(single[0].astype(f32))
    mixed = (lifting[...] * normed + shifting[...]).astype(bf16)
    mixed_out[0] = mixed
    query[0] = (dot(mixed, query_weight[...], 1, 0) + query_bias[...]).astype(bf16).T
    key_value[0, 0, :, :rows] = dot(mixed, key_weight[...], 1, 0).astype(bf16).T
    key_value[0, 1, :, :rows] = dot(mixed, value_weight[...], 1, 0).astype(bf16).T
    gate[0] = jax.nn.sigmoid(dot(mixed, gate_weight[...], 1, 0)).T
    branch = row_valid(meta, rows) * cotangent[0].astype(f32)
    lifted = (finish[...] * branch).astype(bf16)
    delta_gated[0] = dot(lifted, output_weight[...], 1, 1).T


def project(meta, single, cotangent, lifting, shifting, finish, query_bias, weights):
    samples, rows, width = single.shape
    natural, turned = by_sample((rows, width)), by_sample((width, rows))
    flat, square = fixed((rows, width)), fixed((width, width))
    padded = rows + -rows % LANES
    wide = by_sample((2, width, padded))
    return pl.pallas_call(
        project_kernel,
        grid_spec=pltpu.PrefetchScalarGridSpec(
            num_scalar_prefetch=1,
            grid=(samples,),
            in_specs=[natural, natural, flat, flat, flat, fixed((1, width))] + [square] * 5,
            out_specs=[turned, wide, turned, turned, natural],
        ),
        out_shape=[
            jax.ShapeDtypeStruct(shape, dtype)
            for shape, dtype in (
                ((samples, width, rows), bf16),
                ((samples, 2, width, padded), bf16),
                ((samples, width, rows), f32),
                ((samples, width, rows), f32),
            )
        ]
        + [jax.ShapeDtypeStruct((samples, rows, width), bf16)],
        compiler_params=pltpu.CompilerParams(vmem_limit_bytes=VMEM_LIMIT),
        cost_estimate=pl.CostEstimate(flops=1, bytes_accessed=1, transcendentals=0),
    )(meta, single, cotangent, lifting, shifting, finish, query_bias, *weights)


def transition_kernel(
    meta, single, cotangent, lifting, shifting, closing,
    swish_weight, linear_weight, down_weight,
    closed, delta_second, closing_sum, lift_sum, shift_sum, pack_mine, pack_other,
    swish_sum, linear_sum, down_sum,
):
    rows = single.shape[1]
    sample = pl.program_id(0)
    normed, _ = normalize(single[0].astype(f32))
    mixed = (lifting[...] * normed + shifting[...]).astype(bf16)
    up_swish = dot(mixed, swish_weight[...], 1, 0)
    up_linear = dot(mixed, linear_weight[...], 1, 0)
    squash = jax.nn.sigmoid(up_swish)
    silu = up_swish * squash
    hidden = (silu * up_linear).astype(bf16)
    moved = dot(hidden, down_weight[...], 1, 0)
    closing_here = closing[...]
    branch = row_valid(meta, rows) * cotangent[0].astype(f32)
    closed[0] = closing_here * moved
    delta_moved = (closing_here * branch).astype(bf16)
    delta_hidden = dot(delta_moved, down_weight[...], 1, 1)
    delta_swish = (delta_hidden * up_linear * squash * (1.0 + up_swish * (1.0 - squash))).astype(bf16)
    delta_linear = (delta_hidden * silu).astype(bf16)
    second = dot(delta_swish, swish_weight[...], 1, 1) + dot(
        delta_linear, linear_weight[...], 1, 1
    )
    delta_second[0] = second

    def collect(first):
        def put(ref, value):
            if first:
                ref[...] = value
            else:
                ref[...] += value

        put(closing_sum, branch * moved)
        put(lift_sum, second * normed)
        put(shift_sum, second)
        put(swish_sum, dot(mixed, delta_swish, 0, 0))
        put(linear_sum, dot(mixed, delta_linear, 0, 0))
        put(down_sum, dot(hidden, delta_moved, 0, 0))

    @pl.when(sample == 0)
    def _():
        collect(True)

    @pl.when(sample > 0)
    def _():
        collect(False)

    @pl.when(sample == pl.num_programs(0) - 1)
    def _():
        pack_columns(meta, (pack_mine, pack_other), (swish_sum, linear_sum, down_sum))


def transition(meta, single, cotangent, lifting, shifting, closing, weights, pack_rows):
    samples, rows, width = single.shape
    inner = weights[0].shape[1]
    natural, flat = by_sample((rows, width)), fixed((rows, width))
    up, down = (width, inner), (inner, width)
    pack = (pack_rows, width // 2)
    return pl.pallas_call(
        transition_kernel,
        grid_spec=pltpu.PrefetchScalarGridSpec(
            num_scalar_prefetch=1,
            grid=(samples,),
            in_specs=[natural, natural, flat, flat, flat, fixed(up), fixed(up), fixed(down)],
            out_specs=[natural, natural, flat, flat, flat, fixed(pack), fixed(pack)],
            scratch_shapes=[pltpu.VMEM(up, f32), pltpu.VMEM(up, f32), pltpu.VMEM(down, f32)],
        ),
        out_shape=[
            jax.ShapeDtypeStruct(shape, f32)
            for shape in ((samples, rows, width),) * 2 + ((rows, width),) * 3
        ]
        + [jax.ShapeDtypeStruct(pack, bf16)] * 2,
        compiler_params=pltpu.CompilerParams(vmem_limit_bytes=VMEM_LIMIT),
        cost_estimate=pl.CostEstimate(flops=1, bytes_accessed=1, transcendentals=0),
    )(meta, single, cotangent, lifting, shifting, closing, *weights)


def whole(*parts):
    return jnp.concatenate([part[0] for part in parts], axis=0)


def whole_at(*parts):
    return [jnp.concatenate([part[0, i] for part in parts], axis=0) for i in range(2)]


def put(first, ref, value):
    if first:
        ref[...] = value
    else:
        ref[...] += value


def weights_kernel(
    meta, cotangent, mixed, finish,
    key, value, gated_a, gated_b, gate_a, gate_b, query_a, query_b,
    pack_mine, pack_other, bias_sum,
    query_sum, key_sum, value_sum, gate_sum, output_sum,
):
    rows = cotangent.shape[1]
    sample = pl.program_id(0)
    delta_query = whole(query_a, query_b)
    branch = row_valid(meta, rows) * cotangent[0].astype(f32)
    lifted = (finish[...] * branch).astype(bf16)

    def collect(first):
        put(first, query_sum, dot(delta_query, mixed[0], 1, 0))
        put(first, key_sum, dot(key[0], mixed[0], 1, 0))
        put(first, value_sum, dot(value[0], mixed[0], 1, 0))
        put(first, gate_sum, dot(whole(gate_a, gate_b), mixed[0], 1, 0))
        put(first, output_sum, dot(whole(gated_a, gated_b), lifted, 1, 0))
        put(first, bias_sum, jnp.sum(delta_query.astype(f32), axis=1, keepdims=True))

    @pl.when(sample == 0)
    def _():
        collect(True)

    @pl.when(sample > 0)
    def _():
        collect(False)

    @pl.when(sample == pl.num_programs(0) - 1)
    def _():
        width = query_sum.shape[0]
        half = width // 2
        packs = (pack_mine, pack_other)
        for i, array in enumerate((query_sum, key_sum, value_sum, gate_sum)):
            for side in range(2):
                core = meta[1] if side == 0 else 1 - meta[1]
                row = pl.multiple_of(core * half, LANES)
                packs[side][i * width : (i + 1) * width, :] = array[
                    pl.ds(row, half), :
                ].T.astype(bf16)
        pack_columns(meta, packs, (output_sum,), 4 * width)


def weight_sums(meta, cotangent, mixed, finish, turned, pack_rows):
    samples, rows, width = cotangent.shape
    pack = (pack_rows, width // 2)
    natural = by_sample((rows, width))
    return pl.pallas_call(
        weights_kernel,
        grid_spec=pltpu.PrefetchScalarGridSpec(
            num_scalar_prefetch=1,
            grid=(samples,),
            in_specs=[natural, natural, fixed((rows, width))]
            + [by_sample(array.shape[1:]) for array in turned],
            out_specs=[fixed(pack)] * 2 + [fixed((width, 1))],
            scratch_shapes=[pltpu.VMEM((width, width), f32)] * 5,
        ),
        out_shape=[jax.ShapeDtypeStruct(pack, bf16)] * 2
        + [jax.ShapeDtypeStruct((width, 1), f32)],
        compiler_params=pltpu.CompilerParams(vmem_limit_bytes=VMEM_LIMIT),
        cost_estimate=pl.CostEstimate(flops=1, bytes_accessed=1, transcendentals=0),
    )(meta, cotangent, mixed, finish, *turned)


def rows_kernel(
    meta, single, cotangent, closed, delta_second,
    gated_a, gated_b, gate_a, gate_b, query_a, query_b, kept_a, kept_b, came_a, came_b,
    lifting_first, lifting_second, finish,
    query_weight, key_weight, value_weight, gate_weight, output_weight,
    *refs,
):
    block_out, single_grad, key_out, value_out, finish_sum, lift_first, shift_first = refs[-7:]
    rows = single.shape[1]
    kept, came = whole_at(kept_a, kept_b), whole_at(came_a, came_b)
    delta_key, delta_value = [
        (kept[i] + came[i][:, :rows].astype(f32)).astype(bf16) for i in range(2)
    ]
    key_out[0] = delta_key
    value_out[0] = delta_value
    sample = pl.program_id(0)
    residual = single[0].astype(f32)
    normed, factor = normalize(residual)
    valid = row_valid(meta, rows)
    outgoing = cotangent[0].astype(f32)
    branch = valid * outgoing
    raised = dot(whole(gated_a, gated_b), output_weight[...], 0, 0)
    block_out[0] = (residual + valid * (finish[...] * raised + closed[0])).astype(bf16)
    delta_first = (
        dot(whole(query_a, query_b), query_weight[...], 0, 1)
        + dot(delta_key, key_weight[...], 0, 1)
        + dot(delta_value, value_weight[...], 0, 1)
        + dot(whole(gate_a, gate_b), gate_weight[...], 0, 1)
    )
    incoming = delta_first * lifting_first[...] + delta_second[0] * lifting_second[...]
    single_grad[0] = outgoing + normalize_back(incoming, normed, factor)

    def collect(first):
        put(first, finish_sum, branch * raised)
        put(first, lift_first, delta_first * normed)
        put(first, shift_first, delta_first)

    @pl.when(sample == 0)
    def _():
        collect(True)

    @pl.when(sample > 0)
    def _():
        collect(False)


def rows_back(meta, naturals, halved, flats, weights, start, count, earlier):
    samples, rows, width = naturals[0].shape
    flat, square = fixed((rows, width)), fixed((width, width))

    def moved(shape):
        return pl.BlockSpec((1,) + shape, lambda s, *_: (start + s,) + (0,) * len(shape))

    natural = moved((rows, width))
    return pl.pallas_call(
        rows_kernel,
        grid_spec=pltpu.PrefetchScalarGridSpec(
            num_scalar_prefetch=1,
            grid=(count,),
            in_specs=[natural] * 4
            + [moved(array.shape[1:]) for array in halved]
            + [flat] * 3
            + [square] * 5
            + [pl.BlockSpec(memory_space=pl.ANY)] * len(earlier),
            out_specs=[natural] * 2 + [moved((width, rows))] * 2 + [flat] * 3,
        ),
        out_shape=[
            jax.ShapeDtypeStruct((samples, rows, width), bf16),
            jax.ShapeDtypeStruct((samples, rows, width), f32),
        ]
        + [jax.ShapeDtypeStruct((samples, width, rows), bf16)] * 2
        + [jax.ShapeDtypeStruct((rows, width), f32)] * 3,
        input_output_aliases={23 + i: i for i in range(len(earlier))},
        compiler_params=pltpu.CompilerParams(vmem_limit_bytes=VMEM_LIMIT),
        cost_estimate=pl.CostEstimate(flops=1, bytes_accessed=1, transcendentals=0),
    )(meta, *naturals, *halved, *flats, *weights, *earlier)


def swap_cores(array):
    return lax.ppermute(array, "qry", [(0, 1), (1, 0)])


def traded(array, axis):
    return lax.all_to_all(array, axis, 0, 0)


def spread(array, axis):
    return traded(jnp.broadcast_to(array[None], (lax.axis_size(axis),) + array.shape), axis)


def exchange(array, axis, bit):
    return lax.ppermute(array, axis, [(i, i ^ bit) for i in range(lax.axis_size(axis))])


def pick(array, index):
    return lax.dynamic_index_in_dim(array, index, 0, keepdims=False)


def traded_apart(array, axis):
    place = lax.axis_index(axis)
    return [pick(array, place)] + [
        exchange(pick(array, place ^ shift), axis, shift)
        for shift in range(1, lax.axis_size(axis))
    ]


def spread_apart(array, axis):
    return [array] + [exchange(array, axis, shift) for shift in range(1, lax.axis_size(axis))]


def in_order(pieces, axis):
    place, ordered = lax.axis_index(axis), []
    for j in range(len(pieces)):
        chosen = pieces[j]
        for shift in range(1, len(pieces)):
            chosen = jnp.where(place == shift, pieces[j ^ shift], chosen)
        ordered.append(chosen)
    return jnp.stack(ordered)


def summed(pieces):
    total = pieces[0].astype(f32)
    for i in range(1, len(pieces)):
        total = total + pieces[i].astype(f32)
    return total


def filled(packs, start, arrays):
    packs = list(packs)
    for array in arrays:
        for side, half in enumerate(halves(array)):
            packs[side] = lax.dynamic_update_slice(packs[side], half.astype(bf16), (start, 0))
        start += array.shape[0]
    return packs


def padded_rows(count):
    return count + -count % 512


def tied(*values):
    return lax.optimization_barrier(values)


class SliceTotal:
    def __init__(self, mine, other, apart):
        self.mine, self.state, self.apart = mine, swap_cores(other), apart

    def first(self):
        total = (self.mine.astype(f32) + self.state.astype(f32)).astype(bf16)
        places = lax.axis_size("cplx")
        self.sent = total.reshape(places, -1, total.shape[1])

    def second(self, *others):
        levels = lax.axis_size("smp")
        self.depths = [group.sent.shape[1] for group in (self, *others)]
        totals = [
            summed(group.state).astype(bf16).reshape(levels, -1, group.sent.shape[2])
            for group in (self, *others)
        ]
        self.sent = totals[0] if len(totals) == 1 else jnp.concatenate(totals, axis=1)

    def third(self):
        self.sent = summed(self.state).astype(bf16)

    def fourth(self):
        pieces = self.state
        pieces = in_order(pieces, "smp") if "smp" in self.apart else pieces
        self.sent = pieces.reshape(-1, pieces.shape[2])

    def wait(self, value):
        self.state, value = tied(self.state, value)
        return value

    def lead(self, value):
        self.sent, value = tied(self.sent, value)
        return value

    def trade(self, axis):
        self.state = (traded_apart if axis in self.apart else traded)(self.sent, axis)

    def share(self, axis):
        self.state = (spread_apart if axis in self.apart else spread)(self.sent, axis)

    def result(self):
        pieces = in_order(self.state, "cplx") if "cplx" in self.apart else self.state
        levels = lax.axis_size("smp")
        pieces = pieces.reshape(pieces.shape[0] * levels, -1, pieces.shape[2])
        totals, start = [], 0
        for depth in self.depths:
            share = depth // levels
            piece = pieces[:, start : start + share]
            totals.append(piece.reshape(-1, pieces.shape[2]).astype(f32))
            start += share
        return totals


def total_line(vector):
    vector = vector[0] + swap_cores(vector[1])
    return summed(spread_apart(vector, "smp"))


def sum_samples(array):
    return summed(spread_apart(array.astype(bf16), "smp"))


def halves(array):
    portion = array.shape[-1] // 2
    core = lax.axis_index("qry")
    mine = lax.dynamic_slice_in_dim(array, core * portion, portion, array.ndim - 1)
    other = lax.dynamic_slice_in_dim(array, (1 - core) * portion, portion, array.ndim - 1)
    return mine, other


def gather_rows(piece):
    if piece.shape[1] % 16 == 0:
        return lax.all_gather(piece, "smp", axis=0)
    return lax.all_gather(piece, "smp", axis=1, tiled=True)[None]


def scatter_rows(whole):
    if whole.shape[0] == lax.axis_size("smp"):
        return lax.psum_scatter(whole, "smp", scatter_dimension=0)
    return lax.psum_scatter(whole[0], "smp", scatter_dimension=1, tiled=True)


def per_device(
    single,
    condition,
    pair_features,
    lengths,
    cotangent,
    first_gain,
    first_scale,
    first_offset,
    first_shift,
    query_projection_weight,
    query_bias_vector,
    key_projection_weight,
    value_projection_weight,
    attention_gate_weight,
    attention_output_weight,
    pair_gain,
    pair_project,
    finish_weight,
    finish_offset,
    second_gain,
    second_scale,
    second_offset,
    second_shift,
    transition_swish_weight,
    transition_linear_weight,
    transition_down_weight,
    closing_weight,
    closing_offset,
):
    width = single.shape[3]
    narrow = condition.shape[2]
    half = width // 2
    inner = transition_swish_weight.shape[1]
    heads = pair_project.shape[1]
    meta = jnp.stack([lengths[0], lax.axis_index("qry")]).astype(jnp.int32)
    condition_raw = condition[0]
    condition_norm, condition_factor = normalize(condition_raw.astype(f32))
    pair_weight = centred_project(pair_gain, pair_project)
    bias_pieces = pair_forward(pair_features[0], pair_weight)
    meta, *bias_pieces = tied(meta, *bias_pieces)
    bias_rows = [gather_rows(bias_pieces[0])]
    bias_rows[0], bias_pieces[1] = tied(bias_rows[0], bias_pieces[1])
    bias_rows.append(gather_rows(bias_pieces[1]))

    def modulation(gain, scale_weight, offset, shift_weight):
        low = (condition_norm * gain.astype(f32)).astype(bf16)
        lifting = jax.nn.sigmoid(matmul(low, scale_weight) + offset.astype(f32))
        return low, lifting, matmul(low, shift_weight)

    condition_first, lifting_first, shifting_first = modulation(
        first_gain, first_scale, first_offset, first_shift
    )
    condition_second, lifting_second, shifting_second = modulation(
        second_gain, second_scale, second_offset, second_shift
    )
    finish = jax.nn.sigmoid(matmul(condition_raw, finish_weight) + finish_offset.astype(f32))
    closing = jax.nn.sigmoid(matmul(condition_raw, closing_weight) + closing_offset.astype(f32))
    square_weights = (
        query_projection_weight,
        key_projection_weight,
        value_projection_weight,
        attention_gate_weight,
        attention_output_weight,
    )
    closed, delta_second, closing_sum, lift_second, shift_second, *second_packs = transition(
        meta,
        single[0],
        cotangent[0],
        lifting_second,
        shifting_second,
        closing,
        (transition_swish_weight, transition_linear_weight, transition_down_weight),
        padded_rows(3 * inner + 3 * narrow),
    )

    def modulation_back(lift_sum, shift_sum, low, lifting, scale_weight, shift_weight):
        delta_lift = lift_sum * lifting * (1.0 - lifting)
        scale_total = contract("qc,qd->cd", low, delta_lift)
        shift_total = contract("qc,qd->cd", low, shift_sum)
        delta_condition = contract("qd,cd->qc", delta_lift, scale_weight) + contract(
            "qd,cd->qc", shift_sum, shift_weight
        )
        return scale_total, jnp.sum(delta_lift, axis=0), shift_total, delta_condition

    def gate_back(branch_sum, opened, weight):
        delta = branch_sum * opened * (1.0 - opened)
        return (
            contract("qc,qd->cd", condition_raw, delta),
            jnp.sum(delta, axis=0),
            contract("qd,cd->qc", delta, weight),
        )

    scale_second, offset_second, shift_total_second, cond_delta_second = modulation_back(
        lift_second, shift_second, condition_second, lifting_second, second_scale, second_shift
    )
    closing_total, closing_offset_total, condition_closing = gate_back(
        closing_sum, closing, closing_weight
    )
    early = SliceTotal(
        *filled(second_packs, 3 * inner, (scale_second, shift_total_second, closing_total)),
        apart=EARLY_APART,
    )

    early.mine, meta = tied(early.mine, meta)
    query, key_value, gate, delta_gated, mixed_first = project(
        meta,
        single[0],
        cotangent[0],
        lifting_first,
        shifting_first,
        finish,
        query_bias_vector.astype(f32)[None],
        square_weights,
    )
    pair_of_cores = (key_value, swap_cores(key_value))
    def attend(meta, part, call, earlier):
        return list(
            attention(
                meta, query, pair_of_cores, gate, delta_gated, bias_rows[part], part, call, CALLS,
                earlier,
            )
        )

    attended = []
    query = early.wait(query)
    early.first()
    meta = early.lead(meta)
    early.trade("cplx")
    attended = [attend(meta, 0, 1, attend(meta, 0, 0, ()))]
    done = attend(meta, 1, 0, ())
    done[0] = early.wait(done[0])
    early.second()
    meta = early.lead(meta)
    early.trade("smp")
    attended.append(attend(meta, 1, 1, done))
    delta_bias = [scatter_rows(part[5]) for part in attended]

    def both(index):
        return [part[index] for part in attended]

    arrived = [swap_cores(part) for part in both(4)]
    halved = both(0) + both(1) + both(2)
    def back(meta, start, earlier):
        outs = rows_back(
            meta,
            (single[0], cotangent[0], closed, delta_second),
            halved + both(3) + arrived,
            (lifting_first, lifting_second, finish),
            square_weights,
            start,
            single.shape[1] // 2,
            earlier,
        )
        return list(outs)

    done = back(meta, 0, ())
    last = back(meta, single.shape[1] // 2, tuple(done[:4]))
    block_out, single_grad, delta_key, delta_value = last[:4]
    finish_sum, lift_first, shift_first = [done[i] + last[i] for i in (4, 5, 6)]
    scale_first, offset_first, shift_total_first, cond_delta_first = modulation_back(
        lift_first, shift_first, condition_first, lifting_first, first_scale, first_shift
    )
    finish_total, finish_offset_total, condition_finish = gate_back(
        finish_sum, finish, finish_weight
    )
    *first_packs, query_bias_total = weight_sums(
        meta,
        cotangent[0],
        mixed_first,
        finish,
        [delta_key, delta_value] + halved,
        padded_rows(5 * width + 3 * narrow),
    )
    first_packs[1] = early.wait(first_packs[1])
    early.third()
    first_packs[1] = early.lead(first_packs[1])
    early.share("smp")
    late = SliceTotal(
        *filled(first_packs, 5 * width, (scale_first, shift_total_first, finish_total)),
        apart=LATE_APART,
    )
    gain_first = jnp.sum(cond_delta_first * condition_norm, axis=0)
    gain_second = jnp.sum(cond_delta_second * condition_norm, axis=0)
    condition_grad = sum_samples(
        normalize_back(
            cond_delta_first * first_gain.astype(f32) + cond_delta_second * second_gain.astype(f32),
            condition_norm,
            condition_factor,
        )
        + condition_closing
        + condition_finish
    )
    blocks = pair_features.shape[1] // 16 if pair_features.shape[1] % 16 == 0 else 1
    sizes = (blocks - blocks // 2, blocks // 2)
    delta_bias[0] = late.wait(delta_bias[0])
    late.first()
    pair_weight = late.lead(pair_weight)
    late.trade("cplx")
    early.state, late.state, delta_bias[1] = tied(early.state, late.state, delta_bias[1])
    early.fourth()
    pair_weight = early.lead(pair_weight)
    early.share("cplx")
    late.second()
    pair_weight = late.lead(pair_weight)
    late.trade("smp")
    pair_grad, inner_total = pair_backward(
        pair_features[0], pair_weight, delta_bias, 0, sizes[0], ()
    )
    inner_total = late.wait(inner_total)
    late.third()
    pair_weight = late.lead(pair_weight)
    late.share("smp")
    if sizes[1]:
        pair_grad, more = pair_backward(
            pair_features[0], pair_weight, delta_bias, *sizes, (pair_grad,)
        )
        inner_total = inner_total + more
    early.state = late.wait(early.state)
    late.fourth()
    late.share("cplx")
    pair_gain_total = jnp.sum(inner_total * pair_project.astype(f32).T, axis=0)
    pair_project_total = inner_total * pair_gain.astype(f32)[None]
    vectors = (
        gain_first,
        offset_first,
        query_bias_total[:, 0],
        finish_offset_total,
        gain_second,
        offset_second,
        closing_offset_total,
        pair_gain_total,
    )
    small = total_line(
        jnp.concatenate(
            [jnp.stack(halves(vector)) for vector in vectors]
            + [jnp.stack([half.reshape(-1) for half in halves(pair_project_total.T)])],
            axis=1,
        )
    )
    small = summed(spread_apart(small, "cplx"))
    late = late.result()[0]
    early = early.result()[0]
    ends, place = [], 0
    for vector in vectors:
        ends.append(small[place : place + vector.shape[0] // 2])
        place += vector.shape[0] // 2
    def unpack(total, sizes):
        arrays, start = [], 0
        for depth, columns in sizes:
            blocks = columns // half
            arrays.append(
                jnp.concatenate(
                    [
                        total[start + b * depth : start + (b + 1) * depth]
                        for b in range(blocks)
                    ],
                    axis=1,
                )
            )
            start += depth * blocks
        return arrays

    swish_total, linear_total, down_total, scale_second, shift_second, closing_total = unpack(
        early,
        ((width, inner // 2), (width, inner // 2), (inner, half)) + ((narrow, half),) * 3,
    )
    query_total, key_total, value_total, gate_total, output_total, *others = unpack(
        late, ((width, half),) * 5 + ((narrow, half),) * 3
    )
    scale_first, shift_first, finish_total = others
    return (
        block_out[None],
        single_grad[None],
        condition_grad[None],
        pair_grad[None],
        ends[0],
        scale_first,
        ends[1],
        shift_first,
        query_total,
        ends[2],
        key_total,
        value_total,
        gate_total,
        output_total,
        ends[7],
        small[place:].reshape(-1, heads // 2),
        finish_total,
        ends[3],
        ends[4],
        scale_second,
        ends[5],
        shift_second,
        swish_total,
        linear_total,
        down_total,
        closing_total,
        ends[6],
    )


def solution(mesh):
    placed = (
        P("cplx", "smp", "qry", None),
        P("cplx", "qry", None),
        P("cplx", ("qry", "smp"), None, None),
        P("cplx"),
        P("cplx", "smp", "qry", None),
        P(),
        P(),
        P(),
        P(),
        P(),
        P(),
        P(),
        P(),
        P(),
        P(),
        P(),
        P(),
        P(),
        P(),
        P(),
        P(),
        P(),
        P(),
        P(),
        P(),
        P(),
        P(),
        P(),
    )
    return jax.shard_map(
        per_device,
        mesh=mesh,
        in_specs=placed,
        out_specs=(
            P("cplx", "smp", "qry", None),
            P("cplx", "smp", "qry", None),
            P("cplx", "qry", None),
            P("cplx", ("qry", "smp"), None, None),
            P("qry"),
            P(None, "qry"),
            P("qry"),
            P(None, "qry"),
            P(None, "qry"),
            P("qry"),
            P(None, "qry"),
            P(None, "qry"),
            P(None, "qry"),
            P(None, "qry"),
            P("qry"),
            P(None, "qry"),
            P(None, "qry"),
            P("qry"),
            P("qry"),
            P(None, "qry"),
            P("qry"),
            P(None, "qry"),
            P(None, "qry"),
            P(None, "qry"),
            P(None, "qry"),
            P(None, "qry"),
            P("qry"),
        ),
        check_vma=False,
    )
```

```python
import functools

import jax
import jax.numpy as jnp
from jax import lax
from jax.experimental import pallas as pl
from jax.experimental.pallas import tpu as pltpu
from jax.sharding import PartitionSpec as P

EPSILON = 1e-05
LANES = 128
VMEM_LIMIT = 56 * 2**20
SHARES = (10, 6)
CALLS = 2
EARLY_APART = ("smp",)
LATE_APART = ("smp",)
f32 = jnp.float32
bf16 = jnp.bfloat16


def normalize(values):
    centre = values - jnp.mean(values, axis=-1, keepdims=True)
    factor = lax.rsqrt(jnp.mean(centre * centre, axis=-1, keepdims=True) + EPSILON)
    return (centre * factor, factor)


def normalize_back(incoming, normed, factor):
    return factor * (
        incoming
        - jnp.mean(incoming, axis=-1, keepdims=True)
        - normed * jnp.mean(incoming * normed, axis=-1, keepdims=True)
    )


def matmul(left, right):
    return jnp.dot(left, right, preferred_element_type=jnp.float32)


def contract(form, left, right):
    return jnp.einsum(
        form, left.astype(bf16), right.astype(bf16), preferred_element_type=jnp.float32
    )


def dot(left, right, left_dim, right_dim):
    return lax.dot_general(
        left, right, (((left_dim,), (right_dim,)), ((), ())), preferred_element_type=f32
    )


def attention_kernel(
    meta, query, mine, other, gate, delta_gated, bias, *refs, step
):
    (
        gated, delta_gate, delta_query, kept, sent, delta_bias, score, prob, slope,
    ) = refs[-9:]
    samples, head_width, rows = query.shape
    total = 2 * rows
    pieces, piece_rows = bias.shape[0], bias.shape[2]
    scale = head_width ** (-0.5)
    second = meta[1] == 1
    column = lax.broadcasted_iota(jnp.int32, (16, total), 1)
    line = lax.broadcasted_iota(jnp.int32, (16, total), 0)
    masking = jnp.where((line == 0) & (column >= meta[0]), -1e30, 0.0).astype(bf16)
    pair_ones = jnp.where(line < 2, 1.0, 0.0).astype(bf16)
    query_line = lax.broadcasted_iota(jnp.int32, (16, rows), 0)
    one_line = jnp.where(query_line == 0, 1.0, 0.0).astype(bf16)
    spots = [
        (piece, start, piece * piece_rows + start)
        for piece in range(pieces)
        for start in range(0, piece_rows, step)
    ]

    def joined(mine, other):
        mine, other = mine[:, :rows], other[:, :rows]
        first = jnp.where(second, other, mine)
        last = jnp.where(second, mine, other)
        return jnp.concatenate([first, last], axis=1)

    def parted(whole, sample, which):
        first, last = whole[:, :rows], whole[:, rows:]
        kept[sample, which] = jnp.where(second, last, first)
        sent[sample, which, :, :rows] = jnp.where(second, first, last).astype(sent.dtype)

    keys, values = [], []
    for s in range(samples):
        keys.append(joined(mine[s, 0], other[s, 0]))
        values.append(joined(mine[s, 1], other[s, 1]))
        score[s] = dot(
            jnp.concatenate([query[s], one_line], axis=0),
            jnp.concatenate([keys[s], masking], axis=0),
            0,
            0,
        )
    for piece, start, place in spots:
        bias_here = bias[piece, 0, start : start + step, :].astype(f32)
        here = slice(place, place + step)
        for s in range(samples):
            line_scores = score[s, here, :] * scale + bias_here
            highest = jnp.max(line_scores, axis=1, keepdims=True)
            exponent = jnp.exp(line_scores - highest)
            soft = exponent * (1.0 / jnp.sum(exponent, axis=1, keepdims=True))
            score[s, here, :] = soft
            prob[s, here, :] = soft.astype(bf16)
    for s in range(samples):
        attended = dot(values[s], prob[s], 1, 1)
        gate_here, delta_here = gate[s], delta_gated[s]
        gated[s] = (gate_here * attended).astype(bf16)
        delta_attended = (delta_here * gate_here).astype(bf16)
        delta_gate[s] = (delta_here * attended * gate_here * (1.0 - gate_here)).astype(bf16)
        centre = jnp.sum(delta_attended.astype(f32) * attended, axis=0, keepdims=True)
        coarse = centre.astype(bf16).astype(f32)
        rest = jnp.where(
            query_line == 0, -coarse, jnp.where(query_line == 1, coarse - centre, 0.0)
        ).astype(bf16)
        slope[s] = dot(
            jnp.concatenate([delta_attended, rest], axis=0),
            jnp.concatenate([values[s], pair_ones], axis=0),
            0,
            0,
        )
        parted(dot(delta_attended, prob[s], 1, 0), s, 1)
    for piece, start, place in spots:
        here = slice(place, place + step)
        total_here = None
        for s in range(samples):
            delta_scores = score[s, here, :] * slope[s, here, :]
            prob[s, here, :] = delta_scores.astype(bf16)
            total_here = delta_scores if total_here is None else total_here + delta_scores
        delta_bias[piece, 0, start : start + step, :] = total_here.astype(bf16)
    for s in range(samples):
        delta_query[s] = (dot(keys[s], prob[s], 1, 1) * scale).astype(bf16)
        parted(dot(query[s], prob[s], 1, 0) * scale, s, 0)


def attention(
    meta, query, pair_of_cores, gate, delta_gated, bias, part, call, calls, earlier
):
    samples, width, rows = query.shape
    pieces, heads, piece_rows, total = bias.shape
    head_width = width // sum(SHARES)
    step = 16 if piece_rows % 16 == 0 else piece_rows
    count = heads // calls
    inside = call * count
    first = sum(SHARES[:part]) + inside
    padded = pair_of_cores[0].shape[3]

    def spec(columns, offset):
        return pl.BlockSpec((samples, head_width, columns), lambda h, meta: (0, offset + h, 0))

    inner, outer = spec(rows, first), spec(rows, inside)

    def double(columns, offset):
        return pl.BlockSpec(
            (samples, 2, head_width, columns), lambda h, meta: (0, 0, offset + h, 0)
        )

    tile = pl.BlockSpec((pieces, 1, piece_rows, total), lambda h, meta: (0, inside + h, 0, 0))

    def made(dtype, columns=rows, lead=(samples,)):
        return jax.ShapeDtypeStruct(lead + (heads * head_width, columns), dtype)

    return pl.pallas_call(
        functools.partial(attention_kernel, step=step),
        grid_spec=pltpu.PrefetchScalarGridSpec(
            num_scalar_prefetch=1,
            grid=(count,),
            in_specs=[inner]
            + [double(padded, first)] * 2
            + [inner] * 2
            + [tile]
            + [pl.BlockSpec(memory_space=pl.ANY)] * len(earlier),
            out_specs=[outer] * 3 + [double(rows, inside), double(padded, inside), tile],
            scratch_shapes=[
                pltpu.VMEM((samples, rows, total), f32),
                pltpu.VMEM((samples, rows, total), bf16),
                pltpu.VMEM((samples, rows, total), f32),
            ],
        ),
        out_shape=[
            made(bf16), made(bf16), made(bf16), made(f32, rows, (samples, 2)),
            made(bf16, padded, (samples, 2)),
            jax.ShapeDtypeStruct(bias.shape, bf16),
        ],
        input_output_aliases={7 + i: i for i in range(len(earlier))},
        compiler_params=pltpu.CompilerParams(vmem_limit_bytes=VMEM_LIMIT),
        cost_estimate=pl.CostEstimate(flops=1, bytes_accessed=1, transcendentals=0),
    )(meta, query, *pair_of_cores, gate, delta_gated, bias, *earlier)


def centred_project(gain, project):
    weight = (project.astype(f32) * gain.astype(f32)[:, None]).T
    weight = weight - jnp.mean(weight, axis=1, keepdims=True)
    high = lax.reduce_precision(weight, 8, 7)
    return jnp.concatenate([high.astype(bf16), (weight - high).astype(bf16)], axis=0)


def turned_norm(rows):
    turned = rows.T.astype(f32)
    centre = turned - jnp.mean(turned, axis=0, keepdims=True)
    return centre, lax.rsqrt(jnp.mean(centre * centre, axis=0, keepdims=True) + EPSILON)


def head_spots():
    return [(part, i) for part, share in enumerate(SHARES) for i in range(share)]


def pair_forward_kernel(pair, weight, *refs, block, heads):
    outs, wide = refs[:-1], refs[-1]

    def one(i, carry):
        _, factor = turned_norm(pair[i])
        both = dot(weight[...], pair[i], 1, 1)
        line = (both[:heads] + both[heads:]) * factor
        for t in range(wide.shape[0]):
            wide[t, pl.ds(pl.multiple_of(i * heads, heads), heads), :] = line[
                :, t * LANES : (t + 1) * LANES
            ]
        return carry

    lax.fori_loop(0, block, one, 0, unroll=8 if block % 8 == 0 else 1)
    for h, (part, i) in enumerate(head_spots()):
        for t in range(wide.shape[0]):
            outs[part][i, :, t * LANES : (t + 1) * LANES] = wide[
                t, pl.ds(h, block, stride=heads), :
            ].astype(bf16)


def pair_forward(pair, weight):
    rows, length, width = pair.shape
    heads = weight.shape[0] // 2
    block = 16 if rows % 16 == 0 else rows
    return pl.pallas_call(
        functools.partial(pair_forward_kernel, block=block, heads=heads),
        grid=(rows // block,),
        in_specs=[
            pl.BlockSpec((block, length, width), lambda i: (i, 0, 0)),
            pl.BlockSpec((2 * heads, width), lambda i: (0, 0)),
        ],
        out_specs=[pl.BlockSpec((share, block, length), lambda i: (0, i, 0)) for share in SHARES],
        out_shape=[jax.ShapeDtypeStruct((share, rows, length), bf16) for share in SHARES],
        scratch_shapes=[pltpu.VMEM((length // LANES, block * heads, LANES), f32)],
        compiler_params=pltpu.CompilerParams(vmem_limit_bytes=VMEM_LIMIT),
        cost_estimate=pl.CostEstimate(flops=1, bytes_accessed=1, transcendentals=0),
    )(pair, weight)


def pair_backward_kernel(pair, weight, *refs, block, heads):
    deltas = refs[: len(SHARES)]
    out, inner_out, wide, inner_sum = refs[-4:]
    step = pl.program_id(0)

    @pl.when(step == 0)
    def _():
        inner_sum[...] = jnp.zeros_like(inner_sum)

    for h, (part, place) in enumerate(head_spots()):
        for t in range(wide.shape[0]):
            wide[t, h * block : (h + 1) * block, :] = deltas[part][
                place, :, t * LANES : (t + 1) * LANES
            ].astype(f32)

    def one(i, carry):
        centre, factor = turned_norm(pair[i])
        normed = centre * factor
        delta = jnp.concatenate(
            [wide[t, pl.ds(i, heads, stride=block), :] for t in range(wide.shape[0])], axis=1
        ).astype(bf16)
        incoming = dot(weight[...], jnp.concatenate([delta, delta], axis=0), 0, 0)
        inner_sum[...] += dot(delta, normed.astype(bf16), 1, 1)
        along = jnp.mean(incoming * normed, axis=0, keepdims=True)
        out[i] = ((incoming - normed * along) * factor).T
        return carry

    lax.fori_loop(0, block, one, 0, unroll=4 if block % 4 == 0 else 1)

    @pl.when(step == pl.num_programs(0) - 1)
    def _():
        inner_out[...] = inner_sum[...]


def pair_backward(pair, weight, deltas, start, count, earlier):
    rows, length, width = pair.shape
    heads = weight.shape[0] // 2
    parts = len(deltas)
    block = 16 if rows % 16 == 0 else rows
    return pl.pallas_call(
        functools.partial(pair_backward_kernel, block=block, heads=heads),
        grid=(count,),
        in_specs=[
            pl.BlockSpec((block, length, width), lambda i: (start + i, 0, 0)),
            pl.BlockSpec((2 * heads, width), lambda i: (0, 0)),
        ]
        + [
            pl.BlockSpec((share, block, length), lambda i: (0, start + i, 0)) for share in SHARES
        ]
        + [pl.BlockSpec(memory_space=pl.ANY)] * len(earlier),
        out_specs=[
            pl.BlockSpec((block, length, width), lambda i: (start + i, 0, 0)),
            pl.BlockSpec((heads, width), lambda i: (0, 0)),
        ],
        out_shape=[
            jax.ShapeDtypeStruct((rows, length, width), f32),
            jax.ShapeDtypeStruct((heads, width), f32),
        ],
        scratch_shapes=[
            pltpu.VMEM((length // LANES, block * heads, LANES), f32),
            pltpu.VMEM((heads, width), f32),
        ],
        input_output_aliases={2 + parts: 0} if earlier else {},
        compiler_params=pltpu.CompilerParams(vmem_limit_bytes=VMEM_LIMIT),
        cost_estimate=pl.CostEstimate(flops=1, bytes_accessed=1, transcendentals=0),
    )(pair, weight, *deltas, *earlier)


def fixed(shape):
    return pl.BlockSpec(shape, lambda s, *_: (0,) * len(shape), pipeline_mode=pl.Buffered(1))


def by_sample(shape, buffers=2):
    return pl.BlockSpec(
        (1,) + shape,
        lambda s, *_: (s,) + (0,) * len(shape),
        pipeline_mode=pl.Buffered(buffers),
    )


def row_valid(meta, rows):
    place = lax.broadcasted_iota(jnp.int32, (rows, 1), 0) + meta[1] * rows
    return jnp.where(place < meta[0], 1.0, 0.0)


def pack_columns(meta, packs, arrays, start=0):
    tile = packs[0].shape[1]
    for array in arrays:
        depth, share = array.shape[0], array.shape[1] // 2
        for side in range(2):
            core = meta[1] if side == 0 else 1 - meta[1]
            for block in range(share // tile):
                column = pl.multiple_of(core * share + block * tile, LANES)
                packs[side][start + block * depth : start + (block + 1) * depth, :] = array[
                    :, pl.ds(column, tile)
                ].astype(bf16)
        start += depth * (share // tile)


def project_kernel(
    meta, single, cotangent, lifting, shifting, finish, query_bias,
    query_weight, key_weight, value_weight, gate_weight, output_weight,
    query, key_value, gate, delta_gated, mixed_out,
):
    rows = single.shape[1]
    normed, _ = normalize(single[0].astype(f32))
    mixed = (lifting[...] * normed + shifting[...]).astype(bf16)
    mixed_out[0] = mixed
    query[0] = (dot(mixed, query_weight[...], 1, 0) + query_bias[...]).astype(bf16).T
    key_value[0, 0, :, :rows] = dot(mixed, key_weight[...], 1, 0).astype(bf16).T
    key_value[0, 1, :, :rows] = dot(mixed, value_weight[...], 1, 0).astype(bf16).T
    gate[0] = jax.nn.sigmoid(dot(mixed, gate_weight[...], 1, 0)).T
    branch = row_valid(meta, rows) * cotangent[0].astype(f32)
    lifted = (finish[...] * branch).astype(bf16)
    delta_gated[0] = dot(lifted, output_weight[...], 1, 1).T


def project(meta, single, cotangent, lifting, shifting, finish, query_bias, weights):
    samples, rows, width = single.shape
    natural, turned = by_sample((rows, width)), by_sample((width, rows))
    flat, square = fixed((rows, width)), fixed((width, width))
    padded = rows + -rows % LANES
    wide = by_sample((2, width, padded))
    return pl.pallas_call(
        project_kernel,
        grid_spec=pltpu.PrefetchScalarGridSpec(
            num_scalar_prefetch=1,
            grid=(samples,),
            in_specs=[natural, natural, flat, flat, flat, fixed((1, width))] + [square] * 5,
            out_specs=[turned, wide, turned, turned, natural],
        ),
        out_shape=[
            jax.ShapeDtypeStruct(shape, dtype)
            for shape, dtype in (
                ((samples, width, rows), bf16),
                ((samples, 2, width, padded), bf16),
                ((samples, width, rows), f32),
                ((samples, width, rows), f32),
            )
        ]
        + [jax.ShapeDtypeStruct((samples, rows, width), bf16)],
        compiler_params=pltpu.CompilerParams(vmem_limit_bytes=VMEM_LIMIT),
        cost_estimate=pl.CostEstimate(flops=1, bytes_accessed=1, transcendentals=0),
    )(meta, single, cotangent, lifting, shifting, finish, query_bias, *weights)


def transition_kernel(
    meta, single, cotangent, lifting, shifting, closing,
    swish_weight, linear_weight, down_weight,
    closed, delta_second, closing_sum, lift_sum, shift_sum, pack_mine, pack_other,
    swish_sum, linear_sum, down_sum,
):
    rows = single.shape[1]
    sample = pl.program_id(0)
    normed, _ = normalize(single[0].astype(f32))
    mixed = (lifting[...] * normed + shifting[...]).astype(bf16)
    up_swish = dot(mixed, swish_weight[...], 1, 0)
    up_linear = dot(mixed, linear_weight[...], 1, 0)
    squash = jax.nn.sigmoid(up_swish)
    silu = up_swish * squash
    hidden = (silu * up_linear).astype(bf16)
    moved = dot(hidden, down_weight[...], 1, 0)
    closing_here = closing[...]
    branch = row_valid(meta, rows) * cotangent[0].astype(f32)
    closed[0] = closing_here * moved
    delta_moved = (closing_here * branch).astype(bf16)
    delta_hidden = dot(delta_moved, down_weight[...], 1, 1)
    delta_swish = (delta_hidden * up_linear * squash * (1.0 + up_swish * (1.0 - squash))).astype(bf16)
    delta_linear = (delta_hidden * silu).astype(bf16)
    second = dot(delta_swish, swish_weight[...], 1, 1) + dot(
        delta_linear, linear_weight[...], 1, 1
    )
    delta_second[0] = second

    def collect(first):
        def put(ref, value):
            if first:
                ref[...] = value
            else:
                ref[...] += value

        put(closing_sum, branch * moved)
        put(lift_sum, second * normed)
        put(shift_sum, second)
        put(swish_sum, dot(mixed, delta_swish, 0, 0))
        put(linear_sum, dot(mixed, delta_linear, 0, 0))
        put(down_sum, dot(hidden, delta_moved, 0, 0))

    @pl.when(sample == 0)
    def _():
        collect(True)

    @pl.when(sample > 0)
    def _():
        collect(False)

    @pl.when(sample == pl.num_programs(0) - 1)
    def _():
        pack_columns(meta, (pack_mine, pack_other), (swish_sum, linear_sum, down_sum))


def transition(meta, single, cotangent, lifting, shifting, closing, weights, pack_rows):
    samples, rows, width = single.shape
    inner = weights[0].shape[1]
    natural, flat = by_sample((rows, width)), fixed((rows, width))
    up, down = (width, inner), (inner, width)
    pack = (pack_rows, width // 2)
    return pl.pallas_call(
        transition_kernel,
        grid_spec=pltpu.PrefetchScalarGridSpec(
            num_scalar_prefetch=1,
            grid=(samples,),
            in_specs=[natural, natural, flat, flat, flat, fixed(up), fixed(up), fixed(down)],
            out_specs=[natural, natural, flat, flat, flat, fixed(pack), fixed(pack)],
            scratch_shapes=[pltpu.VMEM(up, f32), pltpu.VMEM(up, f32), pltpu.VMEM(down, f32)],
        ),
        out_shape=[
            jax.ShapeDtypeStruct(shape, f32)
            for shape in ((samples, rows, width),) * 2 + ((rows, width),) * 3
        ]
        + [jax.ShapeDtypeStruct(pack, bf16)] * 2,
        compiler_params=pltpu.CompilerParams(vmem_limit_bytes=VMEM_LIMIT),
        cost_estimate=pl.CostEstimate(flops=1, bytes_accessed=1, transcendentals=0),
    )(meta, single, cotangent, lifting, shifting, closing, *weights)


def whole(*parts):
    return jnp.concatenate([part[0] for part in parts], axis=0)


def whole_at(*parts):
    return [jnp.concatenate([part[0, i] for part in parts], axis=0) for i in range(2)]


def put(first, ref, value):
    if first:
        ref[...] = value
    else:
        ref[...] += value


def weights_kernel(
    meta, cotangent, mixed, finish,
    key, value, gated_a, gated_b, gate_a, gate_b, query_a, query_b,
    pack_mine, pack_other, bias_sum,
    query_sum, key_sum, value_sum, gate_sum, output_sum,
):
    count, rows, width = cotangent.shape
    sample = pl.program_id(0)

    def turned(*parts):
        return jnp.concatenate(
            [jnp.concatenate([part[i] for part in parts], axis=0) for i in range(count)], axis=1
        )

    delta_query = turned(query_a, query_b)
    mixed_rows = mixed[...].reshape(count * rows, width)
    masked = finish[...] * row_valid(meta, rows)
    lifted = jnp.concatenate(
        [(masked * cotangent[i].astype(f32)).astype(bf16) for i in range(count)], axis=0
    )

    def collect(first):
        put(first, query_sum, dot(delta_query, mixed_rows, 1, 0))
        put(first, key_sum, dot(turned(key), mixed_rows, 1, 0))
        put(first, value_sum, dot(turned(value), mixed_rows, 1, 0))
        put(first, gate_sum, dot(turned(gate_a, gate_b), mixed_rows, 1, 0))
        put(first, output_sum, dot(turned(gated_a, gated_b), lifted, 1, 0))
        put(first, bias_sum, jnp.sum(delta_query.astype(f32), axis=1, keepdims=True))

    @pl.when(sample == 0)
    def _():
        collect(True)

    @pl.when(sample > 0)
    def _():
        collect(False)

    @pl.when(sample == pl.num_programs(0) - 1)
    def _():
        width = query_sum.shape[0]
        half = width // 2
        packs = (pack_mine, pack_other)
        for i, array in enumerate((query_sum, key_sum, value_sum, gate_sum)):
            for side in range(2):
                core = meta[1] if side == 0 else 1 - meta[1]
                row = pl.multiple_of(core * half, LANES)
                packs[side][i * width : (i + 1) * width, :] = array[
                    pl.ds(row, half), :
                ].T.astype(bf16)
        pack_columns(meta, packs, (output_sum,), 4 * width)


def weight_sums(meta, cotangent, mixed, finish, turned, pack_rows):
    samples, rows, width = cotangent.shape
    pack = (pack_rows, width // 2)
    count = 2 if samples % 2 == 0 else 1

    def several(shape):
        return pl.BlockSpec((count,) + shape, lambda s, *_: (s,) + (0,) * len(shape))

    natural = several((rows, width))
    return pl.pallas_call(
        weights_kernel,
        grid_spec=pltpu.PrefetchScalarGridSpec(
            num_scalar_prefetch=1,
            grid=(samples // count,),
            in_specs=[natural, natural, fixed((rows, width))]
            + [several(array.shape[1:]) for array in turned],
            out_specs=[fixed(pack)] * 2 + [fixed((width, 1))],
            scratch_shapes=[pltpu.VMEM((width, width), f32)] * 5,
        ),
        out_shape=[jax.ShapeDtypeStruct(pack, bf16)] * 2
        + [jax.ShapeDtypeStruct((width, 1), f32)],
        compiler_params=pltpu.CompilerParams(vmem_limit_bytes=VMEM_LIMIT),
        cost_estimate=pl.CostEstimate(flops=1, bytes_accessed=1, transcendentals=0),
    )(meta, cotangent, mixed, finish, *turned)


def rows_kernel(
    meta, single, cotangent, closed, delta_second,
    gated_a, gated_b, gate_a, gate_b, query_a, query_b, kept_a, kept_b, came_a, came_b,
    lifting_first, lifting_second, finish,
    query_weight, key_weight, value_weight, gate_weight, output_weight,
    *refs,
):
    block_out, single_grad, key_out, value_out, finish_sum, lift_first, shift_first = refs[-7:]
    rows = single.shape[1]
    kept, came = whole_at(kept_a, kept_b), whole_at(came_a, came_b)
    delta_key, delta_value = [
        (kept[i] + came[i][:, :rows].astype(f32)).astype(bf16) for i in range(2)
    ]
    key_out[0] = delta_key
    value_out[0] = delta_value
    sample = pl.program_id(0)
    residual = single[0].astype(f32)
    normed, factor = normalize(residual)
    valid = row_valid(meta, rows)
    outgoing = cotangent[0].astype(f32)
    branch = valid * outgoing
    raised = dot(whole(gated_a, gated_b), output_weight[...], 0, 0)
    block_out[0] = (residual + valid * (finish[...] * raised + closed[0])).astype(bf16)
    delta_first = (
        dot(whole(query_a, query_b), query_weight[...], 0, 1)
        + dot(delta_key, key_weight[...], 0, 1)
        + dot(delta_value, value_weight[...], 0, 1)
        + dot(whole(gate_a, gate_b), gate_weight[...], 0, 1)
    )
    incoming = delta_first * lifting_first[...] + delta_second[0] * lifting_second[...]
    single_grad[0] = outgoing + normalize_back(incoming, normed, factor)

    def collect(first):
        put(first, finish_sum, branch * raised)
        put(first, lift_first, delta_first * normed)
        put(first, shift_first, delta_first)

    @pl.when(sample == 0)
    def _():
        collect(True)

    @pl.when(sample > 0)
    def _():
        collect(False)


def rows_back(meta, naturals, halved, flats, weights, start, count, earlier):
    samples, rows, width = naturals[0].shape
    flat, square = fixed((rows, width)), fixed((width, width))

    def moved(shape):
        return pl.BlockSpec((1,) + shape, lambda s, *_: (start + s,) + (0,) * len(shape))

    natural = moved((rows, width))
    return pl.pallas_call(
        rows_kernel,
        grid_spec=pltpu.PrefetchScalarGridSpec(
            num_scalar_prefetch=1,
            grid=(count,),
            in_specs=[natural] * 4
            + [moved(array.shape[1:]) for array in halved]
            + [flat] * 3
            + [square] * 5
            + [pl.BlockSpec(memory_space=pl.ANY)] * len(earlier),
            out_specs=[natural] * 2 + [moved((width, rows))] * 2 + [flat] * 3,
        ),
        out_shape=[
            jax.ShapeDtypeStruct((samples, rows, width), bf16),
            jax.ShapeDtypeStruct((samples, rows, width), f32),
        ]
        + [jax.ShapeDtypeStruct((samples, width, rows), bf16)] * 2
        + [jax.ShapeDtypeStruct((rows, width), f32)] * 3,
        input_output_aliases={23 + i: i for i in range(len(earlier))},
        compiler_params=pltpu.CompilerParams(vmem_limit_bytes=VMEM_LIMIT),
        cost_estimate=pl.CostEstimate(flops=1, bytes_accessed=1, transcendentals=0),
    )(meta, *naturals, *halved, *flats, *weights, *earlier)


def swap_cores(array):
    return lax.ppermute(array, "qry", [(0, 1), (1, 0)])


def traded(array, axis):
    return lax.all_to_all(array, axis, 0, 0)


def spread(array, axis):
    return traded(jnp.broadcast_to(array[None], (lax.axis_size(axis),) + array.shape), axis)


def exchange(array, axis, bit):
    return lax.ppermute(array, axis, [(i, i ^ bit) for i in range(lax.axis_size(axis))])


def pick(array, index):
    return lax.dynamic_index_in_dim(array, index, 0, keepdims=False)


def traded_apart(array, axis):
    place = lax.axis_index(axis)
    return [pick(array, place)] + [
        exchange(pick(array, place ^ shift), axis, shift)
        for shift in range(1, lax.axis_size(axis))
    ]


def spread_apart(array, axis):
    return [array] + [exchange(array, axis, shift) for shift in range(1, lax.axis_size(axis))]


def in_order(pieces, axis):
    place, ordered = lax.axis_index(axis), []
    for j in range(len(pieces)):
        chosen = pieces[j]
        for shift in range(1, len(pieces)):
            chosen = jnp.where(place == shift, pieces[j ^ shift], chosen)
        ordered.append(chosen)
    return jnp.stack(ordered)


def summed(pieces):
    total = pieces[0].astype(f32)
    for i in range(1, len(pieces)):
        total = total + pieces[i].astype(f32)
    return total


def filled(packs, start, arrays):
    packs = list(packs)
    for array in arrays:
        for side, half in enumerate(halves(array)):
            packs[side] = lax.dynamic_update_slice(packs[side], half.astype(bf16), (start, 0))
        start += array.shape[0]
    return packs


def padded_rows(count):
    return count + -count % 512


def tied(*values):
    return lax.optimization_barrier(values)


class SliceTotal:
    def __init__(self, mine, other, apart):
        self.mine, self.state, self.apart = mine, swap_cores(other), apart

    def first(self):
        total = (self.mine.astype(f32) + self.state.astype(f32)).astype(bf16)
        places = lax.axis_size("cplx")
        self.sent = total.reshape(places, -1, total.shape[1])

    def second(self, *others):
        levels = lax.axis_size("smp")
        self.depths = [group.sent.shape[1] for group in (self, *others)]
        totals = [
            summed(group.state).astype(bf16).reshape(levels, -1, group.sent.shape[2])
            for group in (self, *others)
        ]
        self.sent = totals[0] if len(totals) == 1 else jnp.concatenate(totals, axis=1)

    def third(self):
        self.sent = summed(self.state).astype(bf16)

    def fourth(self):
        pieces = self.state
        pieces = in_order(pieces, "smp") if "smp" in self.apart else pieces
        self.sent = pieces.reshape(-1, pieces.shape[2])

    def wait(self, value):
        self.state, value = tied(self.state, value)
        return value

    def lead(self, value):
        self.sent, value = tied(self.sent, value)
        return value

    def trade(self, axis):
        self.state = (traded_apart if axis in self.apart else traded)(self.sent, axis)

    def share(self, axis):
        self.state = (spread_apart if axis in self.apart else spread)(self.sent, axis)

    def result(self):
        pieces = in_order(self.state, "cplx") if "cplx" in self.apart else self.state
        levels = lax.axis_size("smp")
        pieces = pieces.reshape(pieces.shape[0] * levels, -1, pieces.shape[2])
        totals, start = [], 0
        for depth in self.depths:
            share = depth // levels
            piece = pieces[:, start : start + share]
            totals.append(piece.reshape(-1, pieces.shape[2]).astype(f32))
            start += share
        return totals


def total_line(vector):
    vector = vector[0] + swap_cores(vector[1])
    return summed(spread_apart(vector, "smp"))


def sum_samples(array):
    return summed(spread_apart(array.astype(bf16), "smp"))


def halves(array):
    portion = array.shape[-1] // 2
    core = lax.axis_index("qry")
    mine = lax.dynamic_slice_in_dim(array, core * portion, portion, array.ndim - 1)
    other = lax.dynamic_slice_in_dim(array, (1 - core) * portion, portion, array.ndim - 1)
    return mine, other


def gather_rows(piece):
    if piece.shape[1] % 16 == 0:
        return lax.all_gather(piece, "smp", axis=0)
    return lax.all_gather(piece, "smp", axis=1, tiled=True)[None]


def scatter_rows(whole):
    if whole.shape[0] == lax.axis_size("smp"):
        return lax.psum_scatter(whole, "smp", scatter_dimension=0)
    return lax.psum_scatter(whole[0], "smp", scatter_dimension=1, tiled=True)


def per_device(
    single,
    condition,
    pair_features,
    lengths,
    cotangent,
    first_gain,
    first_scale,
    first_offset,
    first_shift,
    query_projection_weight,
    query_bias_vector,
    key_projection_weight,
    value_projection_weight,
    attention_gate_weight,
    attention_output_weight,
    pair_gain,
    pair_project,
    finish_weight,
    finish_offset,
    second_gain,
    second_scale,
    second_offset,
    second_shift,
    transition_swish_weight,
    transition_linear_weight,
    transition_down_weight,
    closing_weight,
    closing_offset,
):
    width = single.shape[3]
    narrow = condition.shape[2]
    half = width // 2
    inner = transition_swish_weight.shape[1]
    heads = pair_project.shape[1]
    meta = jnp.stack([lengths[0], lax.axis_index("qry")]).astype(jnp.int32)
    condition_raw = condition[0]
    condition_norm, condition_factor = normalize(condition_raw.astype(f32))
    pair_weight = centred_project(pair_gain, pair_project)
    bias_pieces = pair_forward(pair_features[0], pair_weight)
    meta, *bias_pieces = tied(meta, *bias_pieces)
    bias_rows = [gather_rows(bias_pieces[0])]
    bias_rows[0], bias_pieces[1] = tied(bias_rows[0], bias_pieces[1])
    bias_rows.append(gather_rows(bias_pieces[1]))

    def modulation(gain, scale_weight, offset, shift_weight):
        low = (condition_norm * gain.astype(f32)).astype(bf16)
        lifting = jax.nn.sigmoid(matmul(low, scale_weight) + offset.astype(f32))
        return low, lifting, matmul(low, shift_weight)

    condition_first, lifting_first, shifting_first = modulation(
        first_gain, first_scale, first_offset, first_shift
    )
    condition_second, lifting_second, shifting_second = modulation(
        second_gain, second_scale, second_offset, second_shift
    )
    finish = jax.nn.sigmoid(matmul(condition_raw, finish_weight) + finish_offset.astype(f32))
    closing = jax.nn.sigmoid(matmul(condition_raw, closing_weight) + closing_offset.astype(f32))
    square_weights = (
        query_projection_weight,
        key_projection_weight,
        value_projection_weight,
        attention_gate_weight,
        attention_output_weight,
    )
    closed, delta_second, closing_sum, lift_second, shift_second, *second_packs = transition(
        meta,
        single[0],
        cotangent[0],
        lifting_second,
        shifting_second,
        closing,
        (transition_swish_weight, transition_linear_weight, transition_down_weight),
        padded_rows(3 * inner + 3 * narrow),
    )

    def modulation_back(lift_sum, shift_sum, low, lifting, scale_weight, shift_weight):
        delta_lift = lift_sum * lifting * (1.0 - lifting)
        scale_total = contract("qc,qd->cd", low, delta_lift)
        shift_total = contract("qc,qd->cd", low, shift_sum)
        delta_condition = contract("qd,cd->qc", delta_lift, scale_weight) + contract(
            "qd,cd->qc", shift_sum, shift_weight
        )
        return scale_total, jnp.sum(delta_lift, axis=0), shift_total, delta_condition

    def gate_back(branch_sum, opened, weight):
        delta = branch_sum * opened * (1.0 - opened)
        return (
            contract("qc,qd->cd", condition_raw, delta),
            jnp.sum(delta, axis=0),
            contract("qd,cd->qc", delta, weight),
        )

    scale_second, offset_second, shift_total_second, cond_delta_second = modulation_back(
        lift_second, shift_second, condition_second, lifting_second, second_scale, second_shift
    )
    closing_total, closing_offset_total, condition_closing = gate_back(
        closing_sum, closing, closing_weight
    )
    early = SliceTotal(
        *filled(second_packs, 3 * inner, (scale_second, shift_total_second, closing_total)),
        apart=EARLY_APART,
    )

    early.mine, meta = tied(early.mine, meta)
    query, key_value, gate, delta_gated, mixed_first = project(
        meta,
        single[0],
        cotangent[0],
        lifting_first,
        shifting_first,
        finish,
        query_bias_vector.astype(f32)[None],
        square_weights,
    )
    pair_of_cores = (key_value, swap_cores(key_value))
    def attend(meta, part, call, earlier):
        return list(
            attention(
                meta, query, pair_of_cores, gate, delta_gated, bias_rows[part], part, call, CALLS,
                earlier,
            )
        )

    attended = []
    query = early.wait(query)
    early.first()
    meta = early.lead(meta)
    early.trade("cplx")
    attended = [attend(meta, 0, 1, attend(meta, 0, 0, ()))]
    done = attend(meta, 1, 0, ())
    done[0] = early.wait(done[0])
    early.second()
    meta = early.lead(meta)
    early.trade("smp")
    attended.append(attend(meta, 1, 1, done))
    delta_bias = [scatter_rows(part[5]) for part in attended]

    def both(index):
        return [part[index] for part in attended]

    arrived = [swap_cores(part) for part in both(4)]
    halved = both(0) + both(1) + both(2)
    def back(meta, start, earlier):
        outs = rows_back(
            meta,
            (single[0], cotangent[0], closed, delta_second),
            halved + both(3) + arrived,
            (lifting_first, lifting_second, finish),
            square_weights,
            start,
            single.shape[1] // 2,
            earlier,
        )
        return list(outs)

    done = back(meta, 0, ())
    last = back(meta, single.shape[1] // 2, tuple(done[:4]))
    block_out, single_grad, delta_key, delta_value = last[:4]
    finish_sum, lift_first, shift_first = [done[i] + last[i] for i in (4, 5, 6)]
    scale_first, offset_first, shift_total_first, cond_delta_first = modulation_back(
        lift_first, shift_first, condition_first, lifting_first, first_scale, first_shift
    )
    finish_total, finish_offset_total, condition_finish = gate_back(
        finish_sum, finish, finish_weight
    )
    *first_packs, query_bias_total = weight_sums(
        meta,
        cotangent[0],
        mixed_first,
        finish,
        [delta_key, delta_value] + halved,
        padded_rows(5 * width + 3 * narrow),
    )
    first_packs[1] = early.wait(first_packs[1])
    early.third()
    first_packs[1] = early.lead(first_packs[1])
    early.share("smp")
    late = SliceTotal(
        *filled(first_packs, 5 * width, (scale_first, shift_total_first, finish_total)),
        apart=LATE_APART,
    )
    gain_first = jnp.sum(cond_delta_first * condition_norm, axis=0)
    gain_second = jnp.sum(cond_delta_second * condition_norm, axis=0)
    condition_grad = sum_samples(
        normalize_back(
            cond_delta_first * first_gain.astype(f32) + cond_delta_second * second_gain.astype(f32),
            condition_norm,
            condition_factor,
        )
        + condition_closing
        + condition_finish
    )
    blocks = pair_features.shape[1] // 16 if pair_features.shape[1] % 16 == 0 else 1
    sizes = (blocks - blocks // 2, blocks // 2)
    delta_bias[0] = late.wait(delta_bias[0])
    late.first()
    pair_weight = late.lead(pair_weight)
    late.trade("cplx")
    early.state, late.state, delta_bias[1] = tied(early.state, late.state, delta_bias[1])
    early.fourth()
    pair_weight = early.lead(pair_weight)
    early.share("cplx")
    late.second()
    pair_weight = late.lead(pair_weight)
    late.trade("smp")
    pair_grad, inner_total = pair_backward(
        pair_features[0], pair_weight, delta_bias, 0, sizes[0], ()
    )
    inner_total = late.wait(inner_total)
    late.third()
    pair_weight = late.lead(pair_weight)
    late.share("smp")
    if sizes[1]:
        pair_grad, more = pair_backward(
            pair_features[0], pair_weight, delta_bias, *sizes, (pair_grad,)
        )
        inner_total = inner_total + more
    early.state = late.wait(early.state)
    late.fourth()
    late.share("cplx")
    pair_gain_total = jnp.sum(inner_total * pair_project.astype(f32).T, axis=0)
    pair_project_total = inner_total * pair_gain.astype(f32)[None]
    vectors = (
        gain_first,
        offset_first,
        query_bias_total[:, 0],
        finish_offset_total,
        gain_second,
        offset_second,
        closing_offset_total,
        pair_gain_total,
    )
    small = total_line(
        jnp.concatenate(
            [jnp.stack(halves(vector)) for vector in vectors]
            + [jnp.stack([half.reshape(-1) for half in halves(pair_project_total.T)])],
            axis=1,
        )
    )
    def unpack(total, sizes):
        arrays, start = [], 0
        for depth, columns in sizes:
            blocks = columns // half
            arrays.append(
                jnp.concatenate(
                    [
                        total[start + b * depth : start + (b + 1) * depth]
                        for b in range(blocks)
                    ],
                    axis=1,
                )
            )
            start += depth * blocks
        return arrays

    early_totals = unpack(
        early.result()[0],
        ((width, inner // 2), (width, inner // 2), (inner, half)) + ((narrow, half),) * 3,
    )
    small, *early_totals = tied(small, *early_totals)
    swish_total, linear_total, down_total, scale_second, shift_second, closing_total = early_totals
    small = summed(spread_apart(small, "cplx"))
    late = late.result()[0]
    ends, place = [], 0
    for vector in vectors:
        ends.append(small[place : place + vector.shape[0] // 2])
        place += vector.shape[0] // 2
    query_total, key_total, value_total, gate_total, output_total, *others = unpack(
        late, ((width, half),) * 5 + ((narrow, half),) * 3
    )
    scale_first, shift_first, finish_total = others
    return (
        block_out[None],
        single_grad[None],
        condition_grad[None],
        pair_grad[None],
        ends[0],
        scale_first,
        ends[1],
        shift_first,
        query_total,
        ends[2],
        key_total,
        value_total,
        gate_total,
        output_total,
        ends[7],
        small[place:].reshape(-1, heads // 2),
        finish_total,
        ends[3],
        ends[4],
        scale_second,
        ends[5],
        shift_second,
        swish_total,
        linear_total,
        down_total,
        closing_total,
        ends[6],
    )


def solution(mesh):
    placed = (
        P("cplx", "smp", "qry", None),
        P("cplx", "qry", None),
        P("cplx", ("qry", "smp"), None, None),
        P("cplx"),
        P("cplx", "smp", "qry", None),
        P(),
        P(),
        P(),
        P(),
        P(),
        P(),
        P(),
        P(),
        P(),
        P(),
        P(),
        P(),
        P(),
        P(),
        P(),
        P(),
        P(),
        P(),
        P(),
        P(),
        P(),
        P(),
        P(),
    )
    return jax.shard_map(
        per_device,
        mesh=mesh,
        in_specs=placed,
        out_specs=(
            P("cplx", "smp", "qry", None),
            P("cplx", "smp", "qry", None),
            P("cplx", "qry", None),
            P("cplx", ("qry", "smp"), None, None),
            P("qry"),
            P(None, "qry"),
            P("qry"),
            P(None, "qry"),
            P(None, "qry"),
            P("qry"),
            P(None, "qry"),
            P(None, "qry"),
            P(None, "qry"),
            P(None, "qry"),
            P("qry"),
            P(None, "qry"),
            P(None, "qry"),
            P("qry"),
            P("qry"),
            P(None, "qry"),
            P("qry"),
            P(None, "qry"),
            P(None, "qry"),
            P(None, "qry"),
            P(None, "qry"),
            P(None, "qry"),
            P("qry"),
        ),
        check_vma=False,
    )
```

```python
import functools

import jax
import jax.numpy as jnp
from jax import lax
from jax.experimental import pallas as pl
from jax.experimental.pallas import tpu as pltpu
from jax.sharding import PartitionSpec as P

EPSILON = 1e-05
LANES = 128
VMEM_LIMIT = 56 * 2**20
SHARES = (10, 6)
CALLS = 2
EARLY_APART = ("smp",)
LATE_APART = ("smp",)
f32 = jnp.float32
bf16 = jnp.bfloat16


def normalize(values):
    centre = values - jnp.mean(values, axis=-1, keepdims=True)
    factor = lax.rsqrt(jnp.mean(centre * centre, axis=-1, keepdims=True) + EPSILON)
    return (centre * factor, factor)


def normalize_back(incoming, normed, factor):
    return factor * (
        incoming
        - jnp.mean(incoming, axis=-1, keepdims=True)
        - normed * jnp.mean(incoming * normed, axis=-1, keepdims=True)
    )


def matmul(left, right):
    return jnp.dot(left, right, preferred_element_type=jnp.float32)


def contract(form, left, right):
    return jnp.einsum(
        form, left.astype(bf16), right.astype(bf16), preferred_element_type=jnp.float32
    )


def dot(left, right, left_dim, right_dim):
    return lax.dot_general(
        left, right, (((left_dim,), (right_dim,)), ((), ())), preferred_element_type=f32
    )


def attention_kernel(
    meta, query, mine, other, gate, delta_gated, bias, *refs, step
):
    (
        gated, delta_gate, delta_query, kept, sent, delta_bias, score, prob, slope,
    ) = refs[-9:]
    samples, head_width, rows = query.shape
    total = 2 * rows
    pieces, piece_rows = bias.shape[0], bias.shape[2]
    scale = head_width ** (-0.5)
    second = meta[1] == 1
    column = lax.broadcasted_iota(jnp.int32, (16, total), 1)
    line = lax.broadcasted_iota(jnp.int32, (16, total), 0)
    masking = jnp.where((line == 0) & (column >= meta[0]), -1e30, 0.0).astype(bf16)
    pair_ones = jnp.where(line < 2, 1.0, 0.0).astype(bf16)
    query_line = lax.broadcasted_iota(jnp.int32, (16, rows), 0)
    one_line = jnp.where(query_line == 0, 1.0, 0.0).astype(bf16)
    spots = [
        (piece, start, piece * piece_rows + start)
        for piece in range(pieces)
        for start in range(0, piece_rows, step)
    ]

    def joined(mine, other):
        mine, other = mine[:, :rows], other[:, :rows]
        first = jnp.where(second, other, mine)
        last = jnp.where(second, mine, other)
        return jnp.concatenate([first, last], axis=1)

    def parted(whole, sample, which):
        first, last = whole[:, :rows], whole[:, rows:]
        kept[sample, which] = jnp.where(second, last, first)
        sent[sample, which, :, :rows] = jnp.where(second, first, last).astype(sent.dtype)

    keys, values = [], []
    for s in range(samples):
        keys.append(joined(mine[s, 0], other[s, 0]))
        values.append(joined(mine[s, 1], other[s, 1]))
        score[s] = dot(
            jnp.concatenate([query[s], one_line], axis=0),
            jnp.concatenate([keys[s], masking], axis=0),
            0,
            0,
        )
    for piece, start, place in spots:
        bias_here = bias[piece, 0, start : start + step, :].astype(f32)
        here = slice(place, place + step)
        for s in range(samples):
            line_scores = score[s, here, :] * scale + bias_here
            highest = jnp.max(line_scores, axis=1, keepdims=True)
            exponent = jnp.exp(line_scores - highest)
            soft = exponent * (1.0 / jnp.sum(exponent, axis=1, keepdims=True))
            score[s, here, :] = soft
            prob[s, here, :] = soft.astype(bf16)
    for s in range(samples):
        attended = dot(values[s], prob[s], 1, 1)
        gate_here, delta_here = gate[s], delta_gated[s]
        gated[s] = (gate_here * attended).astype(bf16)
        delta_attended = (delta_here * gate_here).astype(bf16)
        delta_gate[s] = (delta_here * attended * gate_here * (1.0 - gate_here)).astype(bf16)
        centre = jnp.sum(delta_attended.astype(f32) * attended, axis=0, keepdims=True)
        coarse = centre.astype(bf16).astype(f32)
        rest = jnp.where(
            query_line == 0, -coarse, jnp.where(query_line == 1, coarse - centre, 0.0)
        ).astype(bf16)
        slope[s] = dot(
            jnp.concatenate([delta_attended, rest], axis=0),
            jnp.concatenate([values[s], pair_ones], axis=0),
            0,
            0,
        )
        parted(dot(delta_attended, prob[s], 1, 0), s, 1)
    for piece, start, place in spots:
        here = slice(place, place + step)
        total_here = None
        for s in range(samples):
            delta_scores = score[s, here, :] * slope[s, here, :]
            prob[s, here, :] = delta_scores.astype(bf16)
            total_here = delta_scores if total_here is None else total_here + delta_scores
        delta_bias[piece, 0, start : start + step, :] = total_here.astype(bf16)
    for s in range(samples):
        delta_query[s] = (dot(keys[s], prob[s], 1, 1) * scale).astype(bf16)
        parted(dot(query[s], prob[s], 1, 0) * scale, s, 0)


def attention(
    meta, query, pair_of_cores, gate, delta_gated, bias, part, call, calls, earlier
):
    samples, width, rows = query.shape
    pieces, heads, piece_rows, total = bias.shape
    head_width = width // sum(SHARES)
    step = 16 if piece_rows % 16 == 0 else piece_rows
    count = heads // calls
    inside = call * count
    first = sum(SHARES[:part]) + inside
    padded = pair_of_cores[0].shape[3]

    def spec(columns, offset):
        return pl.BlockSpec((samples, head_width, columns), lambda h, meta: (0, offset + h, 0))

    inner, outer = spec(rows, first), spec(rows, inside)

    def double(columns, offset):
        return pl.BlockSpec(
            (samples, 2, head_width, columns), lambda h, meta: (0, 0, offset + h, 0)
        )

    tile = pl.BlockSpec((pieces, 1, piece_rows, total), lambda h, meta: (0, inside + h, 0, 0))

    def made(dtype, columns=rows, lead=(samples,)):
        return jax.ShapeDtypeStruct(lead + (heads * head_width, columns), dtype)

    return pl.pallas_call(
        functools.partial(attention_kernel, step=step),
        grid_spec=pltpu.PrefetchScalarGridSpec(
            num_scalar_prefetch=1,
            grid=(count,),
            in_specs=[inner]
            + [double(padded, first)] * 2
            + [inner] * 2
            + [tile]
            + [pl.BlockSpec(memory_space=pl.ANY)] * len(earlier),
            out_specs=[outer] * 3 + [double(rows, inside), double(padded, inside), tile],
            scratch_shapes=[
                pltpu.VMEM((samples, rows, total), f32),
                pltpu.VMEM((samples, rows, total), bf16),
                pltpu.VMEM((samples, rows, total), f32),
            ],
        ),
        out_shape=[
            made(bf16), made(bf16), made(bf16), made(f32, rows, (samples, 2)),
            made(bf16, padded, (samples, 2)),
            jax.ShapeDtypeStruct(bias.shape, bf16),
        ],
        input_output_aliases={7 + i: i for i in range(len(earlier))},
        compiler_params=pltpu.CompilerParams(vmem_limit_bytes=VMEM_LIMIT),
        cost_estimate=pl.CostEstimate(flops=1, bytes_accessed=1, transcendentals=0),
    )(meta, query, *pair_of_cores, gate, delta_gated, bias, *earlier)


def centred_project(gain, project):
    weight = (project.astype(f32) * gain.astype(f32)[:, None]).T
    weight = weight - jnp.mean(weight, axis=1, keepdims=True)
    high = lax.reduce_precision(weight, 8, 7)
    return jnp.concatenate([high.astype(bf16), (weight - high).astype(bf16)], axis=0)


def turned_norm(rows):
    turned = rows.T.astype(f32)
    centre = turned - jnp.mean(turned, axis=0, keepdims=True)
    return centre, lax.rsqrt(jnp.mean(centre * centre, axis=0, keepdims=True) + EPSILON)


def head_spots():
    return [(part, i) for part, share in enumerate(SHARES) for i in range(share)]


def pair_forward_kernel(pair, weight, *refs, block, heads):
    outs, wide = refs[:-1], refs[-1]

    def one(i, carry):
        centre, factor = turned_norm(pair[i])
        both = dot(weight[...], centre.astype(bf16), 1, 0)
        line = (both[:heads] + both[heads:]) * factor
        for t in range(wide.shape[0]):
            wide[t, pl.ds(pl.multiple_of(i * heads, heads), heads), :] = line[
                :, t * LANES : (t + 1) * LANES
            ]
        return carry

    lax.fori_loop(0, block, one, 0, unroll=8 if block % 8 == 0 else 1)
    for h, (part, i) in enumerate(head_spots()):
        for t in range(wide.shape[0]):
            outs[part][i, :, t * LANES : (t + 1) * LANES] = wide[
                t, pl.ds(h, block, stride=heads), :
            ].astype(bf16)


def pair_forward(pair, weight):
    rows, length, width = pair.shape
    heads = weight.shape[0] // 2
    block = 16 if rows % 16 == 0 else rows
    return pl.pallas_call(
        functools.partial(pair_forward_kernel, block=block, heads=heads),
        grid=(rows // block,),
        in_specs=[
            pl.BlockSpec((block, length, width), lambda i: (i, 0, 0)),
            pl.BlockSpec((2 * heads, width), lambda i: (0, 0)),
        ],
        out_specs=[pl.BlockSpec((share, block, length), lambda i: (0, i, 0)) for share in SHARES],
        out_shape=[jax.ShapeDtypeStruct((share, rows, length), bf16) for share in SHARES],
        scratch_shapes=[pltpu.VMEM((length // LANES, block * heads, LANES), f32)],
        compiler_params=pltpu.CompilerParams(vmem_limit_bytes=VMEM_LIMIT),
        cost_estimate=pl.CostEstimate(flops=1, bytes_accessed=1, transcendentals=0),
    )(pair, weight)


def pair_backward_kernel(pair, weight, *refs, block, heads):
    deltas = refs[: len(SHARES)]
    out, inner_out, wide, inner_sum = refs[-4:]
    step = pl.program_id(0)

    @pl.when(step == 0)
    def _():
        inner_sum[...] = jnp.zeros_like(inner_sum)

    for h, (part, place) in enumerate(head_spots()):
        for t in range(wide.shape[0]):
            wide[t, h * block : (h + 1) * block, :] = deltas[part][
                place, :, t * LANES : (t + 1) * LANES
            ].astype(f32)

    def one(i, carry):
        centre, factor = turned_norm(pair[i])
        normed = centre * factor
        delta = jnp.concatenate(
            [wide[t, pl.ds(i, heads, stride=block), :] for t in range(wide.shape[0])], axis=1
        ).astype(bf16)
        incoming = dot(weight[...], jnp.concatenate([delta, delta], axis=0), 0, 0)
        inner_sum[...] += dot(delta, normed.astype(bf16), 1, 1)
        along = jnp.mean(incoming * normed, axis=0, keepdims=True)
        out[i] = ((incoming - normed * along) * factor).T
        return carry

    lax.fori_loop(0, block, one, 0, unroll=4 if block % 4 == 0 else 1)

    @pl.when(step == pl.num_programs(0) - 1)
    def _():
        inner_out[...] = inner_sum[...]


def pair_backward(pair, weight, deltas, start, count, earlier):
    rows, length, width = pair.shape
    heads = weight.shape[0] // 2
    parts = len(deltas)
    block = 16 if rows % 16 == 0 else rows
    return pl.pallas_call(
        functools.partial(pair_backward_kernel, block=block, heads=heads),
        grid=(count,),
        in_specs=[
            pl.BlockSpec((block, length, width), lambda i: (start + i, 0, 0)),
            pl.BlockSpec((2 * heads, width), lambda i: (0, 0)),
        ]
        + [
            pl.BlockSpec((share, block, length), lambda i: (0, start + i, 0)) for share in SHARES
        ]
        + [pl.BlockSpec(memory_space=pl.ANY)] * len(earlier),
        out_specs=[
            pl.BlockSpec((block, length, width), lambda i: (start + i, 0, 0)),
            pl.BlockSpec((heads, width), lambda i: (0, 0)),
        ],
        out_shape=[
            jax.ShapeDtypeStruct((rows, length, width), f32),
            jax.ShapeDtypeStruct((heads, width), f32),
        ],
        scratch_shapes=[
            pltpu.VMEM((length // LANES, block * heads, LANES), f32),
            pltpu.VMEM((heads, width), f32),
        ],
        input_output_aliases={2 + parts: 0} if earlier else {},
        compiler_params=pltpu.CompilerParams(vmem_limit_bytes=VMEM_LIMIT),
        cost_estimate=pl.CostEstimate(flops=1, bytes_accessed=1, transcendentals=0),
    )(pair, weight, *deltas, *earlier)


def fixed(shape):
    return pl.BlockSpec(shape, lambda s, *_: (0,) * len(shape), pipeline_mode=pl.Buffered(1))


def by_sample(shape, buffers=2):
    return pl.BlockSpec(
        (1,) + shape,
        lambda s, *_: (s,) + (0,) * len(shape),
        pipeline_mode=pl.Buffered(buffers),
    )


def row_valid(meta, rows):
    place = lax.broadcasted_iota(jnp.int32, (rows, 1), 0) + meta[1] * rows
    return jnp.where(place < meta[0], 1.0, 0.0)


def pack_columns(meta, packs, arrays, start=0):
    tile = packs[0].shape[1]
    for array in arrays:
        depth, share = array.shape[0], array.shape[1] // 2
        for side in range(2):
            core = meta[1] if side == 0 else 1 - meta[1]
            for block in range(share // tile):
                column = pl.multiple_of(core * share + block * tile, LANES)
                packs[side][start + block * depth : start + (block + 1) * depth, :] = array[
                    :, pl.ds(column, tile)
                ].astype(bf16)
        start += depth * (share // tile)


def project_kernel(
    meta, single, cotangent, lifting, shifting, finish, query_bias,
    query_weight, key_weight, value_weight, gate_weight, output_weight,
    query, key_value, gate, delta_gated, mixed_out,
):
    rows = single.shape[1]
    normed, _ = normalize(single[0].astype(f32))
    mixed = (lifting[...] * normed + shifting[...]).astype(bf16)
    mixed_out[0] = mixed
    query[0] = (dot(mixed, query_weight[...], 1, 0) + query_bias[...]).astype(bf16).T
    key_value[0, 0, :, :rows] = dot(mixed, key_weight[...], 1, 0).astype(bf16).T
    key_value[0, 1, :, :rows] = dot(mixed, value_weight[...], 1, 0).astype(bf16).T
    gate[0] = jax.nn.sigmoid(dot(mixed, gate_weight[...], 1, 0)).T
    branch = row_valid(meta, rows) * cotangent[0].astype(f32)
    lifted = (finish[...] * branch).astype(bf16)
    delta_gated[0] = dot(lifted, output_weight[...], 1, 1).T


def project(meta, single, cotangent, lifting, shifting, finish, query_bias, weights):
    samples, rows, width = single.shape
    natural, turned = by_sample((rows, width)), by_sample((width, rows))
    flat, square = fixed((rows, width)), fixed((width, width))
    padded = rows + -rows % LANES
    wide = by_sample((2, width, padded))
    return pl.pallas_call(
        project_kernel,
        grid_spec=pltpu.PrefetchScalarGridSpec(
            num_scalar_prefetch=1,
            grid=(samples,),
            in_specs=[natural, natural, flat, flat, flat, fixed((1, width))] + [square] * 5,
            out_specs=[turned, wide, turned, turned, natural],
        ),
        out_shape=[
            jax.ShapeDtypeStruct(shape, dtype)
            for shape, dtype in (
                ((samples, width, rows), bf16),
                ((samples, 2, width, padded), bf16),
                ((samples, width, rows), f32),
                ((samples, width, rows), f32),
            )
        ]
        + [jax.ShapeDtypeStruct((samples, rows, width), bf16)],
        compiler_params=pltpu.CompilerParams(vmem_limit_bytes=VMEM_LIMIT),
        cost_estimate=pl.CostEstimate(flops=1, bytes_accessed=1, transcendentals=0),
    )(meta, single, cotangent, lifting, shifting, finish, query_bias, *weights)


def transition_kernel(
    meta, single, cotangent, lifting, shifting, closing,
    swish_weight, linear_weight, down_weight,
    closed, delta_second, closing_sum, lift_sum, shift_sum, pack_mine, pack_other,
    swish_sum, linear_sum, down_sum,
):
    rows = single.shape[1]
    sample = pl.program_id(0)
    normed, _ = normalize(single[0].astype(f32))
    mixed = (lifting[...] * normed + shifting[...]).astype(bf16)
    up_swish = dot(mixed, swish_weight[...], 1, 0)
    up_linear = dot(mixed, linear_weight[...], 1, 0)
    squash = jax.nn.sigmoid(up_swish)
    silu = up_swish * squash
    hidden = (silu * up_linear).astype(bf16)
    moved = dot(hidden, down_weight[...], 1, 0)
    closing_here = closing[...]
    branch = row_valid(meta, rows) * cotangent[0].astype(f32)
    closed[0] = closing_here * moved
    delta_moved = (closing_here * branch).astype(bf16)
    delta_hidden = dot(delta_moved, down_weight[...], 1, 1)
    delta_swish = (delta_hidden * up_linear * squash * (1.0 + up_swish * (1.0 - squash))).astype(bf16)
    delta_linear = (delta_hidden * silu).astype(bf16)
    second = dot(delta_swish, swish_weight[...], 1, 1) + dot(
        delta_linear, linear_weight[...], 1, 1
    )
    delta_second[0] = second

    def collect(first):
        def put(ref, value):
            if first:
                ref[...] = value
            else:
                ref[...] += value

        put(closing_sum, branch * moved)
        put(lift_sum, second * normed)
        put(shift_sum, second)
        put(swish_sum, dot(mixed, delta_swish, 0, 0))
        put(linear_sum, dot(mixed, delta_linear, 0, 0))
        put(down_sum, dot(hidden, delta_moved, 0, 0))

    @pl.when(sample == 0)
    def _():
        collect(True)

    @pl.when(sample > 0)
    def _():
        collect(False)

    @pl.when(sample == pl.num_programs(0) - 1)
    def _():
        pack_columns(meta, (pack_mine, pack_other), (swish_sum, linear_sum, down_sum))


def transition(meta, single, cotangent, lifting, shifting, closing, weights, pack_rows):
    samples, rows, width = single.shape
    inner = weights[0].shape[1]
    natural, flat = by_sample((rows, width)), fixed((rows, width))
    up, down = (width, inner), (inner, width)
    pack = (pack_rows, width // 2)
    return pl.pallas_call(
        transition_kernel,
        grid_spec=pltpu.PrefetchScalarGridSpec(
            num_scalar_prefetch=1,
            grid=(samples,),
            in_specs=[natural, natural, flat, flat, flat, fixed(up), fixed(up), fixed(down)],
            out_specs=[natural, natural, flat, flat, flat, fixed(pack), fixed(pack)],
            scratch_shapes=[pltpu.VMEM(up, f32), pltpu.VMEM(up, f32), pltpu.VMEM(down, f32)],
        ),
        out_shape=[
            jax.ShapeDtypeStruct(shape, f32)
            for shape in ((samples, rows, width),) * 2 + ((rows, width),) * 3
        ]
        + [jax.ShapeDtypeStruct(pack, bf16)] * 2,
        compiler_params=pltpu.CompilerParams(vmem_limit_bytes=VMEM_LIMIT),
        cost_estimate=pl.CostEstimate(flops=1, bytes_accessed=1, transcendentals=0),
    )(meta, single, cotangent, lifting, shifting, closing, *weights)


def whole(*parts):
    return jnp.concatenate([part[0] for part in parts], axis=0)


def whole_at(*parts):
    return [jnp.concatenate([part[0, i] for part in parts], axis=0) for i in range(2)]


def put(first, ref, value):
    if first:
        ref[...] = value
    else:
        ref[...] += value


def weights_kernel(
    meta, cotangent, mixed, finish,
    key, value, gated_a, gated_b, gate_a, gate_b, query_a, query_b,
    pack_mine, pack_other, bias_sum,
    query_sum, key_sum, value_sum, gate_sum, output_sum,
):
    count, rows, width = cotangent.shape
    sample = pl.program_id(0)

    def turned(*parts):
        return jnp.concatenate(
            [jnp.concatenate([part[i] for part in parts], axis=0) for i in range(count)], axis=1
        )

    delta_query = turned(query_a, query_b)
    mixed_rows = mixed[...].reshape(count * rows, width)
    masked = finish[...] * row_valid(meta, rows)
    lifted = jnp.concatenate(
        [(masked * cotangent[i].astype(f32)).astype(bf16) for i in range(count)], axis=0
    )

    def collect(first):
        put(first, query_sum, dot(delta_query, mixed_rows, 1, 0))
        put(first, key_sum, dot(turned(key), mixed_rows, 1, 0))
        put(first, value_sum, dot(turned(value), mixed_rows, 1, 0))
        put(first, gate_sum, dot(turned(gate_a, gate_b), mixed_rows, 1, 0))
        put(first, output_sum, dot(turned(gated_a, gated_b), lifted, 1, 0))
        put(first, bias_sum, jnp.sum(delta_query.astype(f32), axis=1, keepdims=True))

    @pl.when(sample == 0)
    def _():
        collect(True)

    @pl.when(sample > 0)
    def _():
        collect(False)

    @pl.when(sample == pl.num_programs(0) - 1)
    def _():
        width = query_sum.shape[0]
        half = width // 2
        packs = (pack_mine, pack_other)
        for i, array in enumerate((query_sum, key_sum, value_sum, gate_sum)):
            for side in range(2):
                core = meta[1] if side == 0 else 1 - meta[1]
                row = pl.multiple_of(core * half, LANES)
                packs[side][i * width : (i + 1) * width, :] = array[
                    pl.ds(row, half), :
                ].T.astype(bf16)
        pack_columns(meta, packs, (output_sum,), 4 * width)


def weight_sums(meta, cotangent, mixed, finish, turned, pack_rows):
    samples, rows, width = cotangent.shape
    pack = (pack_rows, width // 2)
    count = 2 if samples % 2 == 0 else 1

    def several(shape):
        return pl.BlockSpec((count,) + shape, lambda s, *_: (s,) + (0,) * len(shape))

    natural = several((rows, width))
    return pl.pallas_call(
        weights_kernel,
        grid_spec=pltpu.PrefetchScalarGridSpec(
            num_scalar_prefetch=1,
            grid=(samples // count,),
            in_specs=[natural, natural, fixed((rows, width))]
            + [several(array.shape[1:]) for array in turned],
            out_specs=[fixed(pack)] * 2 + [fixed((width, 1))],
            scratch_shapes=[pltpu.VMEM((width, width), f32)] * 5,
        ),
        out_shape=[jax.ShapeDtypeStruct(pack, bf16)] * 2
        + [jax.ShapeDtypeStruct((width, 1), f32)],
        compiler_params=pltpu.CompilerParams(vmem_limit_bytes=VMEM_LIMIT),
        cost_estimate=pl.CostEstimate(flops=1, bytes_accessed=1, transcendentals=0),
    )(meta, cotangent, mixed, finish, *turned)


def rows_kernel(
    meta, single, cotangent, closed, delta_second,
    gated_a, gated_b, gate_a, gate_b, query_a, query_b, kept_a, kept_b, came_a, came_b,
    lifting_first, lifting_second, finish,
    query_weight, key_weight, value_weight, gate_weight, output_weight,
    *refs,
):
    block_out, single_grad, key_out, value_out, finish_sum, lift_first, shift_first = refs[-7:]
    rows = single.shape[1]
    kept, came = whole_at(kept_a, kept_b), whole_at(came_a, came_b)
    delta_key, delta_value = [
        (kept[i] + came[i][:, :rows].astype(f32)).astype(bf16) for i in range(2)
    ]
    key_out[0] = delta_key
    value_out[0] = delta_value
    sample = pl.program_id(0)
    residual = single[0].astype(f32)
    normed, factor = normalize(residual)
    valid = row_valid(meta, rows)
    outgoing = cotangent[0].astype(f32)
    branch = valid * outgoing
    raised = dot(whole(gated_a, gated_b), output_weight[...], 0, 0)
    block_out[0] = (residual + valid * (finish[...] * raised + closed[0])).astype(bf16)
    delta_first = (
        dot(whole(query_a, query_b), query_weight[...], 0, 1)
        + dot(delta_key, key_weight[...], 0, 1)
        + dot(delta_value, value_weight[...], 0, 1)
        + dot(whole(gate_a, gate_b), gate_weight[...], 0, 1)
    )
    incoming = delta_first * lifting_first[...] + delta_second[0] * lifting_second[...]
    single_grad[0] = outgoing + normalize_back(incoming, normed, factor)

    def collect(first):
        put(first, finish_sum, branch * raised)
        put(first, lift_first, delta_first * normed)
        put(first, shift_first, delta_first)

    @pl.when(sample == 0)
    def _():
        collect(True)

    @pl.when(sample > 0)
    def _():
        collect(False)


def rows_back(meta, naturals, halved, flats, weights, start, count, earlier):
    samples, rows, width = naturals[0].shape
    flat, square = fixed((rows, width)), fixed((width, width))

    def moved(shape):
        return pl.BlockSpec((1,) + shape, lambda s, *_: (start + s,) + (0,) * len(shape))

    natural = moved((rows, width))
    return pl.pallas_call(
        rows_kernel,
        grid_spec=pltpu.PrefetchScalarGridSpec(
            num_scalar_prefetch=1,
            grid=(count,),
            in_specs=[natural] * 4
            + [moved(array.shape[1:]) for array in halved]
            + [flat] * 3
            + [square] * 5
            + [pl.BlockSpec(memory_space=pl.ANY)] * len(earlier),
            out_specs=[natural] * 2 + [moved((width, rows))] * 2 + [flat] * 3,
        ),
        out_shape=[
            jax.ShapeDtypeStruct((samples, rows, width), bf16),
            jax.ShapeDtypeStruct((samples, rows, width), f32),
        ]
        + [jax.ShapeDtypeStruct((samples, width, rows), bf16)] * 2
        + [jax.ShapeDtypeStruct((rows, width), f32)] * 3,
        input_output_aliases={23 + i: i for i in range(len(earlier))},
        compiler_params=pltpu.CompilerParams(vmem_limit_bytes=VMEM_LIMIT),
        cost_estimate=pl.CostEstimate(flops=1, bytes_accessed=1, transcendentals=0),
    )(meta, *naturals, *halved, *flats, *weights, *earlier)


def swap_cores(array):
    return lax.ppermute(array, "qry", [(0, 1), (1, 0)])


def traded(array, axis):
    return lax.all_to_all(array, axis, 0, 0)


def spread(array, axis):
    return traded(jnp.broadcast_to(array[None], (lax.axis_size(axis),) + array.shape), axis)


def exchange(array, axis, bit):
    return lax.ppermute(array, axis, [(i, i ^ bit) for i in range(lax.axis_size(axis))])


def pick(array, index):
    return lax.dynamic_index_in_dim(array, index, 0, keepdims=False)


def traded_apart(array, axis):
    place = lax.axis_index(axis)
    return [pick(array, place)] + [
        exchange(pick(array, place ^ shift), axis, shift)
        for shift in range(1, lax.axis_size(axis))
    ]


def spread_apart(array, axis):
    return [array] + [exchange(array, axis, shift) for shift in range(1, lax.axis_size(axis))]


def in_order(pieces, axis):
    place, ordered = lax.axis_index(axis), []
    for j in range(len(pieces)):
        chosen = pieces[j]
        for shift in range(1, len(pieces)):
            chosen = jnp.where(place == shift, pieces[j ^ shift], chosen)
        ordered.append(chosen)
    return jnp.stack(ordered)


def summed(pieces):
    total = pieces[0].astype(f32)
    for i in range(1, len(pieces)):
        total = total + pieces[i].astype(f32)
    return total


def filled(packs, start, arrays):
    packs = list(packs)
    for array in arrays:
        for side, half in enumerate(halves(array)):
            packs[side] = lax.dynamic_update_slice(packs[side], half.astype(bf16), (start, 0))
        start += array.shape[0]
    return packs


def padded_rows(count):
    return count + -count % 512


def tied(*values):
    return lax.optimization_barrier(values)


class SliceTotal:
    def __init__(self, mine, other, apart):
        self.mine, self.state, self.apart = mine, swap_cores(other), apart

    def first(self):
        total = (self.mine.astype(f32) + self.state.astype(f32)).astype(bf16)
        places = lax.axis_size("cplx")
        self.sent = total.reshape(places, -1, total.shape[1])

    def second(self, *others):
        levels = lax.axis_size("smp")
        self.depths = [group.sent.shape[1] for group in (self, *others)]
        totals = [
            summed(group.state).astype(bf16).reshape(levels, -1, group.sent.shape[2])
            for group in (self, *others)
        ]
        self.sent = totals[0] if len(totals) == 1 else jnp.concatenate(totals, axis=1)

    def third(self):
        self.sent = summed(self.state).astype(bf16)

    def fourth(self):
        pieces = self.state
        pieces = in_order(pieces, "smp") if "smp" in self.apart else pieces
        self.sent = pieces.reshape(-1, pieces.shape[2])

    def wait(self, value):
        self.state, value = tied(self.state, value)
        return value

    def lead(self, value):
        self.sent, value = tied(self.sent, value)
        return value

    def trade(self, axis):
        self.state = (traded_apart if axis in self.apart else traded)(self.sent, axis)

    def share(self, axis):
        self.state = (spread_apart if axis in self.apart else spread)(self.sent, axis)

    def result(self):
        pieces = in_order(self.state, "cplx") if "cplx" in self.apart else self.state
        levels = lax.axis_size("smp")
        pieces = pieces.reshape(pieces.shape[0] * levels, -1, pieces.shape[2])
        totals, start = [], 0
        for depth in self.depths:
            share = depth // levels
            piece = pieces[:, start : start + share]
            totals.append(piece.reshape(-1, pieces.shape[2]).astype(f32))
            start += share
        return totals


def total_line(vector):
    vector = vector[0] + swap_cores(vector[1])
    return summed(spread_apart(vector, "smp"))


def sum_samples(array):
    return summed(spread_apart(array.astype(bf16), "smp"))


def halves(array):
    portion = array.shape[-1] // 2
    core = lax.axis_index("qry")
    mine = lax.dynamic_slice_in_dim(array, core * portion, portion, array.ndim - 1)
    other = lax.dynamic_slice_in_dim(array, (1 - core) * portion, portion, array.ndim - 1)
    return mine, other


def gather_rows(piece):
    if piece.shape[1] % 16 == 0:
        return lax.all_gather(piece, "smp", axis=0)
    return lax.all_gather(piece, "smp", axis=1, tiled=True)[None]


def scatter_rows(whole):
    if whole.shape[0] == lax.axis_size("smp"):
        return lax.psum_scatter(whole, "smp", scatter_dimension=0)
    return lax.psum_scatter(whole[0], "smp", scatter_dimension=1, tiled=True)


def per_device(
    single,
    condition,
    pair_features,
    lengths,
    cotangent,
    first_gain,
    first_scale,
    first_offset,
    first_shift,
    query_projection_weight,
    query_bias_vector,
    key_projection_weight,
    value_projection_weight,
    attention_gate_weight,
    attention_output_weight,
    pair_gain,
    pair_project,
    finish_weight,
    finish_offset,
    second_gain,
    second_scale,
    second_offset,
    second_shift,
    transition_swish_weight,
    transition_linear_weight,
    transition_down_weight,
    closing_weight,
    closing_offset,
):
    width = single.shape[3]
    narrow = condition.shape[2]
    half = width // 2
    inner = transition_swish_weight.shape[1]
    heads = pair_project.shape[1]
    meta = jnp.stack([lengths[0], lax.axis_index("qry")]).astype(jnp.int32)
    condition_raw = condition[0]
    condition_norm, condition_factor = normalize(condition_raw.astype(f32))
    pair_weight = centred_project(pair_gain, pair_project)
    bias_pieces = pair_forward(pair_features[0], pair_weight)
    meta, *bias_pieces = tied(meta, *bias_pieces)
    bias_rows = [gather_rows(bias_pieces[0])]
    bias_rows[0], bias_pieces[1] = tied(bias_rows[0], bias_pieces[1])
    bias_rows.append(gather_rows(bias_pieces[1]))

    def modulation(gain, scale_weight, offset, shift_weight):
        low = (condition_norm * gain.astype(f32)).astype(bf16)
        lifting = jax.nn.sigmoid(matmul(low, scale_weight) + offset.astype(f32))
        return low, lifting, matmul(low, shift_weight)

    condition_first, lifting_first, shifting_first = modulation(
        first_gain, first_scale, first_offset, first_shift
    )
    condition_second, lifting_second, shifting_second = modulation(
        second_gain, second_scale, second_offset, second_shift
    )
    finish = jax.nn.sigmoid(matmul(condition_raw, finish_weight) + finish_offset.astype(f32))
    closing = jax.nn.sigmoid(matmul(condition_raw, closing_weight) + closing_offset.astype(f32))
    square_weights = (
        query_projection_weight,
        key_projection_weight,
        value_projection_weight,
        attention_gate_weight,
        attention_output_weight,
    )
    closed, delta_second, closing_sum, lift_second, shift_second, *second_packs = transition(
        meta,
        single[0],
        cotangent[0],
        lifting_second,
        shifting_second,
        closing,
        (transition_swish_weight, transition_linear_weight, transition_down_weight),
        padded_rows(3 * inner + 3 * narrow),
    )

    def modulation_back(lift_sum, shift_sum, low, lifting, scale_weight, shift_weight):
        delta_lift = lift_sum * lifting * (1.0 - lifting)
        scale_total = contract("qc,qd->cd", low, delta_lift)
        shift_total = contract("qc,qd->cd", low, shift_sum)
        delta_condition = contract("qd,cd->qc", delta_lift, scale_weight) + contract(
            "qd,cd->qc", shift_sum, shift_weight
        )
        return scale_total, jnp.sum(delta_lift, axis=0), shift_total, delta_condition

    def gate_back(branch_sum, opened, weight):
        delta = branch_sum * opened * (1.0 - opened)
        return (
            contract("qc,qd->cd", condition_raw, delta),
            jnp.sum(delta, axis=0),
            contract("qd,cd->qc", delta, weight),
        )

    scale_second, offset_second, shift_total_second, cond_delta_second = modulation_back(
        lift_second, shift_second, condition_second, lifting_second, second_scale, second_shift
    )
    closing_total, closing_offset_total, condition_closing = gate_back(
        closing_sum, closing, closing_weight
    )
    early = SliceTotal(
        *filled(second_packs, 3 * inner, (scale_second, shift_total_second, closing_total)),
        apart=EARLY_APART,
    )

    early.mine, meta = tied(early.mine, meta)
    query, key_value, gate, delta_gated, mixed_first = project(
        meta,
        single[0],
        cotangent[0],
        lifting_first,
        shifting_first,
        finish,
        query_bias_vector.astype(f32)[None],
        square_weights,
    )
    pair_of_cores = (key_value, swap_cores(key_value))
    def attend(meta, part, call, earlier):
        return list(
            attention(
                meta, query, pair_of_cores, gate, delta_gated, bias_rows[part], part, call, CALLS,
                earlier,
            )
        )

    attended = []
    query = early.wait(query)
    early.first()
    meta = early.lead(meta)
    early.trade("cplx")
    attended = [attend(meta, 0, 1, attend(meta, 0, 0, ()))]
    done = attend(meta, 1, 0, ())
    done[0] = early.wait(done[0])
    early.second()
    meta = early.lead(meta)
    early.trade("smp")
    attended.append(attend(meta, 1, 1, done))
    delta_bias = [scatter_rows(part[5]) for part in attended]

    def both(index):
        return [part[index] for part in attended]

    arrived = [swap_cores(part) for part in both(4)]
    halved = both(0) + both(1) + both(2)
    def back(meta, start, earlier):
        outs = rows_back(
            meta,
            (single[0], cotangent[0], closed, delta_second),
            halved + both(3) + arrived,
            (lifting_first, lifting_second, finish),
            square_weights,
            start,
            single.shape[1] // 2,
            earlier,
        )
        return list(outs)

    done = back(meta, 0, ())
    last = back(meta, single.shape[1] // 2, tuple(done[:4]))
    block_out, single_grad, delta_key, delta_value = last[:4]
    finish_sum, lift_first, shift_first = [done[i] + last[i] for i in (4, 5, 6)]
    scale_first, offset_first, shift_total_first, cond_delta_first = modulation_back(
        lift_first, shift_first, condition_first, lifting_first, first_scale, first_shift
    )
    finish_total, finish_offset_total, condition_finish = gate_back(
        finish_sum, finish, finish_weight
    )
    *first_packs, query_bias_total = weight_sums(
        meta,
        cotangent[0],
        mixed_first,
        finish,
        [delta_key, delta_value] + halved,
        padded_rows(5 * width + 3 * narrow),
    )
    first_packs[1] = early.wait(first_packs[1])
    early.third()
    first_packs[1] = early.lead(first_packs[1])
    early.share("smp")
    late = SliceTotal(
        *filled(first_packs, 5 * width, (scale_first, shift_total_first, finish_total)),
        apart=LATE_APART,
    )
    gain_first = jnp.sum(cond_delta_first * condition_norm, axis=0)
    gain_second = jnp.sum(cond_delta_second * condition_norm, axis=0)
    condition_grad = sum_samples(
        normalize_back(
            cond_delta_first * first_gain.astype(f32) + cond_delta_second * second_gain.astype(f32),
            condition_norm,
            condition_factor,
        )
        + condition_closing
        + condition_finish
    )
    blocks = pair_features.shape[1] // 16 if pair_features.shape[1] % 16 == 0 else 1
    sizes = (blocks - blocks // 2, blocks // 2)
    delta_bias[0] = late.wait(delta_bias[0])
    late.first()
    pair_weight = late.lead(pair_weight)
    late.trade("cplx")
    early.state, late.state, delta_bias[1] = tied(early.state, late.state, delta_bias[1])
    early.fourth()
    pair_weight = early.lead(pair_weight)
    early.share("cplx")
    late.second()
    pair_weight = late.lead(pair_weight)
    late.trade("smp")
    pair_grad, inner_total = pair_backward(
        pair_features[0], pair_weight, delta_bias, 0, sizes[0], ()
    )
    inner_total = late.wait(inner_total)
    late.third()
    pair_weight = late.lead(pair_weight)
    late.share("smp")
    if sizes[1]:
        pair_grad, more = pair_backward(
            pair_features[0], pair_weight, delta_bias, *sizes, (pair_grad,)
        )
        inner_total = inner_total + more
    early.state = late.wait(early.state)
    late.fourth()
    late.share("cplx")
    pair_gain_total = jnp.sum(inner_total * pair_project.astype(f32).T, axis=0)
    pair_project_total = inner_total * pair_gain.astype(f32)[None]
    vectors = (
        gain_first,
        offset_first,
        query_bias_total[:, 0],
        finish_offset_total,
        gain_second,
        offset_second,
        closing_offset_total,
        pair_gain_total,
    )
    small = total_line(
        jnp.concatenate(
            [jnp.stack(halves(vector)) for vector in vectors]
            + [jnp.stack([half.reshape(-1) for half in halves(pair_project_total.T)])],
            axis=1,
        )
    )
    def unpack(total, sizes):
        arrays, start = [], 0
        for depth, columns in sizes:
            blocks = columns // half
            arrays.append(
                jnp.concatenate(
                    [
                        total[start + b * depth : start + (b + 1) * depth]
                        for b in range(blocks)
                    ],
                    axis=1,
                )
            )
            start += depth * blocks
        return arrays

    early_totals = unpack(
        early.result()[0],
        ((width, inner // 2), (width, inner // 2), (inner, half)) + ((narrow, half),) * 3,
    )
    small, *early_totals = tied(small, *early_totals)
    swish_total, linear_total, down_total, scale_second, shift_second, closing_total = early_totals
    small = summed(spread_apart(small, "cplx"))
    late = late.result()[0]
    ends, place = [], 0
    for vector in vectors:
        ends.append(small[place : place + vector.shape[0] // 2])
        place += vector.shape[0] // 2
    query_total, key_total, value_total, gate_total, output_total, *others = unpack(
        late, ((width, half),) * 5 + ((narrow, half),) * 3
    )
    scale_first, shift_first, finish_total = others
    return (
        block_out[None],
        single_grad[None],
        condition_grad[None],
        pair_grad[None],
        ends[0],
        scale_first,
        ends[1],
        shift_first,
        query_total,
        ends[2],
        key_total,
        value_total,
        gate_total,
        output_total,
        ends[7],
        small[place:].reshape(-1, heads // 2),
        finish_total,
        ends[3],
        ends[4],
        scale_second,
        ends[5],
        shift_second,
        swish_total,
        linear_total,
        down_total,
        closing_total,
        ends[6],
    )


def solution(mesh):
    placed = (
        P("cplx", "smp", "qry", None),
        P("cplx", "qry", None),
        P("cplx", ("qry", "smp"), None, None),
        P("cplx"),
        P("cplx", "smp", "qry", None),
        P(),
        P(),
        P(),
        P(),
        P(),
        P(),
        P(),
        P(),
        P(),
        P(),
        P(),
        P(),
        P(),
        P(),
        P(),
        P(),
        P(),
        P(),
        P(),
        P(),
        P(),
        P(),
        P(),
    )
    return jax.shard_map(
        per_device,
        mesh=mesh,
        in_specs=placed,
        out_specs=(
            P("cplx", "smp", "qry", None),
            P("cplx", "smp", "qry", None),
            P("cplx", "qry", None),
            P("cplx", ("qry", "smp"), None, None),
            P("qry"),
            P(None, "qry"),
            P("qry"),
            P(None, "qry"),
            P(None, "qry"),
            P("qry"),
            P(None, "qry"),
            P(None, "qry"),
            P(None, "qry"),
            P(None, "qry"),
            P("qry"),
            P(None, "qry"),
            P(None, "qry"),
            P("qry"),
            P("qry"),
            P(None, "qry"),
            P("qry"),
            P(None, "qry"),
            P(None, "qry"),
            P(None, "qry"),
            P(None, "qry"),
            P(None, "qry"),
            P("qry"),
        ),
        check_vma=False,
    )
```

```python
import functools

import jax
import jax.numpy as jnp
from jax import lax
from jax.experimental import pallas as pl
from jax.experimental.pallas import tpu as pltpu
from jax.sharding import PartitionSpec as P

EPSILON = 1e-05
LANES = 128
VMEM_LIMIT = 56 * 2**20
SHARES = (10, 6)
CALLS = (1, 2)
EARLY_APART = ("smp",)
LATE_APART = ("smp",)
f32 = jnp.float32
bf16 = jnp.bfloat16


def normalize(values):
    centre = values - jnp.mean(values, axis=-1, keepdims=True)
    factor = lax.rsqrt(jnp.mean(centre * centre, axis=-1, keepdims=True) + EPSILON)
    return (centre * factor, factor)


def normalize_back(incoming, normed, factor):
    return factor * (
        incoming
        - jnp.mean(incoming, axis=-1, keepdims=True)
        - normed * jnp.mean(incoming * normed, axis=-1, keepdims=True)
    )


def matmul(left, right):
    return jnp.dot(left, right, preferred_element_type=jnp.float32)


def contract(form, left, right):
    return jnp.einsum(
        form, left.astype(bf16), right.astype(bf16), preferred_element_type=jnp.float32
    )


def dot(left, right, left_dim, right_dim):
    return lax.dot_general(
        left, right, (((left_dim,), (right_dim,)), ((), ())), preferred_element_type=f32
    )


def attention_kernel(
    meta, query, mine, other, gate, delta_gated, bias, *refs, step
):
    (
        gated, delta_gate, delta_query, kept, sent, delta_bias, score, prob, slope,
    ) = refs[-9:]
    samples, head_width, rows = query.shape
    total = 2 * rows
    pieces, piece_rows = bias.shape[0], bias.shape[2]
    scale = head_width ** (-0.5)
    second = meta[1] == 1
    column = lax.broadcasted_iota(jnp.int32, (16, total), 1)
    line = lax.broadcasted_iota(jnp.int32, (16, total), 0)
    masking = jnp.where((line == 0) & (column >= meta[0]), -1e30, 0.0).astype(bf16)
    pair_ones = jnp.where(line < 2, 1.0, 0.0).astype(bf16)
    query_line = lax.broadcasted_iota(jnp.int32, (16, rows), 0)
    one_line = jnp.where(query_line == 0, 1.0, 0.0).astype(bf16)
    spots = [
        (piece, start, piece * piece_rows + start)
        for piece in range(pieces)
        for start in range(0, piece_rows, step)
    ]

    def joined(mine, other):
        mine, other = mine[:, :rows], other[:, :rows]
        first = jnp.where(second, other, mine)
        last = jnp.where(second, mine, other)
        return jnp.concatenate([first, last], axis=1)

    def parted(whole, sample, which):
        first, last = whole[:, :rows], whole[:, rows:]
        kept[sample, which] = jnp.where(second, last, first)
        sent[sample, which, :, :rows] = jnp.where(second, first, last).astype(sent.dtype)

    keys, values = [], []
    for s in range(samples):
        keys.append(joined(mine[s, 0], other[s, 0]))
        values.append(joined(mine[s, 1], other[s, 1]))
        score[s] = dot(
            jnp.concatenate([query[s], one_line], axis=0),
            jnp.concatenate([keys[s], masking], axis=0),
            0,
            0,
        )
    for piece, start, place in spots:
        bias_here = bias[piece, 0, start : start + step, :].astype(f32)
        here = slice(place, place + step)
        for s in range(samples):
            line_scores = score[s, here, :] * scale + bias_here
            highest = jnp.max(line_scores, axis=1, keepdims=True)
            exponent = jnp.exp(line_scores - highest)
            soft = exponent * (1.0 / jnp.sum(exponent, axis=1, keepdims=True))
            score[s, here, :] = soft
            prob[s, here, :] = soft.astype(bf16)
    for s in range(samples):
        attended = dot(values[s], prob[s], 1, 1)
        gate_here, delta_here = gate[s], delta_gated[s]
        gated[s] = (gate_here * attended).astype(bf16)
        delta_attended = (delta_here * gate_here).astype(bf16)
        delta_gate[s] = (delta_here * attended * gate_here * (1.0 - gate_here)).astype(bf16)
        centre = jnp.sum(delta_attended.astype(f32) * attended, axis=0, keepdims=True)
        coarse = centre.astype(bf16).astype(f32)
        rest = jnp.where(
            query_line == 0, -coarse, jnp.where(query_line == 1, coarse - centre, 0.0)
        ).astype(bf16)
        slope[s] = dot(
            jnp.concatenate([delta_attended, rest], axis=0),
            jnp.concatenate([values[s], pair_ones], axis=0),
            0,
            0,
        )
        parted(dot(delta_attended, prob[s], 1, 0), s, 1)
    for piece, start, place in spots:
        here = slice(place, place + step)
        total_here = None
        for s in range(samples):
            delta_scores = score[s, here, :] * slope[s, here, :]
            prob[s, here, :] = delta_scores.astype(bf16)
            total_here = delta_scores if total_here is None else total_here + delta_scores
        delta_bias[piece, 0, start : start + step, :] = total_here.astype(bf16)
    for s in range(samples):
        delta_query[s] = (dot(keys[s], prob[s], 1, 1) * scale).astype(bf16)
        parted(dot(query[s], prob[s], 1, 0) * scale, s, 0)


def attention(
    meta, query, pair_of_cores, gate, delta_gated, bias, part, call, calls, earlier
):
    samples, width, rows = query.shape
    pieces, heads, piece_rows, total = bias.shape
    head_width = width // sum(SHARES)
    step = 16 if piece_rows % 16 == 0 else piece_rows
    count = heads // calls
    inside = call * count
    first = sum(SHARES[:part]) + inside
    padded = pair_of_cores[0].shape[3]

    def spec(columns, offset):
        return pl.BlockSpec((samples, head_width, columns), lambda h, meta: (0, offset + h, 0))

    inner, outer = spec(rows, first), spec(rows, inside)

    def double(columns, offset):
        return pl.BlockSpec(
            (samples, 2, head_width, columns), lambda h, meta: (0, 0, offset + h, 0)
        )

    tile = pl.BlockSpec((pieces, 1, piece_rows, total), lambda h, meta: (0, inside + h, 0, 0))

    def made(dtype, columns=rows, lead=(samples,)):
        return jax.ShapeDtypeStruct(lead + (heads * head_width, columns), dtype)

    return pl.pallas_call(
        functools.partial(attention_kernel, step=step),
        grid_spec=pltpu.PrefetchScalarGridSpec(
            num_scalar_prefetch=1,
            grid=(count,),
            in_specs=[inner]
            + [double(padded, first)] * 2
            + [inner] * 2
            + [tile]
            + [pl.BlockSpec(memory_space=pl.ANY)] * len(earlier),
            out_specs=[outer] * 3 + [double(rows, inside), double(padded, inside), tile],
            scratch_shapes=[
                pltpu.VMEM((samples, rows, total), f32),
                pltpu.VMEM((samples, rows, total), bf16),
                pltpu.VMEM((samples, rows, total), f32),
            ],
        ),
        out_shape=[
            made(bf16), made(bf16), made(bf16), made(f32, rows, (samples, 2)),
            made(bf16, padded, (samples, 2)),
            jax.ShapeDtypeStruct(bias.shape, bf16),
        ],
        input_output_aliases={7 + i: i for i in range(len(earlier))},
        compiler_params=pltpu.CompilerParams(vmem_limit_bytes=VMEM_LIMIT),
        cost_estimate=pl.CostEstimate(flops=1, bytes_accessed=1, transcendentals=0),
    )(meta, query, *pair_of_cores, gate, delta_gated, bias, *earlier)


def centred_project(gain, project):
    weight = (project.astype(f32) * gain.astype(f32)[:, None]).T
    weight = weight - jnp.mean(weight, axis=1, keepdims=True)
    high = lax.reduce_precision(weight, 8, 7)
    return jnp.concatenate([high.astype(bf16), (weight - high).astype(bf16)], axis=0)


def turned_norm(rows):
    turned = rows.T.astype(f32)
    centre = turned - jnp.mean(turned, axis=0, keepdims=True)
    return centre, lax.rsqrt(jnp.mean(centre * centre, axis=0, keepdims=True) + EPSILON)


def head_spots():
    return [(part, i) for part, share in enumerate(SHARES) for i in range(share)]


def pair_forward_kernel(pair, weight, *refs, block, heads):
    outs, wide = refs[:-1], refs[-1]

    def one(i, carry):
        centre, factor = turned_norm(pair[i])
        both = dot(weight[...], centre.astype(bf16), 1, 0)
        line = (both[:heads] + both[heads:]) * factor
        for t in range(wide.shape[0]):
            wide[t, pl.ds(pl.multiple_of(i * heads, heads), heads), :] = line[
                :, t * LANES : (t + 1) * LANES
            ]
        return carry

    lax.fori_loop(0, block, one, 0, unroll=8 if block % 8 == 0 else 1)
    for h, (part, i) in enumerate(head_spots()):
        for t in range(wide.shape[0]):
            outs[part][i, :, t * LANES : (t + 1) * LANES] = wide[
                t, pl.ds(h, block, stride=heads), :
            ].astype(bf16)


def pair_forward(pair, weight):
    rows, length, width = pair.shape
    heads = weight.shape[0] // 2
    block = 16 if rows % 16 == 0 else rows
    return pl.pallas_call(
        functools.partial(pair_forward_kernel, block=block, heads=heads),
        grid=(rows // block,),
        in_specs=[
            pl.BlockSpec((block, length, width), lambda i: (i, 0, 0)),
            pl.BlockSpec((2 * heads, width), lambda i: (0, 0)),
        ],
        out_specs=[pl.BlockSpec((share, block, length), lambda i: (0, i, 0)) for share in SHARES],
        out_shape=[jax.ShapeDtypeStruct((share, rows, length), bf16) for share in SHARES],
        scratch_shapes=[pltpu.VMEM((length // LANES, block * heads, LANES), f32)],
        compiler_params=pltpu.CompilerParams(vmem_limit_bytes=VMEM_LIMIT),
        cost_estimate=pl.CostEstimate(flops=1, bytes_accessed=1, transcendentals=0),
    )(pair, weight)


def pair_backward_kernel(pair, weight, *refs, block, heads):
    deltas = refs[: len(SHARES)]
    out, inner_out, wide, inner_sum = refs[-4:]
    step = pl.program_id(0)

    @pl.when(step == 0)
    def _():
        inner_sum[...] = jnp.zeros_like(inner_sum)

    for h, (part, place) in enumerate(head_spots()):
        for t in range(wide.shape[0]):
            wide[t, h * block : (h + 1) * block, :] = deltas[part][
                place, :, t * LANES : (t + 1) * LANES
            ].astype(f32)

    def one(i, carry):
        centre, factor = turned_norm(pair[i])
        normed = centre * factor
        delta = jnp.concatenate(
            [wide[t, pl.ds(i, heads, stride=block), :] for t in range(wide.shape[0])], axis=1
        ).astype(bf16)
        incoming = dot(weight[...], jnp.concatenate([delta, delta], axis=0), 0, 0)
        inner_sum[...] += dot(delta, normed.astype(bf16), 1, 1)
        along = jnp.mean(incoming * normed, axis=0, keepdims=True)
        out[i] = ((incoming - normed * along) * factor).T
        return carry

    lax.fori_loop(0, block, one, 0, unroll=4 if block % 4 == 0 else 1)

    @pl.when(step == pl.num_programs(0) - 1)
    def _():
        inner_out[...] = inner_sum[...]


def pair_backward(pair, weight, deltas, start, count, earlier):
    rows, length, width = pair.shape
    heads = weight.shape[0] // 2
    parts = len(deltas)
    block = 16 if rows % 16 == 0 else rows
    return pl.pallas_call(
        functools.partial(pair_backward_kernel, block=block, heads=heads),
        grid=(count,),
        in_specs=[
            pl.BlockSpec((block, length, width), lambda i: (start + i, 0, 0)),
            pl.BlockSpec((2 * heads, width), lambda i: (0, 0)),
        ]
        + [
            pl.BlockSpec((share, block, length), lambda i: (0, start + i, 0)) for share in SHARES
        ]
        + [pl.BlockSpec(memory_space=pl.ANY)] * len(earlier),
        out_specs=[
            pl.BlockSpec((block, length, width), lambda i: (start + i, 0, 0)),
            pl.BlockSpec((heads, width), lambda i: (0, 0)),
        ],
        out_shape=[
            jax.ShapeDtypeStruct((rows, length, width), f32),
            jax.ShapeDtypeStruct((heads, width), f32),
        ],
        scratch_shapes=[
            pltpu.VMEM((length // LANES, block * heads, LANES), f32),
            pltpu.VMEM((heads, width), f32),
        ],
        input_output_aliases={2 + parts: 0} if earlier else {},
        compiler_params=pltpu.CompilerParams(vmem_limit_bytes=VMEM_LIMIT),
        cost_estimate=pl.CostEstimate(flops=1, bytes_accessed=1, transcendentals=0),
    )(pair, weight, *deltas, *earlier)


def fixed(shape):
    return pl.BlockSpec(shape, lambda s, *_: (0,) * len(shape), pipeline_mode=pl.Buffered(1))


def by_sample(shape, buffers=2):
    return pl.BlockSpec(
        (1,) + shape,
        lambda s, *_: (s,) + (0,) * len(shape),
        pipeline_mode=pl.Buffered(buffers),
    )


def row_valid(meta, rows):
    place = lax.broadcasted_iota(jnp.int32, (rows, 1), 0) + meta[1] * rows
    return jnp.where(place < meta[0], 1.0, 0.0)


def pack_columns(meta, packs, arrays, start=0):
    tile = packs[0].shape[1]
    for array in arrays:
        depth, share = array.shape[0], array.shape[1] // 2
        for side in range(2):
            core = meta[1] if side == 0 else 1 - meta[1]
            for block in range(share // tile):
                column = pl.multiple_of(core * share + block * tile, LANES)
                packs[side][start + block * depth : start + (block + 1) * depth, :] = array[
                    :, pl.ds(column, tile)
                ].astype(bf16)
        start += depth * (share // tile)


def project_kernel(
    meta, single, cotangent, lifting, shifting, finish, query_bias,
    query_weight, key_weight, value_weight, gate_weight, output_weight,
    query, key_value, gate, delta_gated, mixed_out,
):
    rows = single.shape[1]
    normed, _ = normalize(single[0].astype(f32))
    mixed = (lifting[...] * normed + shifting[...]).astype(bf16)
    mixed_out[0] = mixed
    query[0] = (dot(mixed, query_weight[...], 1, 0) + query_bias[...]).astype(bf16).T
    key_value[0, 0, :, :rows] = dot(mixed, key_weight[...], 1, 0).astype(bf16).T
    key_value[0, 1, :, :rows] = dot(mixed, value_weight[...], 1, 0).astype(bf16).T
    gate[0] = jax.nn.sigmoid(dot(mixed, gate_weight[...], 1, 0)).T
    branch = row_valid(meta, rows) * cotangent[0].astype(f32)
    lifted = (finish[...] * branch).astype(bf16)
    delta_gated[0] = dot(lifted, output_weight[...], 1, 1).T


def project(meta, single, cotangent, lifting, shifting, finish, query_bias, weights):
    samples, rows, width = single.shape
    natural, turned = by_sample((rows, width)), by_sample((width, rows))
    flat, square = fixed((rows, width)), fixed((width, width))
    padded = rows + -rows % LANES
    wide = by_sample((2, width, padded))
    return pl.pallas_call(
        project_kernel,
        grid_spec=pltpu.PrefetchScalarGridSpec(
            num_scalar_prefetch=1,
            grid=(samples,),
            in_specs=[natural, natural, flat, flat, flat, fixed((1, width))] + [square] * 5,
            out_specs=[turned, wide, turned, turned, natural],
        ),
        out_shape=[
            jax.ShapeDtypeStruct(shape, dtype)
            for shape, dtype in (
                ((samples, width, rows), bf16),
                ((samples, 2, width, padded), bf16),
                ((samples, width, rows), f32),
                ((samples, width, rows), f32),
            )
        ]
        + [jax.ShapeDtypeStruct((samples, rows, width), bf16)],
        compiler_params=pltpu.CompilerParams(vmem_limit_bytes=VMEM_LIMIT),
        cost_estimate=pl.CostEstimate(flops=1, bytes_accessed=1, transcendentals=0),
    )(meta, single, cotangent, lifting, shifting, finish, query_bias, *weights)


def transition_kernel(
    meta, single, cotangent, lifting, shifting, closing,
    swish_weight, linear_weight, down_weight,
    closed, delta_second, closing_sum, lift_sum, shift_sum, pack_mine, pack_other,
    swish_sum, linear_sum, down_sum,
):
    rows = single.shape[1]
    sample = pl.program_id(0)
    normed, _ = normalize(single[0].astype(f32))
    mixed = (lifting[...] * normed + shifting[...]).astype(bf16)
    up_swish = dot(mixed, swish_weight[...], 1, 0)
    up_linear = dot(mixed, linear_weight[...], 1, 0)
    squash = jax.nn.sigmoid(up_swish)
    silu = up_swish * squash
    hidden = (silu * up_linear).astype(bf16)
    moved = dot(hidden, down_weight[...], 1, 0)
    closing_here = closing[...]
    branch = row_valid(meta, rows) * cotangent[0].astype(f32)
    closed[0] = closing_here * moved
    delta_moved = (closing_here * branch).astype(bf16)
    delta_hidden = dot(delta_moved, down_weight[...], 1, 1)
    delta_swish = (delta_hidden * up_linear * squash * (1.0 + up_swish * (1.0 - squash))).astype(bf16)
    delta_linear = (delta_hidden * silu).astype(bf16)
    second = dot(delta_swish, swish_weight[...], 1, 1) + dot(
        delta_linear, linear_weight[...], 1, 1
    )
    delta_second[0] = second

    def collect(first):
        def put(ref, value):
            if first:
                ref[...] = value
            else:
                ref[...] += value

        put(closing_sum, branch * moved)
        put(lift_sum, second * normed)
        put(shift_sum, second)
        put(swish_sum, dot(mixed, delta_swish, 0, 0))
        put(linear_sum, dot(mixed, delta_linear, 0, 0))
        put(down_sum, dot(hidden, delta_moved, 0, 0))

    @pl.when(sample == 0)
    def _():
        collect(True)

    @pl.when(sample > 0)
    def _():
        collect(False)

    @pl.when(sample == pl.num_programs(0) - 1)
    def _():
        pack_columns(meta, (pack_mine, pack_other), (swish_sum, linear_sum, down_sum))


def transition(meta, single, cotangent, lifting, shifting, closing, weights, pack_rows):
    samples, rows, width = single.shape
    inner = weights[0].shape[1]
    natural, flat = by_sample((rows, width)), fixed((rows, width))
    up, down = (width, inner), (inner, width)
    pack = (pack_rows, width // 2)
    return pl.pallas_call(
        transition_kernel,
        grid_spec=pltpu.PrefetchScalarGridSpec(
            num_scalar_prefetch=1,
            grid=(samples,),
            in_specs=[natural, natural, flat, flat, flat, fixed(up), fixed(up), fixed(down)],
            out_specs=[natural, natural, flat, flat, flat, fixed(pack), fixed(pack)],
            scratch_shapes=[pltpu.VMEM(up, f32), pltpu.VMEM(up, f32), pltpu.VMEM(down, f32)],
        ),
        out_shape=[
            jax.ShapeDtypeStruct(shape, f32)
            for shape in ((samples, rows, width),) * 2 + ((rows, width),) * 3
        ]
        + [jax.ShapeDtypeStruct(pack, bf16)] * 2,
        compiler_params=pltpu.CompilerParams(vmem_limit_bytes=VMEM_LIMIT),
        cost_estimate=pl.CostEstimate(flops=1, bytes_accessed=1, transcendentals=0),
    )(meta, single, cotangent, lifting, shifting, closing, *weights)


def whole(*parts):
    return jnp.concatenate([part[0] for part in parts], axis=0)


def whole_at(*parts):
    return [jnp.concatenate([part[0, i] for part in parts], axis=0) for i in range(2)]


def put(first, ref, value):
    if first:
        ref[...] = value
    else:
        ref[...] += value


def weights_kernel(
    meta, cotangent, mixed, finish,
    key, value, gated_a, gated_b, gate_a, gate_b, query_a, query_b,
    pack_mine, pack_other, bias_sum,
    query_sum, key_sum, value_sum, gate_sum, output_sum,
):
    count, rows, width = cotangent.shape
    sample = pl.program_id(0)

    def turned(*parts):
        return jnp.concatenate(
            [jnp.concatenate([part[i] for part in parts], axis=0) for i in range(count)], axis=1
        )

    delta_query = turned(query_a, query_b)
    mixed_rows = mixed[...].reshape(count * rows, width)
    masked = finish[...] * row_valid(meta, rows)
    lifted = jnp.concatenate(
        [(masked * cotangent[i].astype(f32)).astype(bf16) for i in range(count)], axis=0
    )

    def collect(first):
        put(first, query_sum, dot(delta_query, mixed_rows, 1, 0))
        put(first, key_sum, dot(turned(key), mixed_rows, 1, 0))
        put(first, value_sum, dot(turned(value), mixed_rows, 1, 0))
        put(first, gate_sum, dot(turned(gate_a, gate_b), mixed_rows, 1, 0))
        put(first, output_sum, dot(turned(gated_a, gated_b), lifted, 1, 0))
        put(first, bias_sum, jnp.sum(delta_query.astype(f32), axis=1, keepdims=True))

    @pl.when(sample == 0)
    def _():
        collect(True)

    @pl.when(sample > 0)
    def _():
        collect(False)

    @pl.when(sample == pl.num_programs(0) - 1)
    def _():
        width = query_sum.shape[0]
        half = width // 2
        packs = (pack_mine, pack_other)
        for i, array in enumerate((query_sum, key_sum, value_sum, gate_sum)):
            for side in range(2):
                core = meta[1] if side == 0 else 1 - meta[1]
                row = pl.multiple_of(core * half, LANES)
                packs[side][i * width : (i + 1) * width, :] = array[
                    pl.ds(row, half), :
                ].T.astype(bf16)
        pack_columns(meta, packs, (output_sum,), 4 * width)


def weight_sums(meta, cotangent, mixed, finish, turned, pack_rows):
    samples, rows, width = cotangent.shape
    pack = (pack_rows, width // 2)
    count = 2 if samples % 2 == 0 else 1

    def several(shape):
        return pl.BlockSpec((count,) + shape, lambda s, *_: (s,) + (0,) * len(shape))

    natural = several((rows, width))
    return pl.pallas_call(
        weights_kernel,
        grid_spec=pltpu.PrefetchScalarGridSpec(
            num_scalar_prefetch=1,
            grid=(samples // count,),
            in_specs=[natural, natural, fixed((rows, width))]
            + [several(array.shape[1:]) for array in turned],
            out_specs=[fixed(pack)] * 2 + [fixed((width, 1))],
            scratch_shapes=[pltpu.VMEM((width, width), f32)] * 5,
        ),
        out_shape=[jax.ShapeDtypeStruct(pack, bf16)] * 2
        + [jax.ShapeDtypeStruct((width, 1), f32)],
        compiler_params=pltpu.CompilerParams(vmem_limit_bytes=VMEM_LIMIT),
        cost_estimate=pl.CostEstimate(flops=1, bytes_accessed=1, transcendentals=0),
    )(meta, cotangent, mixed, finish, *turned)


def rows_kernel(
    meta, single, cotangent, closed, delta_second,
    gated_a, gated_b, gate_a, gate_b, query_a, query_b, kept_a, kept_b, came_a, came_b,
    lifting_first, lifting_second, finish,
    query_weight, key_weight, value_weight, gate_weight, output_weight,
    *refs,
):
    block_out, single_grad, key_out, value_out, finish_sum, lift_first, shift_first = refs[-7:]
    rows = single.shape[1]
    kept, came = whole_at(kept_a, kept_b), whole_at(came_a, came_b)
    delta_key, delta_value = [
        (kept[i] + came[i][:, :rows].astype(f32)).astype(bf16) for i in range(2)
    ]
    key_out[0] = delta_key
    value_out[0] = delta_value
    sample = pl.program_id(0)
    residual = single[0].astype(f32)
    normed, factor = normalize(residual)
    valid = row_valid(meta, rows)
    outgoing = cotangent[0].astype(f32)
    branch = valid * outgoing
    raised = dot(whole(gated_a, gated_b), output_weight[...], 0, 0)
    block_out[0] = (residual + valid * (finish[...] * raised + closed[0])).astype(bf16)
    delta_first = (
        dot(whole(query_a, query_b), query_weight[...], 0, 1)
        + dot(delta_key, key_weight[...], 0, 1)
        + dot(delta_value, value_weight[...], 0, 1)
        + dot(whole(gate_a, gate_b), gate_weight[...], 0, 1)
    )
    incoming = delta_first * lifting_first[...] + delta_second[0] * lifting_second[...]
    single_grad[0] = outgoing + normalize_back(incoming, normed, factor)

    def collect(first):
        put(first, finish_sum, branch * raised)
        put(first, lift_first, delta_first * normed)
        put(first, shift_first, delta_first)

    @pl.when(sample == 0)
    def _():
        collect(True)

    @pl.when(sample > 0)
    def _():
        collect(False)


def rows_back(meta, naturals, halved, flats, weights, start, count, earlier):
    samples, rows, width = naturals[0].shape
    flat, square = fixed((rows, width)), fixed((width, width))

    def moved(shape):
        return pl.BlockSpec((1,) + shape, lambda s, *_: (start + s,) + (0,) * len(shape))

    natural = moved((rows, width))
    return pl.pallas_call(
        rows_kernel,
        grid_spec=pltpu.PrefetchScalarGridSpec(
            num_scalar_prefetch=1,
            grid=(count,),
            in_specs=[natural] * 4
            + [moved(array.shape[1:]) for array in halved]
            + [flat] * 3
            + [square] * 5
            + [pl.BlockSpec(memory_space=pl.ANY)] * len(earlier),
            out_specs=[natural] * 2 + [moved((width, rows))] * 2 + [flat] * 3,
        ),
        out_shape=[
            jax.ShapeDtypeStruct((samples, rows, width), bf16),
            jax.ShapeDtypeStruct((samples, rows, width), f32),
        ]
        + [jax.ShapeDtypeStruct((samples, width, rows), bf16)] * 2
        + [jax.ShapeDtypeStruct((rows, width), f32)] * 3,
        input_output_aliases={23 + i: i for i in range(len(earlier))},
        compiler_params=pltpu.CompilerParams(vmem_limit_bytes=VMEM_LIMIT),
        cost_estimate=pl.CostEstimate(flops=1, bytes_accessed=1, transcendentals=0),
    )(meta, *naturals, *halved, *flats, *weights, *earlier)


def swap_cores(array):
    return lax.ppermute(array, "qry", [(0, 1), (1, 0)])


def traded(array, axis):
    return lax.all_to_all(array, axis, 0, 0)


def spread(array, axis):
    return traded(jnp.broadcast_to(array[None], (lax.axis_size(axis),) + array.shape), axis)


def exchange(array, axis, bit):
    return lax.ppermute(array, axis, [(i, i ^ bit) for i in range(lax.axis_size(axis))])


def pick(array, index):
    return lax.dynamic_index_in_dim(array, index, 0, keepdims=False)


def traded_apart(array, axis):
    place = lax.axis_index(axis)
    return [pick(array, place)] + [
        exchange(pick(array, place ^ shift), axis, shift)
        for shift in range(1, lax.axis_size(axis))
    ]


def spread_apart(array, axis):
    return [array] + [exchange(array, axis, shift) for shift in range(1, lax.axis_size(axis))]


def in_order(pieces, axis):
    place, ordered = lax.axis_index(axis), []
    for j in range(len(pieces)):
        chosen = pieces[j]
        for shift in range(1, len(pieces)):
            chosen = jnp.where(place == shift, pieces[j ^ shift], chosen)
        ordered.append(chosen)
    return jnp.stack(ordered)


def summed(pieces):
    total = pieces[0].astype(f32)
    for i in range(1, len(pieces)):
        total = total + pieces[i].astype(f32)
    return total


def filled(packs, start, arrays):
    packs = list(packs)
    for array in arrays:
        for side, half in enumerate(halves(array)):
            packs[side] = lax.dynamic_update_slice(packs[side], half.astype(bf16), (start, 0))
        start += array.shape[0]
    return packs


def padded_rows(count):
    return count + -count % 512


def tied(*values):
    return lax.optimization_barrier(values)


class SliceTotal:
    def __init__(self, mine, other, apart):
        self.mine, self.state, self.apart = mine, swap_cores(other), apart

    def first(self):
        total = (self.mine.astype(f32) + self.state.astype(f32)).astype(bf16)
        places = lax.axis_size("cplx")
        self.sent = total.reshape(places, -1, total.shape[1])

    def second(self, *others):
        levels = lax.axis_size("smp")
        self.depths = [group.sent.shape[1] for group in (self, *others)]
        totals = [
            summed(group.state).astype(bf16).reshape(levels, -1, group.sent.shape[2])
            for group in (self, *others)
        ]
        self.sent = totals[0] if len(totals) == 1 else jnp.concatenate(totals, axis=1)

    def third(self):
        self.sent = summed(self.state).astype(bf16)

    def fourth(self):
        pieces = self.state
        pieces = in_order(pieces, "smp") if "smp" in self.apart else pieces
        self.sent = pieces.reshape(-1, pieces.shape[2])

    def wait(self, value):
        self.state, value = tied(self.state, value)
        return value

    def lead(self, value):
        self.sent, value = tied(self.sent, value)
        return value

    def trade(self, axis):
        self.state = (traded_apart if axis in self.apart else traded)(self.sent, axis)

    def share(self, axis):
        self.state = (spread_apart if axis in self.apart else spread)(self.sent, axis)

    def result(self):
        pieces = in_order(self.state, "cplx") if "cplx" in self.apart else self.state
        levels = lax.axis_size("smp")
        pieces = pieces.reshape(pieces.shape[0] * levels, -1, pieces.shape[2])
        totals, start = [], 0
        for depth in self.depths:
            share = depth // levels
            piece = pieces[:, start : start + share]
            totals.append(piece.reshape(-1, pieces.shape[2]).astype(f32))
            start += share
        return totals


def total_line(vector):
    vector = vector[0] + swap_cores(vector[1])
    return summed(spread_apart(vector, "smp"))


def sum_samples(array):
    return summed(spread_apart(array.astype(bf16), "smp"))


def halves(array):
    portion = array.shape[-1] // 2
    core = lax.axis_index("qry")
    mine = lax.dynamic_slice_in_dim(array, core * portion, portion, array.ndim - 1)
    other = lax.dynamic_slice_in_dim(array, (1 - core) * portion, portion, array.ndim - 1)
    return mine, other


def gather_rows(piece):
    if piece.shape[1] % 16 == 0:
        return lax.all_gather(piece, "smp", axis=0)
    return lax.all_gather(piece, "smp", axis=1, tiled=True)[None]


def scatter_rows(whole):
    if whole.shape[0] == lax.axis_size("smp"):
        return lax.psum_scatter(whole, "smp", scatter_dimension=0)
    return lax.psum_scatter(whole[0], "smp", scatter_dimension=1, tiled=True)


def per_device(
    single,
    condition,
    pair_features,
    lengths,
    cotangent,
    first_gain,
    first_scale,
    first_offset,
    first_shift,
    query_projection_weight,
    query_bias_vector,
    key_projection_weight,
    value_projection_weight,
    attention_gate_weight,
    attention_output_weight,
    pair_gain,
    pair_project,
    finish_weight,
    finish_offset,
    second_gain,
    second_scale,
    second_offset,
    second_shift,
    transition_swish_weight,
    transition_linear_weight,
    transition_down_weight,
    closing_weight,
    closing_offset,
):
    width = single.shape[3]
    narrow = condition.shape[2]
    half = width // 2
    inner = transition_swish_weight.shape[1]
    heads = pair_project.shape[1]
    meta = jnp.stack([lengths[0], lax.axis_index("qry")]).astype(jnp.int32)
    condition_raw = condition[0]
    condition_norm, condition_factor = normalize(condition_raw.astype(f32))
    pair_weight = centred_project(pair_gain, pair_project)
    bias_pieces = pair_forward(pair_features[0], pair_weight)
    meta, *bias_pieces = tied(meta, *bias_pieces)
    bias_rows = [gather_rows(bias_pieces[0])]
    bias_rows[0], bias_pieces[1] = tied(bias_rows[0], bias_pieces[1])
    bias_rows.append(gather_rows(bias_pieces[1]))

    def modulation(gain, scale_weight, offset, shift_weight):
        low = (condition_norm * gain.astype(f32)).astype(bf16)
        lifting = jax.nn.sigmoid(matmul(low, scale_weight) + offset.astype(f32))
        return low, lifting, matmul(low, shift_weight)

    condition_first, lifting_first, shifting_first = modulation(
        first_gain, first_scale, first_offset, first_shift
    )
    condition_second, lifting_second, shifting_second = modulation(
        second_gain, second_scale, second_offset, second_shift
    )
    finish = jax.nn.sigmoid(matmul(condition_raw, finish_weight) + finish_offset.astype(f32))
    closing = jax.nn.sigmoid(matmul(condition_raw, closing_weight) + closing_offset.astype(f32))
    square_weights = (
        query_projection_weight,
        key_projection_weight,
        value_projection_weight,
        attention_gate_weight,
        attention_output_weight,
    )
    closed, delta_second, closing_sum, lift_second, shift_second, *second_packs = transition(
        meta,
        single[0],
        cotangent[0],
        lifting_second,
        shifting_second,
        closing,
        (transition_swish_weight, transition_linear_weight, transition_down_weight),
        padded_rows(3 * inner + 3 * narrow),
    )

    def modulation_back(lift_sum, shift_sum, low, lifting, scale_weight, shift_weight):
        delta_lift = lift_sum * lifting * (1.0 - lifting)
        scale_total = contract("qc,qd->cd", low, delta_lift)
        shift_total = contract("qc,qd->cd", low, shift_sum)
        delta_condition = contract("qd,cd->qc", delta_lift, scale_weight) + contract(
            "qd,cd->qc", shift_sum, shift_weight
        )
        return scale_total, jnp.sum(delta_lift, axis=0), shift_total, delta_condition

    def gate_back(branch_sum, opened, weight):
        delta = branch_sum * opened * (1.0 - opened)
        return (
            contract("qc,qd->cd", condition_raw, delta),
            jnp.sum(delta, axis=0),
            contract("qd,cd->qc", delta, weight),
        )

    scale_second, offset_second, shift_total_second, cond_delta_second = modulation_back(
        lift_second, shift_second, condition_second, lifting_second, second_scale, second_shift
    )
    closing_total, closing_offset_total, condition_closing = gate_back(
        closing_sum, closing, closing_weight
    )
    early = SliceTotal(
        *filled(second_packs, 3 * inner, (scale_second, shift_total_second, closing_total)),
        apart=EARLY_APART,
    )

    early.mine, meta = tied(early.mine, meta)
    query, key_value, gate, delta_gated, mixed_first = project(
        meta,
        single[0],
        cotangent[0],
        lifting_first,
        shifting_first,
        finish,
        query_bias_vector.astype(f32)[None],
        square_weights,
    )
    pair_of_cores = (key_value, swap_cores(key_value))
    def attend(meta, part, call, earlier):
        return list(
            attention(
                meta, query, pair_of_cores, gate, delta_gated, bias_rows[part], part, call, CALLS[part],
                earlier,
            )
        )

    attended = []
    query = early.wait(query)
    early.first()
    meta = early.lead(meta)
    early.trade("cplx")
    attended = [attend(meta, 0, 0, ())]
    done = attend(meta, 1, 0, ())
    done[0] = early.wait(done[0])
    early.second()
    meta = early.lead(meta)
    early.trade("smp")
    attended.append(attend(meta, 1, 1, done))
    delta_bias = [scatter_rows(part[5]) for part in attended]

    def both(index):
        return [part[index] for part in attended]

    arrived = [swap_cores(part) for part in both(4)]
    halved = both(0) + both(1) + both(2)
    def back(meta, start, earlier):
        outs = rows_back(
            meta,
            (single[0], cotangent[0], closed, delta_second),
            halved + both(3) + arrived,
            (lifting_first, lifting_second, finish),
            square_weights,
            start,
            single.shape[1] // 2,
            earlier,
        )
        return list(outs)

    done = back(meta, 0, ())
    last = back(meta, single.shape[1] // 2, tuple(done[:4]))
    block_out, single_grad, delta_key, delta_value = last[:4]
    finish_sum, lift_first, shift_first = [done[i] + last[i] for i in (4, 5, 6)]
    scale_first, offset_first, shift_total_first, cond_delta_first = modulation_back(
        lift_first, shift_first, condition_first, lifting_first, first_scale, first_shift
    )
    finish_total, finish_offset_total, condition_finish = gate_back(
        finish_sum, finish, finish_weight
    )
    *first_packs, query_bias_total = weight_sums(
        meta,
        cotangent[0],
        mixed_first,
        finish,
        [delta_key, delta_value] + halved,
        padded_rows(5 * width + 3 * narrow),
    )
    first_packs[1] = early.wait(first_packs[1])
    early.third()
    first_packs[1] = early.lead(first_packs[1])
    early.share("smp")
    late = SliceTotal(
        *filled(first_packs, 5 * width, (scale_first, shift_total_first, finish_total)),
        apart=LATE_APART,
    )
    gain_first = jnp.sum(cond_delta_first * condition_norm, axis=0)
    gain_second = jnp.sum(cond_delta_second * condition_norm, axis=0)
    condition_grad = sum_samples(
        normalize_back(
            cond_delta_first * first_gain.astype(f32) + cond_delta_second * second_gain.astype(f32),
            condition_norm,
            condition_factor,
        )
        + condition_closing
        + condition_finish
    )
    blocks = pair_features.shape[1] // 16 if pair_features.shape[1] % 16 == 0 else 1
    sizes = (blocks - blocks // 2, blocks // 2)
    delta_bias[0] = late.wait(delta_bias[0])
    late.first()
    pair_weight = late.lead(pair_weight)
    late.trade("cplx")
    early.state, late.state, delta_bias[1] = tied(early.state, late.state, delta_bias[1])
    early.fourth()
    pair_weight = early.lead(pair_weight)
    early.share("cplx")
    late.second()
    pair_weight = late.lead(pair_weight)
    late.trade("smp")
    pair_grad, inner_total = pair_backward(
        pair_features[0], pair_weight, delta_bias, 0, sizes[0], ()
    )
    inner_total = late.wait(inner_total)
    late.third()
    pair_weight = late.lead(pair_weight)
    late.share("smp")
    if sizes[1]:
        pair_grad, more = pair_backward(
            pair_features[0], pair_weight, delta_bias, *sizes, (pair_grad,)
        )
        inner_total = inner_total + more
    early.state = late.wait(early.state)
    late.fourth()
    late.share("cplx")
    pair_gain_total = jnp.sum(inner_total * pair_project.astype(f32).T, axis=0)
    pair_project_total = inner_total * pair_gain.astype(f32)[None]
    vectors = (
        gain_first,
        offset_first,
        query_bias_total[:, 0],
        finish_offset_total,
        gain_second,
        offset_second,
        closing_offset_total,
        pair_gain_total,
    )
    small = total_line(
        jnp.concatenate(
            [jnp.stack(halves(vector)) for vector in vectors]
            + [jnp.stack([half.reshape(-1) for half in halves(pair_project_total.T)])],
            axis=1,
        )
    )
    def unpack(total, sizes):
        arrays, start = [], 0
        for depth, columns in sizes:
            blocks = columns // half
            arrays.append(
                jnp.concatenate(
                    [
                        total[start + b * depth : start + (b + 1) * depth]
                        for b in range(blocks)
                    ],
                    axis=1,
                )
            )
            start += depth * blocks
        return arrays

    early_totals = unpack(
        early.result()[0],
        ((width, inner // 2), (width, inner // 2), (inner, half)) + ((narrow, half),) * 3,
    )
    small, *early_totals = tied(small, *early_totals)
    swish_total, linear_total, down_total, scale_second, shift_second, closing_total = early_totals
    small = summed(spread_apart(small, "cplx"))
    late = late.result()[0]
    ends, place = [], 0
    for vector in vectors:
        ends.append(small[place : place + vector.shape[0] // 2])
        place += vector.shape[0] // 2
    query_total, key_total, value_total, gate_total, output_total, *others = unpack(
        late, ((width, half),) * 5 + ((narrow, half),) * 3
    )
    scale_first, shift_first, finish_total = others
    return (
        block_out[None],
        single_grad[None],
        condition_grad[None],
        pair_grad[None],
        ends[0],
        scale_first,
        ends[1],
        shift_first,
        query_total,
        ends[2],
        key_total,
        value_total,
        gate_total,
        output_total,
        ends[7],
        small[place:].reshape(-1, heads // 2),
        finish_total,
        ends[3],
        ends[4],
        scale_second,
        ends[5],
        shift_second,
        swish_total,
        linear_total,
        down_total,
        closing_total,
        ends[6],
    )


def solution(mesh):
    placed = (
        P("cplx", "smp", "qry", None),
        P("cplx", "qry", None),
        P("cplx", ("qry", "smp"), None, None),
        P("cplx"),
        P("cplx", "smp", "qry", None),
        P(),
        P(),
        P(),
        P(),
        P(),
        P(),
        P(),
        P(),
        P(),
        P(),
        P(),
        P(),
        P(),
        P(),
        P(),
        P(),
        P(),
        P(),
        P(),
        P(),
        P(),
        P(),
        P(),
    )
    return jax.shard_map(
        per_device,
        mesh=mesh,
        in_specs=placed,
        out_specs=(
            P("cplx", "smp", "qry", None),
            P("cplx", "smp", "qry", None),
            P("cplx", "qry", None),
            P("cplx", ("qry", "smp"), None, None),
            P("qry"),
            P(None, "qry"),
            P("qry"),
            P(None, "qry"),
            P(None, "qry"),
            P("qry"),
            P(None, "qry"),
            P(None, "qry"),
            P(None, "qry"),
            P(None, "qry"),
            P("qry"),
            P(None, "qry"),
            P(None, "qry"),
            P("qry"),
            P("qry"),
            P(None, "qry"),
            P("qry"),
            P(None, "qry"),
            P(None, "qry"),
            P(None, "qry"),
            P(None, "qry"),
            P(None, "qry"),
            P("qry"),
        ),
        check_vma=False,
    )
```
